128 devices in a mesh: kv: 16 (over y, z_hi, core), tp: 8 (over z_lo, x).
Axes of the slice: x: 4, y: 4, z: 4 (z_hi: 2, z_lo: 2; z = z_hi * 2 + z_lo), core: 2. Of those that a mesh axis runs over, the one named last changes fastest.
Arguments:
- hidden_in: bfloat16 [8320, 2048], P(('kv', 'tp')), may hold values from -6 to 6
- norm_attn: bfloat16 [2048], replicated, may hold values from 0.099609375 to 1.8984375
- w_query: bfloat16 [2048, 2048], P(None, 'tp'), may hold values from -0.125 to 0.125
- w_key: bfloat16 [2048, 256], replicated, may hold values from -0.375 to 0.375
- w_value: bfloat16 [2048, 256], replicated, may hold values from -0.125 to 0.125
- w_out: bfloat16 [2048, 2048], P('tp'), may hold values from -0.125 to 0.125
- norm_mlp: bfloat16 [2048], replicated, may hold values from 0.099609375 to 1.8984375
- w_gate: bfloat16 [2048, 5632], P(None, 'tp'), may hold values from -0.125 to 0.125
- w_up: bfloat16 [2048, 5632], P(None, 'tp'), may hold values from -0.125 to 0.125
- w_down: bfloat16 [5632, 2048], P('tp'), may hold values from -0.078125 to 0.078125
- cache_keys: bfloat16 [16384, 256], P('kv'), may hold values from -1000 to 1000
- cache_values: bfloat16 [16384, 256], P('kv'), may hold values from -18 to 18
- leaf_parent: int32 [16], replicated, may hold values from 0 to 3, as said below
- leaf_owner: int32 [16], replicated, may hold values from 0 to 15, each once
- leaf_length: int32 [16], replicated, may hold values from 1 to 512, as said below
- prompt_leaf: int32 [16], replicated, may hold values from 0 to 15
- decode_leaf: int32 [128], replicated, may hold values from 0 to 15
Outputs:
- layer_out: bfloat16 [8320, 2048], P(('kv', 'tp'))
- attended: bfloat16 [8320, 2048], P('kv', 'tp')
The draws below stay inside these ranges and needn't reach their ends.
Inputs may be any that keep to these rules, and one draw needn't show every extreme that they name: `leaf_parent`: each of the 4 branches has exactly 4 leaves. `leaf_length`: some leaf holds exactly 512 tokens. `leaf_owner`: each owner holds exactly one leaf.
All inputs are finite; a program needn't handle non-finite values.
Results may differ from the reference program's by a relative error of at most 0.025.
The reference program's roundings to bfloat16 on the way (of `normed`, `query_rot`, `key_new`, `value_new`, `slab_weights`, `own_weights`, `normed_mlp` and `hidden_units`) count: a program that leaves them out, or rounds other values in their place, can miss the bound.
Values may be sent and summed in bfloat16 or wider, within the bound.
A program may use at most 384 MiB of HBM per device.

```python
import math
import jax
import jax.numpy as jnp
import numpy as np
from jax import lax

D = 2048
HEADS = 32
KV_HEADS = 4
HD = 64
FF = 5632
PLEN = 512
DEC_DEV = 8
RSEG = 256
BSEG = 256
LEAF_MAX = 512
FANOUT = 4
LEAVES = 16
ROOT = 4096
SLAB = 1024
TOKENS = 8320
N_KV = 16


def draw_cache_keys(key, part):
    owner_total = ROOT // RSEG
    row_total = owner_total * SLAB
    col_total = KV_HEADS * HD
    key_base = jax.random.fold_in(key, 0)
    base = jnp.clip(jax.random.normal(key_base, (row_total, col_total), jnp.float32), -6.0, 6.0) * 1.5
    return base.astype(jnp.bfloat16)


def draw_leaf_parent(key, part):
    order = jax.random.permutation(key, LEAVES)
    parents = jnp.zeros((LEAVES,), jnp.int32).at[order].set(jnp.arange(LEAVES, dtype=jnp.int32) // FANOUT)
    return parents.astype(jnp.int32)


def draw_leaf_length(key, part):
    key_lengths, key_full = jax.random.split(key)
    lengths = jax.random.randint(key_lengths, (LEAVES,), 1, LEAF_MAX + 1)
    full_leaf = jax.random.randint(key_full, (), 0, LEAVES)
    return jnp.where(jnp.arange(LEAVES) == full_leaf, LEAF_MAX, lengths).astype(jnp.int32)


def plant(drawn, own_key, smallest, high):
    longest = drawn.shape.index(max(drawn.shape))
    spots = []
    for shift in (0, 1):
        where = [jax.random.randint(jax.random.fold_in(own_key, axis), (), 0, length) for axis, length in enumerate(drawn.shape)]
        where[longest] = (where[longest] + shift) % drawn.shape[longest]
        spots.append(tuple(where))
    return drawn.at[spots[0]].set(smallest).at[spots[1]].set(high)


def level_of(key, extent, cuts, least, largest):
    factor_of = 1.0
    for dim, shards_of in cuts:
        draws = jax.random.uniform(jax.random.fold_in(jax.random.fold_in(key, 6), dim), (shards_of,), jnp.float32, least / len(cuts), largest / len(cuts))
        factor_of = factor_of * jnp.repeat(jnp.exp(draws), extent[dim] // shards_of).reshape((-1,) + (1,) * (len(extent) - 1 - dim))
    return factor_of


def cumulative_ranks(count, skew):
    loads = [(1 << 20) // math.isqrt(rank ** skew) + 1 for rank in range(1, count + 1)]
    spread = 1 + sum(loads) // (1 << 30)
    return np.cumsum(np.array([max(1, weight // spread) for weight in loads]))


def ranked_ids(key, shape, count, slope):
    listing = cumulative_ranks(count, slope)
    lot = jax.random.randint(jax.random.fold_in(key, 1), shape, 0, int(listing[count - 1]))
    rank = jnp.searchsorted(jnp.asarray(listing, jnp.int32), lot, side="right")
    return jax.random.permutation(jax.random.fold_in(key, 2), count)[rank].astype(jnp.int32)


def scatter_about(key, shape, spread, limit, cuts=(), kind=jnp.bfloat16):
    drawn = spread * jax.random.normal(key, shape, jnp.float32)
    if cuts:
        drawn = drawn * level_of(key, shape, cuts, -0.22, 0.18)
    return jnp.clip(drawn, -limit, limit).astype(kind)


def setup_inputs(seed: int = 0) -> dict:
    streams_of = jax.random.split(jax.random.key(seed), 18)
    return {
        "hidden_in": scatter_about(streams_of[0], (TOKENS, D), 1.0, 6.0, ((0, 128),)),
        "norm_attn": jnp.clip(1.0 + 0.18 * jax.random.normal(streams_of[1], (D,), jnp.float32), 0.099609375, 1.8984375).astype(jnp.bfloat16),
        "w_query": scatter_about(streams_of[2], (D, HEADS * HD), D ** -0.5, 0.125, ((1, 8),)),
        "w_key": scatter_about(streams_of[3], (D, KV_HEADS * HD), (D // 9) ** -0.5, 0.375),
        "w_value": scatter_about(streams_of[4], (D, KV_HEADS * HD), D ** -0.5, 0.125),
        "w_out": scatter_about(streams_of[5], (HEADS * HD, D), (HEADS * HD) ** -0.5, 0.125, ((0, 8),)),
        "norm_mlp": jnp.clip(1.0 + 0.18 * jax.random.normal(streams_of[6], (D,), jnp.float32), 0.099609375, 1.8984375).astype(jnp.bfloat16),
        "w_gate": scatter_about(streams_of[7], (D, FF), D ** -0.5, 0.125, ((1, 8),)),
        "w_up": scatter_about(streams_of[8], (D, FF), D ** -0.5, 0.125, ((1, 8),)),
        "w_down": scatter_about(streams_of[9], (FF, D), FF ** -0.5, 0.078125, ((0, 8),)),
        "cache_keys": draw_cache_keys(jax.random.fold_in(streams_of[17], 71), 0),
        "cache_values": scatter_about(streams_of[11], (N_KV * SLAB, KV_HEADS * HD), 3.0, 18.0, ((0, 16),)),
        "leaf_parent": draw_leaf_parent(jax.random.fold_in(streams_of[17], 71), 0),
        "leaf_owner": jax.random.permutation(streams_of[13], LEAVES).astype(jnp.int32),
        "leaf_length": draw_leaf_length(jax.random.fold_in(streams_of[17], 71), 0),
        "prompt_leaf": plant(jax.random.randint(streams_of[15], (N_KV,), 0, LEAVES), jax.random.fold_in(streams_of[15], 1), 0, LEAVES - 1).astype(jnp.int32),
        "decode_leaf": plant(ranked_ids(streams_of[16], (N_KV * DEC_DEV,), LEAVES, 2), jax.random.fold_in(streams_of[16], 3), 0, LEAVES - 1).astype(jnp.int32),
    }


epsilon = 1e-05

def rms_scale(values, gain_vector):
    floats = values.astype(jnp.float32)
    mean_square = lax.optimization_barrier(jnp.mean(floats * floats, axis=-1, keepdims=True))
    return floats * lax.rsqrt(mean_square + epsilon) * gain_vector.astype(jnp.float32)

def rotate(vectors, positions, head_width):
    half_width = head_width // 2
    frequencies = 10000.0 ** (-(jnp.arange(half_width, dtype=jnp.float32) * 2.0 / head_width))
    angles = positions.astype(jnp.float32)[:, None] * frequencies[None, :]
    angles = jnp.concatenate([angles, angles], axis=-1)
    turned = jnp.concatenate([-vectors[..., half_width:], vectors[..., :half_width]], axis=-1)
    return vectors * jnp.cos(angles)[:, None, :] + turned * jnp.sin(angles)[:, None, :]

def lookup(values_table, indices):
    labels = jnp.arange(values_table.shape[0], dtype=jnp.int32)
    return lax.optimization_barrier(jnp.sum(jnp.where(indices[..., None] == labels, values_table, 0), axis=-1)).astype(jnp.int32)

def row_leaves(prompt_leaf, decode_leaf, group_total):
    prompt_rows = jnp.broadcast_to(prompt_leaf[:, None], (group_total, PLEN))
    return jnp.concatenate([prompt_rows, decode_leaf.reshape(group_total, DEC_DEV)], axis=1).astype(jnp.int32)

def reference(hidden_in, norm_attn, w_query, w_key, w_value, w_out, norm_mlp, w_gate, w_up, w_down, cache_keys, cache_values, leaf_parent, leaf_owner, leaf_length, prompt_leaf, decode_leaf):
    rows_group = PLEN + DEC_DEV
    group_heads = HEADS // KV_HEADS
    score_scale = HD ** (-0.5)
    all_leaves = row_leaves(prompt_leaf, decode_leaf, N_KV)
    offsets = jnp.concatenate([jnp.arange(PLEN, dtype=jnp.int32), jnp.zeros((DEC_DEV,), jnp.int32)])
    positions = (RSEG * N_KV + BSEG * FANOUT + lookup(leaf_length, all_leaves) + offsets[None, :]).reshape(-1)
    normed = rms_scale(hidden_in, norm_attn).astype(jnp.bfloat16)
    query_rot = rotate(jnp.dot(normed, w_query, preferred_element_type=jnp.float32).reshape(-1, HEADS, HD), positions, HD).astype(jnp.bfloat16)
    key_new = rotate(jnp.dot(normed, w_key, preferred_element_type=jnp.float32).reshape(-1, KV_HEADS, HD), positions, HD).astype(jnp.bfloat16)
    value_new = jnp.dot(normed, w_value, preferred_element_type=jnp.float32).reshape(-1, KV_HEADS, HD).astype(jnp.bfloat16)
    labels = jnp.arange(LEAVES, dtype=jnp.int32)
    owner_ids = jnp.arange(N_KV, dtype=jnp.int32)
    owned_leaf = lax.optimization_barrier(jnp.sum(jnp.where(leaf_owner[None, :] == owner_ids[:, None], labels[None, :], 0), axis=1)).astype(jnp.int32)
    owned_branch = lookup(leaf_parent, owned_leaf)
    owned_length = lookup(leaf_length, owned_leaf)
    slot_ids = jnp.arange(SLAB, dtype=jnp.int32)
    in_root = slot_ids < RSEG
    in_branch = (slot_ids >= RSEG) & (slot_ids < RSEG + BSEG)
    leaf_valid = (slot_ids[None, :] >= RSEG + BSEG) & (slot_ids[None, :] - RSEG - BSEG < owned_length[:, None])
    cache_k = cache_keys.astype(jnp.float32).reshape(N_KV, SLAB, KV_HEADS, HD)
    cache_v = cache_values.astype(jnp.float32).reshape(N_KV, SLAB, KV_HEADS, HD)
    row_ids = jnp.arange(rows_group, dtype=jnp.int32)[:, None]
    col_ids = jnp.arange(rows_group, dtype=jnp.int32)[None, :]
    own_visible = (col_ids == row_ids) | (col_ids <= row_ids) & (row_ids < PLEN)

    def one_group(group_index):
        start_row = (group_index * rows_group).astype(jnp.int32)
        group_query = lax.dynamic_slice_in_dim(query_rot, start_row, rows_group, 0).astype(jnp.float32)
        group_key = lax.dynamic_slice_in_dim(key_new, start_row, rows_group, 0).astype(jnp.float32)
        group_value = lax.dynamic_slice_in_dim(value_new, start_row, rows_group, 0).astype(jnp.float32)
        leaves_here = lax.dynamic_index_in_dim(all_leaves, group_index, 0, keepdims=False)
        branch_here = lookup(leaf_parent, leaves_here)
        visible = in_root[None, None, :] | in_branch[None, None, :] & (branch_here[:, None] == owned_branch[None, :])[:, :, None] | leaf_valid[None, :, :] & (leaves_here[:, None] == owned_leaf[None, :])[:, :, None]
        outputs = []
        for kv_index in range(KV_HEADS):
            head_query = group_query[:, kv_index * group_heads:(kv_index + 1) * group_heads]
            scores = jnp.einsum('rgd,osd->rgos', head_query, cache_k[:, :, kv_index]) * score_scale
            scores = jnp.where(visible[:, None], scores, -jnp.inf)
            slab_max = lax.optimization_barrier(jnp.max(scores, axis=-1))
            slab_weights = lax.optimization_barrier(jnp.exp(scores - slab_max[..., None]).astype(jnp.bfloat16)).astype(jnp.float32)
            slab_total = lax.optimization_barrier(jnp.sum(slab_weights, axis=-1))
            slab_sum = jnp.einsum('rgos,osd->rgod', slab_weights, cache_v[:, :, kv_index])
            own_scores = jnp.einsum('rgd,cd->rgc', head_query, group_key[:, kv_index]) * score_scale
            own_scores = jnp.where(own_visible[:, None, :], own_scores, -jnp.inf)
            own_max = lax.optimization_barrier(jnp.max(own_scores, axis=-1))
            own_weights = lax.optimization_barrier(jnp.exp(own_scores - own_max[..., None]).astype(jnp.bfloat16)).astype(jnp.float32)
            own_total = lax.optimization_barrier(jnp.sum(own_weights, axis=-1))
            own_sum = jnp.einsum('rgc,cd->rgd', own_weights, group_value[:, kv_index])
            highest = jnp.maximum(lax.optimization_barrier(jnp.max(slab_max, axis=-1)), own_max)
            lift_far = jnp.exp(slab_max - highest[..., None])
            lift_own = jnp.exp(own_max - highest)
            denominator = lax.optimization_barrier(jnp.sum(slab_total * lift_far, axis=-1)) + own_total * lift_own
            numerator = lax.optimization_barrier(jnp.sum(slab_sum * lift_far[..., None], axis=2)) + own_sum * lift_own[..., None]
            outputs.append(numerator / denominator[..., None])
        return jnp.concatenate(outputs, axis=1).reshape(rows_group, HEADS * HD).astype(jnp.bfloat16)
    attended = lax.map(one_group, jnp.arange(N_KV, dtype=jnp.int32)).reshape(-1, HEADS * HD)
    residual = hidden_in.astype(jnp.float32) + jnp.dot(attended, w_out, preferred_element_type=jnp.float32)
    normed_mlp = rms_scale(residual, norm_mlp).astype(jnp.bfloat16)
    gate_part = jnp.dot(normed_mlp, w_gate, preferred_element_type=jnp.float32)
    up_part = jnp.dot(normed_mlp, w_up, preferred_element_type=jnp.float32)
    hidden_units = (jax.nn.silu(gate_part) * up_part).astype(jnp.bfloat16)
    layer_out = (residual + jnp.dot(hidden_units, w_down, preferred_element_type=jnp.float32)).astype(jnp.bfloat16)
    return (layer_out, attended)
```

```python
import jax, jax.numpy as jnp
from jax import lax
from jax.experimental import pallas as pl
from jax.experimental.pallas import tpu as pltpu
from jax.sharding import PartitionSpec as P

NEG = -1e30
NT = (((1,), (1,)), ((), ()))

def flash_step(state, qb, kvb, mask):
    m, acc = state
    s = lax.dot_general(qb, kvb, NT, preferred_element_type=jnp.float32)
    if mask is not None:
        s = jnp.where(mask, s, NEG)
    m_new = jnp.maximum(m, jnp.max(s, axis=1, keepdims=True))
    p = jnp.exp(s - m_new).astype(jnp.bfloat16)
    lane = lax.broadcasted_iota(jnp.int32, kvb.shape, 1)
    vaug = jnp.where(lane < 64, jnp.ones_like(kvb), kvb)
    acc = acc * jnp.exp(m - m_new) + jnp.dot(p, vaug, preferred_element_type=jnp.float32)
    return m_new, acc

def finish(state, rows):
    m, acc = state
    ratio = pltpu.roll(acc, 64, 1) / acc
    h = [ratio[i * rows:(i + 1) * rows] for i in range(4)]
    lane = lax.broadcasted_iota(jnp.int32, (rows, 128), 1)
    a = jnp.where(lane < 64, h[0], pltpu.roll(h[1], 64, 1))
    b = jnp.where(lane < 64, h[2], pltpu.roll(h[3], 64, 1))
    return jnp.concatenate([a, b], axis=1)

def token_of(idx):
    return jnp.where(idx < 512, 65 * (idx // 64) + idx % 64,
                     jnp.where(idx < 520, 65 * (idx - 512) + 64, 1 << 20))

def attn_kernel(info, qmain, qtail, tailinfo, kv, kvown, out, rows_out, main_ref, acc_ref):
    def start(rows):
        return jnp.full((rows, 1), NEG, jnp.float32), jnp.zeros((rows, 128), jnp.float32)

    own_rows = kvown.shape[0]
    def block(j, _):
        base = pl.multiple_of(j * 64, 64)
        qb = jnp.concatenate([qmain[h, pl.ds(base, 64), :] for h in range(4)], axis=0)
        def root(g, st):
            kvb = jnp.concatenate([kv[pl.ds(pl.multiple_of(g * 4096 + i * 1024, 256), 256), :] for i in range(4)], axis=0)
            return flash_step(st, qb, kvb, None)
        st = lax.fori_loop(0, 4, root, start(256))
        kvb = jnp.concatenate([kv[pl.ds(pl.multiple_of(info[i] * 1024 + 256, 256), 256), :] for i in range(4)], axis=0)
        st = flash_step(st, qb, kvb, None)
        kvb = jnp.concatenate([kv[pl.ds(pl.multiple_of(info[4] * 1024 + 512, 256), 512), :], kvown[...]], axis=0)
        col = lax.broadcasted_iota(jnp.int32, (1, 512 + own_rows), 1)
        rtok = 65 * j + lax.broadcasted_iota(jnp.int32, (256, 1), 0) % 64
        ktok = jnp.where(col < 512, jnp.where(col < info[5], -1, 1 << 20), token_of(col - 512))
        st = flash_step(st, qb, kvb, ktok <= rtok)
        main_ref[pl.ds(base, 64), :] = finish(st, 64)
        return 0
    lax.fori_loop(0, 8, block, 0)

    qt = jnp.concatenate([qtail[h] for h in range(4)], axis=0)
    r_owner = tailinfo[:, 0:1]
    r_branch = tailinfo[:, 1:2]
    r_tok = tailinfo[:, 2:3]
    def slab(o, st):
        kvb = kv[pl.ds(pl.multiple_of(o * 1024, 1024), 1024), :]
        col = lax.broadcasted_iota(jnp.int32, (1, 1024), 1)
        see_branch = jnp.where(r_branch == info[8 + o], 512, 256)
        see_leaf = jnp.where(r_owner == o, 512 + info[24 + o], 512)
        ok = (col < see_branch) | ((col >= 512) & (col < see_leaf))
        return flash_step(st, qt, kvb, ok)
    st = lax.fori_loop(0, 16, slab, start(64))
    ktok = token_of(lax.broadcasted_iota(jnp.int32, (1, own_rows), 1))
    st = flash_step(st, qt, kvown[...], (ktok == r_tok) | ((ktok <= r_tok) & (r_tok < 512)))
    res = finish(st, 16)
    main_ref[504:512, :] = res[0:8]
    rows_out[0:512, :] = main_ref[...].astype(jnp.bfloat16)
    rows_out[512:528, :] = jnp.concatenate([res[8:16], jnp.zeros((8, 256), jnp.float32)], axis=0).astype(jnp.bfloat16)
    for b in range(8):
        acc_ref[65 * b:65 * b + 64, :] = main_ref[64 * b:64 * b + 64, :]
    for e in range(8):
        acc_ref[65 * e + 64: 65 * e + 65, :] = res[8 + e: 9 + e]
    out[...] = acc_ref[...].astype(jnp.bfloat16)

def attn_call(info, qmain, qtail, tailinfo, kv, kvown):
    vm = pl.BlockSpec(memory_space=pltpu.VMEM)
    return pl.pallas_call(
        attn_kernel,
        out_shape=(jax.ShapeDtypeStruct((520, 256), jnp.bfloat16), jax.ShapeDtypeStruct((528, 256), jnp.bfloat16)),
        in_specs=[pl.BlockSpec(memory_space=pltpu.SMEM)] + [vm] * 5,
        out_specs=(vm, vm),
        scratch_shapes=[pltpu.VMEM((512, 256), jnp.float32), pltpu.VMEM((520, 256), jnp.float32)],
        compiler_params=pltpu.CompilerParams(vmem_limit_bytes=50 << 20),
        cost_estimate=pl.CostEstimate(flops=4 * 10**9, bytes_accessed=6 * 10**6, transcendentals=13 * 10**6),
        name="tree_attention",
    )(info, qmain, qtail, tailinfo, kv, kvown)


MESH = pl.DeviceIdType.MESH
A = pl.ds(0, 1024)
B = pl.ds(1024, 1024)
QUARTERS = tuple(pl.ds(512 * i, 512) for i in range(4))
A0, A1, B0, B1 = QUARTERS


class Links:
    def __init__(self, send_sem, recv_sem):
        self.send_sem, self.recv_sem, self.count, self.open = send_sem, recv_sem, 0, []

    def send(self, src, dst, where):
        k = self.count
        self.count += 1
        copy = pltpu.make_async_remote_copy(src_ref=src, dst_ref=dst, send_sem=self.send_sem.at[k], recv_sem=self.recv_sem.at[k],
                                            device_id=where, device_id_type=MESH)
        copy.start()
        self.open.append(copy)
        return copy

    def drain(self):
        for copy in self.open:
            copy.wait_send()
        self.open = []


class Place:
    def __init__(self):
        self.t = lax.axis_index("tp")
        self.z, self.x = lax.div(self.t, 4), lax.rem(self.t, 4)
        self.xr, self.xl, self.opp = lax.rem(self.x + 1, 4), lax.rem(self.x + 3, 4), lax.rem(self.x + 2, 4)
        self.oz = 1 - self.z
        self.right = {"tp": self.z * 4 + self.xr}
        self.left = {"tp": self.z * 4 + self.xl}
        self.mate = {"tp": self.oz * 4 + self.x}

    def peer(self, k):
        return lax.rem(self.t + k, 8)


def rows_of(rank):
    return pl.ds(pl.multiple_of(rank * 64, 64), 64)


def greet_group(place):
    barrier = pltpu.get_barrier_semaphore()
    for k in range(1, 8):
        pl.semaphore_signal(barrier, inc=1, device_id={"tp": place.peer(k)}, device_id_type=MESH)
    pl.semaphore_wait(barrier, 7)


def gather_rows(links, p, xall, ext):
    def blk(z, x, cols):
        return xall.at[rows_of(z * 4 + x), cols]
    def go(z, x, cols, where):
        return links.send(blk(z, x, cols), blk(z, x, cols), where)
    az = go(p.z, p.x, A, p.mate)
    br, bl = go(p.z, p.x, B, p.right), go(p.z, p.x, B, p.left)
    ar, al = go(p.z, p.x, A, p.right), go(p.z, p.x, A, p.left)
    bz = [go(p.z, p.x, B, p.mate)]
    singles = [links.send(ext.at[p.t], ext.at[p.t], {"tp": p.peer(k)}) for k in range(1, 8)]
    br.wait_recv()
    last = [go(p.z, p.xl, B0, p.right)]
    bz.append(go(p.z, p.xl, B, p.mate))
    bl.wait_recv()
    last.append(go(p.z, p.xr, B1, p.left))
    bz.append(go(p.z, p.xr, B, p.mate))
    az.wait_recv()
    far_r, far_l = go(p.oz, p.x, A, p.right), go(p.oz, p.x, A, p.left)
    ar.wait_recv()
    ends = [go(p.z, p.xl, A0, p.right)]
    al.wait_recv()
    ends.append(go(p.z, p.xr, A1, p.left))
    last[0].wait_recv()
    bz.append(go(p.z, p.opp, B0, p.mate))
    last[1].wait_recv()
    bz.append(go(p.z, p.opp, B1, p.mate))
    far_r.wait_recv()
    ends.append(go(p.oz, p.xl, A0, p.right))
    far_l.wait_recv()
    ends.append(go(p.oz, p.xr, A1, p.left))
    for copy in ends + bz + singles:
        copy.wait_recv()


def f32(x):
    return x.astype(jnp.float32)


def scatter_sums(links, p, produce, part, pe, bufs):
    near, wide, zb, bq, bw, za, eb = bufs
    planes = (p.oz, p.z)
    def blk(z, x, cols):
        return part.at[rows_of(z * 4 + x), cols]
    def add(z, x, cols, more):
        at = blk(z, x, cols)
        at[...] = (f32(at[...]) + f32(more)).astype(jnp.bfloat16)
    produce(2)
    produce(3)
    order = (p.opp, p.xr, p.xl, p.x)
    bz = [links.send(blk(p.oz, xd, B), zb.at[i], p.mate) for i, xd in enumerate(order)]
    produce(0)
    ar = [links.send(blk(z, p.opp, A0), near.at[0, i], p.right) for i, z in enumerate(planes)]
    produce(1)
    al = [links.send(blk(z, p.opp, A1), near.at[1, i], p.left) for i, z in enumerate(planes)]
    singles = [links.send(pe.at[p.peer(k)], eb.at[k], {"tp": p.peer(k)}) for k in range(1, 8)]
    bz[0].wait_recv()
    add(p.z, p.opp, B, zb[0])
    b_r = links.send(blk(p.z, p.opp, B0), bq.at[0], p.right)
    b_l = links.send(blk(p.z, p.opp, B1), bq.at[1], p.left)
    wr, wl = [], []
    for i, z in enumerate(planes):
        ar[i].wait_recv()
        add(z, p.xr, A0, near[0, i])
        wr.append(links.send(blk(z, p.xr, A), wide.at[0, i], p.right))
        al[i].wait_recv()
        add(z, p.xl, A1, near[1, i])
        wl.append(links.send(blk(z, p.xl, A), wide.at[1, i], p.left))
    bz[1].wait_recv()
    add(p.z, p.xr, B, zb[1])
    b_r.wait_recv()
    add(p.z, p.xr, B0, bq[0])
    b_rw = links.send(blk(p.z, p.xr, B), bw.at[0], p.right)
    bz[2].wait_recv()
    add(p.z, p.xl, B, zb[2])
    b_l.wait_recv()
    add(p.z, p.xl, B1, bq[1])
    b_lw = links.send(blk(p.z, p.xl, B), bw.at[1], p.left)
    wr[0].wait_recv()
    wl[0].wait_recv()
    add(p.oz, p.x, A, f32(wide[0, 0]) + f32(wide[1, 0]))
    a_z = links.send(blk(p.oz, p.x, A), za, p.mate)
    for copy in (wr[1], wl[1], bz[3], b_rw, b_lw):
        copy.wait_recv()
    mine_a = f32(blk(p.z, p.x, A)[...]) + f32(wide[0, 1]) + f32(wide[1, 1])
    mine_b = f32(blk(p.z, p.x, B)[...]) + f32(zb[3]) + f32(bw[0]) + f32(bw[1])
    for copy in singles:
        copy.wait_recv()
    single = pe[p.t]
    for k in range(1, 8):
        single = single + eb[k]
    a_z.wait_recv()
    return jnp.concatenate([mine_a + f32(za[...]), mine_b], axis=1), single


def sum_bufs():
    bf = jnp.bfloat16
    return [pltpu.VMEM((2, 2, 64, 512), bf), pltpu.VMEM((2, 2, 64, 1024), bf), pltpu.VMEM((4, 64, 1024), bf),
            pltpu.VMEM((2, 64, 512), bf), pltpu.VMEM((2, 64, 1024), bf), pltpu.VMEM((64, 1024), bf),
            pltpu.VMEM((8, 1, 2048), jnp.float32)]


def scaled(values, gain):
    mean_square = jnp.mean(values * values, axis=-1, keepdims=True)
    return (values * lax.rsqrt(mean_square + 1e-05) * gain).astype(jnp.bfloat16)


def place_singles(ext, xall):
    rows = [ext[e] for e in range(8)]
    xall[512:528, :] = jnp.concatenate(rows + [jnp.zeros((8, 2048), jnp.float32)], axis=0).astype(jnp.bfloat16)


def tail_kernel(att, hidden, gain, wo_h, wg_h, wu_h, wd_h, out, *s):
    (wo, wg, wu, wd, part, pe, xall, ext, hid, res, part2, pe2), s = s[:12], s[12:]
    bufs1, bufs2, (send_sem, recv_sem, wsem) = s[:7], s[7:14], s[14:]
    loads = [pltpu.make_async_copy(a, b, wsem.at[i]) for i, (a, b) in enumerate(((wo_h, wo), (wg_h, wg), (wu_h, wu), (wd_h, wd)))]
    for load in loads:
        load.start()
    p = Place()
    links = Links(send_sem, recv_sem)
    greet_group(p)
    loads[0].wait()

    def project(lhs, weights, part, pe):
        def produce(q):
            y = jnp.dot(lhs[...], weights[:, QUARTERS[q]], preferred_element_type=jnp.float32)
            part[:, QUARTERS[q]] = y[:512].astype(jnp.bfloat16)
            for e in range(8):
                pe[e, :, QUARTERS[q]] = y[512 + e:513 + e]
        return produce

    gains = gain[...].astype(jnp.float32)
    main, single = scatter_sums(links, p, project(att, wo, part, pe), part, pe, bufs1)
    main = f32(hidden[0:64, :]) + main
    single = f32(hidden[64:65, :]) + single
    res[0:64, :] = main
    res[64:65, :] = single
    xall[rows_of(p.t), :] = scaled(main, gains)
    ext[p.t] = f32(scaled(single, gains))
    gather_rows(links, p, xall, ext)
    place_singles(ext, xall)
    loads[1].wait()
    loads[2].wait()
    for lo, n in ((0, 256), (256, 256), (512, 192)):
        g = jnp.dot(xall[...], wg[:, lo:lo + n], preferred_element_type=jnp.float32)
        u = jnp.dot(xall[...], wu[:, lo:lo + n], preferred_element_type=jnp.float32)
        hid[:, lo:lo + n] = (g / (1.0 + jnp.exp(-g)) * u).astype(jnp.bfloat16)
    loads[3].wait()
    main, single = scatter_sums(links, p, project(hid, wd, part2, pe2), part2, pe2, bufs2)
    out[0:64, :] = (res[0:64, :] + main).astype(jnp.bfloat16)
    out[64:65, :] = (res[64:65, :] + single).astype(jnp.bfloat16)
    links.drain()


def tail_call(att, hidden, gain, w_out, w_gate, w_up, w_down):
    vm = pl.BlockSpec(memory_space=pltpu.VMEM)
    hbm = pl.BlockSpec(memory_space=pl.ANY)
    bf, fl = jnp.bfloat16, jnp.float32
    scratch = [pltpu.VMEM(w_out.shape, bf), pltpu.VMEM(w_gate.shape, bf), pltpu.VMEM(w_up.shape, bf), pltpu.VMEM(w_down.shape, bf),
               pltpu.VMEM((512, 2048), bf), pltpu.VMEM((8, 1, 2048), fl), pltpu.VMEM((528, 2048), bf), pltpu.VMEM((8, 1, 2048), fl),
               pltpu.VMEM((528, w_gate.shape[1]), bf), pltpu.VMEM((65, 2048), fl), pltpu.VMEM((512, 2048), bf), pltpu.VMEM((8, 1, 2048), fl)]
    scratch += sum_bufs() + sum_bufs()
    scratch += [pltpu.SemaphoreType.DMA((80,)), pltpu.SemaphoreType.DMA((80,)), pltpu.SemaphoreType.DMA((4,))]
    return pl.pallas_call(
        tail_kernel,
        out_shape=jax.ShapeDtypeStruct((65, 2048), bf),
        in_specs=[vm, vm, vm, hbm, hbm, hbm, hbm],
        out_specs=vm,
        scratch_shapes=scratch,
        compiler_params=pltpu.CompilerParams(vmem_limit_bytes=56 << 20, collective_id=1, has_side_effects=True),
        cost_estimate=pl.CostEstimate(flops=52 * 10**8, bytes_accessed=11 * 10**6, transcendentals=10**6),
        name="out_and_mlp",
    )(att, hidden, gain.reshape(1, 2048), w_out, w_gate, w_up, w_down)

HEADS = 32
KV_HEADS = 4
HD = 64
PLEN = 512
DEC_DEV = 8
RSEG = 256
BSEG = 256
FANOUT = 4
epsilon = 1e-05


def rms_scale(values, gain_vector):
    floats = values.astype(jnp.float32)
    mean_square = jnp.mean(floats * floats, axis=-1, keepdims=True)
    return floats * lax.rsqrt(mean_square + epsilon) * gain_vector.astype(jnp.float32)


def rotate(vectors, positions):
    half = HD // 2
    frequencies = 10000.0 ** (-(jnp.arange(half, dtype=jnp.float32) * 2.0 / HD))
    angles = positions.astype(jnp.float32)[:, None] * frequencies[None, :]
    angles = jnp.concatenate([angles, angles], axis=-1)
    turned = jnp.concatenate([-vectors[..., half:], vectors[..., :half]], axis=-1)
    return vectors * jnp.cos(angles)[:, None, :] + turned * jnp.sin(angles)[:, None, :]


def lookup(values_table, indices):
    labels = jnp.arange(values_table.shape[0], dtype=jnp.int32)
    return jnp.sum(jnp.where(indices[..., None] == labels, values_table, 0), axis=-1)


def tree_info(owner_index, leaf_parent, leaf_owner, leaf_length, prompt_leaf, decode_leaf):
    owners = jnp.arange(16, dtype=jnp.int32)
    leaf_of = jnp.sum(jnp.where(leaf_owner[None, :] == owners[:, None], owners[None, :], 0), axis=1)
    branch_of = lookup(leaf_parent, leaf_of)
    length_of = lookup(leaf_length, leaf_of)
    my_leaf = lookup(prompt_leaf, owner_index[None])[0]
    my_owner = lookup(leaf_owner, my_leaf[None])[0]
    my_branch = lookup(leaf_parent, my_leaf[None])[0]
    my_length = lookup(leaf_length, my_leaf[None])[0]
    same = (branch_of == my_branch).astype(jnp.int32)
    order = jnp.sum(jnp.where(owners[None, :] < owners[:, None], same[None, :], 0), axis=1)
    picks = jnp.arange(4, dtype=jnp.int32)
    mates = jnp.sum(jnp.where((order[None, :] == picks[:, None]) & (same[None, :] == 1), owners[None, :], 0), axis=1)
    info = jnp.concatenate([mates, my_owner[None], my_length[None], jnp.zeros((2,), jnp.int32), branch_of, length_of])
    dec = lax.dynamic_slice_in_dim(decode_leaf, owner_index * DEC_DEV, DEC_DEV, 0)
    tail_leaf = jnp.concatenate([my_leaf[None], dec[:7], jnp.broadcast_to(my_leaf[None], (7,)), dec[7:]])
    tail_token = jnp.concatenate([jnp.arange(511, 519, dtype=jnp.int32), 65 * jnp.arange(8, dtype=jnp.int32) + 64])
    columns = jnp.stack([lookup(leaf_owner, tail_leaf), lookup(leaf_parent, tail_leaf), tail_token], axis=1)
    return info, my_length, dec, jnp.tile(columns, (4, 1))


def per_device(hidden_in, norm_attn, w_query, w_key, w_value, w_out, norm_mlp, w_gate, w_up, w_down,
               cache_keys, cache_values, leaf_parent, leaf_owner, leaf_length, prompt_leaf, decode_leaf):
    owner_index = lax.axis_index("kv")
    kv_head = lax.axis_index("tp") // 2
    def cols(x):
        return lax.dynamic_slice_in_dim(x, kv_head * HD, HD, 1)
    slab = jnp.concatenate([cols(cache_keys), cols(cache_values)], axis=1)
    kv = lax.all_gather(slab, "kv", axis=0, tiled=True)
    info, my_length, dec, tailinfo = tree_info(owner_index, leaf_parent, leaf_owner, leaf_length, prompt_leaf, decode_leaf)
    joined = jnp.concatenate([w_query, cols(w_key), cols(w_value)], axis=1)
    normed = rms_scale(hidden_in, norm_attn).astype(jnp.bfloat16)
    rows = lax.all_gather(normed, "tp", axis=0)
    rows = jnp.concatenate([rows[:, :64].reshape(512, 2048), rows[:, 64]], axis=0)
    projected = jnp.dot(rows, joined, preferred_element_type=jnp.float32)
    token = token_of(jnp.arange(520, dtype=jnp.int32))
    dec_length = lookup(leaf_length, dec)
    spot = jnp.arange(8, dtype=jnp.int32)
    picked = jnp.sum(jnp.where((token[:, None] - 512) == spot[None, :], dec_length[None, :], 0), axis=1)
    positions = RSEG * 16 + BSEG * FANOUT + jnp.where(token < 512, my_length + token, picked)
    query = (rotate(projected[:, :256].reshape(520, 4, HD), positions).astype(jnp.bfloat16) * jnp.bfloat16(0.125))
    query = jnp.pad(query.transpose(1, 0, 2), ((0, 0), (0, 0), (0, 64)))
    qtail = query[:, 504:520]
    key_new = rotate(projected[:, 256:320].reshape(520, 1, HD), positions).reshape(520, HD).astype(jnp.bfloat16)
    kvown = jnp.pad(jnp.concatenate([key_new, projected[:, 320:].astype(jnp.bfloat16)], axis=1), ((0, 120), (0, 0)))
    attended, att = attn_call(info, query[:, :512], qtail, tailinfo, kv, kvown)
    return tail_call(att, hidden_in, norm_mlp, w_out, w_gate, w_up, w_down), attended


def solution(mesh):
    in_specs = (P(("kv", "tp"), None), P(), P(None, "tp"), P(), P(), P("tp", None), P(), P(None, "tp"), P(None, "tp"),
                P("tp", None), P("kv", None), P("kv", None), P(), P(), P(), P(), P())
    out_specs = (P(("kv", "tp"), None), P("kv", "tp"))
    return jax.shard_map(per_device, mesh=mesh, in_specs=in_specs, out_specs=out_specs, check_vma=False)
```

```python
import jax
import jax.numpy as jnp
import numpy as np
from jax import lax
from jax.experimental import pallas as pl
from jax.experimental.pallas import tpu as pltpu
from jax.sharding import PartitionSpec as P

NEG = -1e30
NT = (((1,), (1,)), ((), ()))

def flash_step(state, qb, kvb, mask):
    m, acc = state
    s = lax.dot_general(qb, kvb, NT, preferred_element_type=jnp.float32)
    if mask is not None:
        s = jnp.where(mask, s, NEG)
    m_new = jnp.maximum(m, jnp.max(s, axis=1, keepdims=True))
    p = jnp.exp(s - m_new).astype(jnp.bfloat16)
    lane = lax.broadcasted_iota(jnp.int32, kvb.shape, 1)
    vaug = jnp.where(lane < 64, jnp.ones_like(kvb), kvb)
    acc = acc * jnp.exp(m - m_new) + jnp.dot(p, vaug, preferred_element_type=jnp.float32)
    return m_new, acc

def finish(state, rows):
    m, acc = state
    ratio = pltpu.roll(acc, 64, 1) / acc
    h = [ratio[i * rows:(i + 1) * rows] for i in range(4)]
    lane = lax.broadcasted_iota(jnp.int32, (rows, 128), 1)
    a = jnp.where(lane < 64, h[0], pltpu.roll(h[1], 64, 1))
    b = jnp.where(lane < 64, h[2], pltpu.roll(h[3], 64, 1))
    return jnp.concatenate([a, b], axis=1)

def token_of(idx):
    return jnp.where(idx < 512, 65 * (idx // 64) + idx % 64,
                     jnp.where(idx < 520, 65 * (idx - 512) + 64, 1 << 20))

def attn_kernel(leaf_parent, leaf_owner, leaf_length, prompt_leaf, decode_leaf, qmain, qtail, kv, kvown, out, rows_out,
                main_ref, acc_ref, leaf_of, mates):
    me = lax.axis_index("kv")
    my_leaf = prompt_leaf[me]
    my_owner = leaf_owner[my_leaf]
    my_length = leaf_length[my_leaf]
    my_branch = leaf_parent[my_leaf]
    def invert(leaf, _):
        leaf_of[leaf_owner[leaf]] = leaf
        return 0
    lax.fori_loop(0, 16, invert, 0)
    def collect(o, found):
        mates[found] = o
        return found + jnp.where(leaf_parent[leaf_of[o]] == my_branch, 1, 0)
    lax.fori_loop(0, 16, collect, 0)

    def start(rows):
        return jnp.full((rows, 1), NEG, jnp.float32), jnp.zeros((rows, 128), jnp.float32)

    own_rows = kvown.shape[0]
    def block(j, _):
        base = pl.multiple_of(j * 64, 64)
        qb = jnp.concatenate([qmain[h, pl.ds(base, 64), :] for h in range(4)], axis=0)
        def root(g, st):
            kvb = jnp.concatenate([kv[pl.ds(pl.multiple_of(g * 4096 + i * 1024, 256), 256), :] for i in range(4)], axis=0)
            return flash_step(st, qb, kvb, None)
        st = lax.fori_loop(0, 4, root, start(256))
        kvb = jnp.concatenate([kv[pl.ds(pl.multiple_of(mates[i] * 1024 + 256, 256), 256), :] for i in range(4)], axis=0)
        st = flash_step(st, qb, kvb, None)
        kvb = jnp.concatenate([kv[pl.ds(pl.multiple_of(my_owner * 1024 + 512, 256), 512), :], kvown[...]], axis=0)
        col = lax.broadcasted_iota(jnp.int32, (1, 512 + own_rows), 1)
        rtok = 65 * j + lax.broadcasted_iota(jnp.int32, (256, 1), 0) % 64
        ktok = jnp.where(col < 512, jnp.where(col < my_length, -1, 1 << 20), token_of(col - 512))
        st = flash_step(st, qb, kvb, ktok <= rtok)
        main_ref[pl.ds(base, 64), :] = finish(st, 64)
        return 0
    lax.fori_loop(0, 8, block, 0)

    qt = jnp.concatenate([qtail[h] for h in range(4)], axis=0)
    row = lax.broadcasted_iota(jnp.int32, (64, 1), 0) % 16
    r_tok = jnp.where(row < 8, 511 + row, 65 * (row - 8) + 64)
    r_owner = jnp.full((64, 1), my_owner, jnp.int32)
    r_branch = jnp.full((64, 1), my_branch, jnp.int32)
    for i in range(8):
        leaf = decode_leaf[me * 8 + i]
        r_owner = jnp.where(r_tok == 512 + i, leaf_owner[leaf], r_owner)
        r_branch = jnp.where(r_tok == 512 + i, leaf_parent[leaf], r_branch)
    def slab(o, st):
        kvb = kv[pl.ds(pl.multiple_of(o * 1024, 1024), 1024), :]
        col = lax.broadcasted_iota(jnp.int32, (1, 1024), 1)
        leaf = leaf_of[o]
        see_branch = jnp.where(r_branch == leaf_parent[leaf], 512, 256)
        see_leaf = jnp.where(r_owner == o, 512 + leaf_length[leaf], 512)
        ok = (col < see_branch) | ((col >= 512) & (col < see_leaf))
        return flash_step(st, qt, kvb, ok)
    st = lax.fori_loop(0, 16, slab, start(64))
    ktok = token_of(lax.broadcasted_iota(jnp.int32, (1, own_rows), 1))
    st = flash_step(st, qt, kvown[...], (ktok == r_tok) | ((ktok <= r_tok) & (r_tok < 512)))
    res = finish(st, 16)
    main_ref[504:512, :] = res[0:8]
    rows_out[0:512, :] = main_ref[...].astype(jnp.bfloat16)
    rows_out[512:528, :] = jnp.concatenate([res[8:16], jnp.zeros((8, 256), jnp.float32)], axis=0).astype(jnp.bfloat16)
    for b in range(8):
        acc_ref[65 * b:65 * b + 64, :] = main_ref[64 * b:64 * b + 64, :]
    for e in range(8):
        acc_ref[65 * e + 64: 65 * e + 65, :] = res[8 + e: 9 + e]
    out[...] = acc_ref[...].astype(jnp.bfloat16)

def attn_call(tables, qmain, qtail, kv, kvown):
    vm = pl.BlockSpec(memory_space=pltpu.VMEM)
    return pl.pallas_call(
        attn_kernel,
        out_shape=(jax.ShapeDtypeStruct((520, 256), jnp.bfloat16), jax.ShapeDtypeStruct((528, 256), jnp.bfloat16)),
        in_specs=[pl.BlockSpec(memory_space=pltpu.SMEM)] * 5 + [vm] * 4,
        out_specs=(vm, vm),
        scratch_shapes=[pltpu.VMEM((512, 256), jnp.float32), pltpu.VMEM((520, 256), jnp.float32),
                        pltpu.SMEM((16,), jnp.int32), pltpu.SMEM((17,), jnp.int32)],
        compiler_params=pltpu.CompilerParams(vmem_limit_bytes=50 << 20),
        cost_estimate=pl.CostEstimate(flops=4 * 10**9, bytes_accessed=6 * 10**6, transcendentals=13 * 10**6),
        name="tree_attention",
    )(*tables, qmain, qtail, kv, kvown)


MESH = pl.DeviceIdType.MESH
A = pl.ds(0, 1024)
B = pl.ds(1024, 1024)
QUARTERS = tuple(pl.ds(512 * i, 512) for i in range(4))
A0, A1, B0, B1 = QUARTERS


class Links:
    def __init__(self, send_sem, recv_sem):
        self.send_sem, self.recv_sem, self.count, self.open = send_sem, recv_sem, 0, []

    def send(self, src, dst, where):
        k = self.count
        self.count += 1
        copy = pltpu.make_async_remote_copy(src_ref=src, dst_ref=dst, send_sem=self.send_sem.at[k], recv_sem=self.recv_sem.at[k],
                                            device_id=where, device_id_type=MESH)
        copy.start()
        self.open.append(copy)
        return copy

    def drain(self):
        for copy in self.open:
            copy.wait_send()
        self.open = []


class Place:
    def __init__(self):
        self.t = lax.axis_index("tp")
        self.z, self.x = lax.div(self.t, 4), lax.rem(self.t, 4)
        self.xr, self.xl, self.opp = lax.rem(self.x + 1, 4), lax.rem(self.x + 3, 4), lax.rem(self.x + 2, 4)
        self.oz = 1 - self.z
        self.right = {"tp": self.z * 4 + self.xr}
        self.left = {"tp": self.z * 4 + self.xl}
        self.mate = {"tp": self.oz * 4 + self.x}

    def peer(self, k):
        return lax.rem(self.t + k, 8)


def rows_of(rank):
    return pl.ds(pl.multiple_of(rank * 64, 64), 64)


def greet_group(place):
    barrier = pltpu.get_barrier_semaphore()
    for k in range(1, 8):
        pl.semaphore_signal(barrier, inc=1, device_id={"tp": place.peer(k)}, device_id_type=MESH)
    pl.semaphore_wait(barrier, 7)


def gather_rows_steps(links, p, xall, ext):
    def blk(z, x, cols):
        return xall.at[rows_of(z * 4 + x), cols]
    def go(z, x, cols, where):
        return links.send(blk(z, x, cols), blk(z, x, cols), where)
    az = go(p.z, p.x, A, p.mate)
    br, bl = go(p.z, p.x, B, p.right), go(p.z, p.x, B, p.left)
    ar, al = go(p.z, p.x, A, p.right), go(p.z, p.x, A, p.left)
    bz = [go(p.z, p.x, B, p.mate)]
    singles = [links.send(ext.at[p.t], ext.at[p.t], {"tp": p.peer(k)}) for k in range(1, 8)]
    yield 1
    br.wait_recv()
    last = [go(p.z, p.xl, B0, p.right)]
    bz.append(go(p.z, p.xl, B, p.mate))
    yield 1
    bl.wait_recv()
    last.append(go(p.z, p.xr, B1, p.left))
    bz.append(go(p.z, p.xr, B, p.mate))
    yield 1
    az.wait_recv()
    far_r, far_l = go(p.oz, p.x, A, p.right), go(p.oz, p.x, A, p.left)
    yield 1
    ar.wait_recv()
    ends = [go(p.z, p.xl, A0, p.right)]
    yield 1
    al.wait_recv()
    ends.append(go(p.z, p.xr, A1, p.left))
    yield 1
    last[0].wait_recv()
    bz.append(go(p.z, p.opp, B0, p.mate))
    last[1].wait_recv()
    bz.append(go(p.z, p.opp, B1, p.mate))
    yield 1
    far_r.wait_recv()
    ends.append(go(p.oz, p.xl, A0, p.right))
    yield 1
    far_l.wait_recv()
    ends.append(go(p.oz, p.xr, A1, p.left))
    yield 1
    for copy in ends + bz + singles:
        copy.wait_recv()


def gather_rows(links, p, xall, ext):
    for _ in gather_rows_steps(links, p, xall, ext):
        pass


def f32(x):
    return x.astype(jnp.float32)


def scatter_sums(links, p, produce, part, pe, bufs):
    near, wide, zb, bq, bw, za, eb = bufs
    planes = (p.oz, p.z)
    def blk(z, x, cols):
        return part.at[rows_of(z * 4 + x), cols]
    def add(z, x, cols, more):
        at = blk(z, x, cols)
        at[...] = (f32(at[...]) + f32(more)).astype(jnp.bfloat16)
    produce(2)
    produce(3)
    order = (p.opp, p.xr, p.xl, p.x)
    bz = [links.send(blk(p.oz, xd, B), zb.at[i], p.mate) for i, xd in enumerate(order)]
    produce(0)
    ar = [links.send(blk(z, p.opp, A0), near.at[0, i], p.right) for i, z in enumerate(planes)]
    produce(1)
    al = [links.send(blk(z, p.opp, A1), near.at[1, i], p.left) for i, z in enumerate(planes)]
    singles = [links.send(pe.at[p.peer(k)], eb.at[k], {"tp": p.peer(k)}) for k in range(1, 8)]
    bz[0].wait_recv()
    add(p.z, p.opp, B, zb[0])
    b_r = links.send(blk(p.z, p.opp, B0), bq.at[0], p.right)
    b_l = links.send(blk(p.z, p.opp, B1), bq.at[1], p.left)
    wr, wl = [], []
    for i, z in enumerate(planes):
        ar[i].wait_recv()
        add(z, p.xr, A0, near[0, i])
        wr.append(links.send(blk(z, p.xr, A), wide.at[0, i], p.right))
        al[i].wait_recv()
        add(z, p.xl, A1, near[1, i])
        wl.append(links.send(blk(z, p.xl, A), wide.at[1, i], p.left))
    bz[1].wait_recv()
    add(p.z, p.xr, B, zb[1])
    b_r.wait_recv()
    add(p.z, p.xr, B0, bq[0])
    b_rw = links.send(blk(p.z, p.xr, B), bw.at[0], p.right)
    bz[2].wait_recv()
    add(p.z, p.xl, B, zb[2])
    b_l.wait_recv()
    add(p.z, p.xl, B1, bq[1])
    b_lw = links.send(blk(p.z, p.xl, B), bw.at[1], p.left)
    wr[0].wait_recv()
    wl[0].wait_recv()
    add(p.oz, p.x, A, f32(wide[0, 0]) + f32(wide[1, 0]))
    a_z = links.send(blk(p.oz, p.x, A), za, p.mate)
    for copy in (wr[1], wl[1], bz[3], b_rw, b_lw):
        copy.wait_recv()
    mine_a = f32(blk(p.z, p.x, A)[...]) + f32(wide[0, 1]) + f32(wide[1, 1])
    mine_b = f32(blk(p.z, p.x, B)[...]) + f32(zb[3]) + f32(bw[0]) + f32(bw[1])
    for copy in singles:
        copy.wait_recv()
    single = pe[p.t]
    for k in range(1, 8):
        single = single + eb[k]
    a_z.wait_recv()
    return jnp.concatenate([mine_a + f32(za[...]), mine_b], axis=1), single


def sum_bufs():
    bf = jnp.bfloat16
    return [pltpu.VMEM((2, 2, 64, 512), bf), pltpu.VMEM((2, 2, 64, 1024), bf), pltpu.VMEM((4, 64, 1024), bf),
            pltpu.VMEM((2, 64, 512), bf), pltpu.VMEM((2, 64, 1024), bf), pltpu.VMEM((64, 1024), bf),
            pltpu.VMEM((8, 1, 2048), jnp.float32)]


def scaled(values, gain):
    mean_square = jnp.mean(values * values, axis=-1, keepdims=True)
    return (values * lax.rsqrt(mean_square + 1e-05) * gain).astype(jnp.bfloat16)


def place_singles(ext, xall):
    rows = [ext[e] for e in range(8)]
    xall[512:528, :] = jnp.concatenate(rows + [jnp.zeros((8, 2048), jnp.float32)], axis=0).astype(jnp.bfloat16)


def tail_kernel(att, hidden, gain, wo_h, wg_h, wu_h, wd_h, out, *s):
    (wo, wg, wu, wd, part, pe, xall, ext, hid, res, part2, pe2), s = s[:12], s[12:]
    bufs1, bufs2, (send_sem, recv_sem, wsem) = s[:7], s[7:14], s[14:]
    loads = [pltpu.make_async_copy(a, b, wsem.at[i]) for i, (a, b) in enumerate(((wo_h, wo), (wg_h, wg), (wu_h, wu), (wd_h, wd)))]
    for load in loads:
        load.start()
    p = Place()
    links = Links(send_sem, recv_sem)
    greet_group(p)
    loads[0].wait()

    def project(lhs, weights, part, pe):
        def produce(q):
            y = jnp.dot(lhs[...], weights[:, QUARTERS[q]], preferred_element_type=jnp.float32)
            part[:, QUARTERS[q]] = y[:512].astype(jnp.bfloat16)
            for e in range(8):
                pe[e, :, QUARTERS[q]] = y[512 + e:513 + e]
        return produce

    gains = gain[...].astype(jnp.float32)
    main, single = scatter_sums(links, p, project(att, wo, part, pe), part, pe, bufs1)
    main = f32(hidden[0:64, :]) + main
    single = f32(hidden[64:65, :]) + single
    res[0:64, :] = main
    res[64:65, :] = single
    xall[rows_of(p.t), :] = scaled(main, gains)
    ext[p.t] = f32(scaled(single, gains))
    gather_rows(links, p, xall, ext)
    place_singles(ext, xall)
    loads[1].wait()
    loads[2].wait()
    for lo, n in ((0, 256), (256, 256), (512, 192)):
        g = jnp.dot(xall[...], wg[:, lo:lo + n], preferred_element_type=jnp.float32)
        u = jnp.dot(xall[...], wu[:, lo:lo + n], preferred_element_type=jnp.float32)
        hid[:, lo:lo + n] = (g / (1.0 + jnp.exp(-g)) * u).astype(jnp.bfloat16)
    loads[3].wait()
    main, single = scatter_sums(links, p, project(hid, wd, part2, pe2), part2, pe2, bufs2)
    out[0:64, :] = (res[0:64, :] + main).astype(jnp.bfloat16)
    out[64:65, :] = (res[64:65, :] + single).astype(jnp.bfloat16)
    links.drain()


def tail_call(att, hidden, gain, w_out, w_gate, w_up, w_down):
    vm = pl.BlockSpec(memory_space=pltpu.VMEM)
    hbm = pl.BlockSpec(memory_space=pl.ANY)
    bf, fl = jnp.bfloat16, jnp.float32
    scratch = [pltpu.VMEM(w_out.shape, bf), pltpu.VMEM(w_gate.shape, bf), pltpu.VMEM(w_up.shape, bf), pltpu.VMEM(w_down.shape, bf),
               pltpu.VMEM((512, 2048), bf), pltpu.VMEM((8, 1, 2048), fl), pltpu.VMEM((528, 2048), bf), pltpu.VMEM((8, 1, 2048), fl),
               pltpu.VMEM((528, w_gate.shape[1]), bf), pltpu.VMEM((65, 2048), fl), pltpu.VMEM((512, 2048), bf), pltpu.VMEM((8, 1, 2048), fl)]
    scratch += sum_bufs() + sum_bufs()
    scratch += [pltpu.SemaphoreType.DMA((80,)), pltpu.SemaphoreType.DMA((80,)), pltpu.SemaphoreType.DMA((4,))]
    return pl.pallas_call(
        tail_kernel,
        out_shape=jax.ShapeDtypeStruct((65, 2048), bf),
        in_specs=[vm, vm, vm, hbm, hbm, hbm, hbm],
        out_specs=vm,
        scratch_shapes=scratch,
        compiler_params=pltpu.CompilerParams(vmem_limit_bytes=56 << 20, collective_id=1, has_side_effects=True),
        cost_estimate=pl.CostEstimate(flops=52 * 10**8, bytes_accessed=11 * 10**6, transcendentals=10**6),
        name="out_and_mlp",
    )(att, hidden, gain.reshape(1, 2048), w_out, w_gate, w_up, w_down)


def interleave(*chains):
    chains = list(chains)
    while chains:
        for chain in list(chains):
            if next(chain, None) is None:
                chains.remove(chain)


class Ring:
    def __init__(self):
        self.o = lax.axis_index("kv")
        self.y, rest = lax.div(self.o, 4), lax.rem(self.o, 4)
        self.h, self.c = lax.div(rest, 2), lax.rem(rest, 2)
        self.yr, self.yl, self.opp = lax.rem(self.y + 1, 4), lax.rem(self.y + 3, 4), lax.rem(self.y + 2, 4)
        self.oh = 1 - self.h
        self.right, self.left = {"kv": self.at(self.yr, self.h)}, {"kv": self.at(self.yl, self.h)}
        self.mate, self.twin = {"kv": self.at(self.y, self.oh)}, {"kv": self.o + 1 - 2 * self.c}

    def at(self, y, h):
        return y * 4 + h * 2 + self.c


def gather_cache(links, r, kv):
    top, low, whole = pl.ds(0, 512), pl.ds(512, 512), pl.ds(0, 1024)
    twins = []
    def go(y, h, rows, where):
        at = kv.at[r.at(y, h), rows, :]
        return links.send(at, at, where)
    def share(y, h, rows):
        twins.append(go(y, h, rows, r.twin))
    m = go(r.y, r.h, whole, r.mate)
    a = go(r.y, r.h, whole, r.right), go(r.y, r.h, whole, r.left)
    share(r.y, r.h, whole)
    yield 1
    m.wait_recv()
    b = go(r.y, r.oh, whole, r.right), go(r.y, r.oh, whole, r.left)
    share(r.y, r.oh, whole)
    yield 1
    ends = []
    for (from_left, from_right), h in ((a, r.h), (b, r.oh)):
        from_left.wait_recv()
        ends.append((go(r.yl, h, top, r.right), h, top))
        share(r.yl, h, whole)
        yield 1
        from_right.wait_recv()
        ends.append((go(r.yr, h, low, r.left), h, low))
        share(r.yr, h, whole)
        yield 1
    for copy, h, rows in ends:
        copy.wait_recv()
        share(r.opp, h, rows)
        yield 1
    for copy in twins:
        copy.wait_recv()


def head_kernel(hidden, gain, freq, leaf_length, prompt_leaf, decode_leaf, wq_h, wk_h, wv_h, ck_h, cv_h,
                q_out, qt_out, own_out, kv_out, kv, xall, ext, w, ck, cv, cos, sin, send_sem, recv_sem, wsem, osem):
    p, r = Place(), Ring()
    links = Links(send_sem, recv_sem)
    head = lax.div(p.t, 2)
    odd = lax.rem(head, 2)
    pair = pl.ds(pl.multiple_of(lax.div(head, 2) * 128, 128), 128)
    loads = [pltpu.make_async_copy(ck_h.at[:, pair], ck, wsem.at[0]), pltpu.make_async_copy(cv_h.at[:, pair], cv, wsem.at[1]),
             pltpu.make_async_copy(wq_h, w.at[:, 0:256], wsem.at[2]), pltpu.make_async_copy(wk_h.at[:, pair], w.at[:, 256:384], wsem.at[3]),
             pltpu.make_async_copy(wv_h.at[:, pair], w.at[:, 384:512], wsem.at[4])]
    for load in loads:
        load.start()
    barrier = pltpu.get_barrier_semaphore()
    for where in [{"tp": p.peer(k)} for k in range(1, 8)] + [r.right, r.left, r.mate, r.twin]:
        pl.semaphore_signal(barrier, inc=1, device_id=where, device_id_type=MESH)
    gains = gain[...].astype(jnp.float32)
    xall[rows_of(p.t), :] = scaled(f32(hidden[0:64, :]), gains)
    ext[p.t] = f32(scaled(f32(hidden[64:65, :]), gains))
    loads[0].wait()
    loads[1].wait()
    lane = lax.broadcasted_iota(jnp.int32, (1, 128), 1)

    def joined(keys, values):
        k = jnp.where(odd == 1, pltpu.roll(keys, 64, 1), keys)
        v = jnp.where(odd == 1, values, pltpu.roll(values, 64, 1))
        return jnp.where(lane < 64, k, v)

    kv[r.o] = joined(f32(ck[...]), f32(cv[...])).astype(jnp.bfloat16)
    pl.semaphore_wait(barrier, 11)

    rows = gather_rows_steps(links, p, xall, ext)
    cache = gather_cache(links, r, kv)
    next(rows)
    next(cache)
    a = r.o
    token = token_of(lax.broadcasted_iota(jnp.int32, (528, 1), 0))
    base = jnp.full((528, 1), leaf_length[prompt_leaf[a]], jnp.int32) + token
    for i in range(8):
        base = jnp.where(token == 512 + i, leaf_length[decode_leaf[a * 8 + i]], base)
    angle = (base + 5120).astype(jnp.float32) * freq[0:1, :]
    cos[...] = jnp.cos(angle)
    sin[...] = jnp.sin(angle)
    interleave(rows, cache)
    place_singles(ext, xall)
    for load in loads[2:]:
        load.wait()

    def rotated(x):
        turned = jnp.where(lane % 64 < 32, -pltpu.roll(x, 96, 1), pltpu.roll(x, 32, 1))
        return x * cos[...] + turned * sin[...]

    y = jnp.dot(xall[...], w[...], preferred_element_type=jnp.float32)
    zero = jnp.zeros((528, 128), jnp.float32)
    for i in range(2):
        q = f32(rotated(y[:, 128 * i:128 * i + 128]).astype(jnp.bfloat16)) * 0.125
        for j, x in enumerate((q, pltpu.roll(q, 64, 1))):
            x = jnp.where(lane < 64, x, zero)
            q_out[2 * i + j] = x[:512].astype(jnp.bfloat16)
            qt_out[2 * i + j] = x[504:520].astype(jnp.bfloat16)
    own_out[0:528, :] = joined(rotated(y[:, 256:384]), y[:, 384:512]).astype(jnp.bfloat16)
    own_out[528:640, :] = jnp.zeros((112, 128), jnp.bfloat16)
    out = pltpu.make_async_copy(kv, kv_out, osem)
    out.start()
    out.wait()
    links.drain()


def head_call(hidden, gain, freq, leaf_length, prompt_leaf, decode_leaf, w_query, w_key, w_value, cache_keys, cache_values):
    vm = pl.BlockSpec(memory_space=pltpu.VMEM)
    sm = pl.BlockSpec(memory_space=pltpu.SMEM)
    hbm = pl.BlockSpec(memory_space=pl.ANY)
    bf, fl = jnp.bfloat16, jnp.float32
    return pl.pallas_call(
        head_kernel,
        out_shape=(jax.ShapeDtypeStruct((4, 512, 128), bf), jax.ShapeDtypeStruct((4, 16, 128), bf),
                   jax.ShapeDtypeStruct((640, 128), bf), jax.ShapeDtypeStruct((16, 1024, 128), bf)),
        in_specs=[vm, vm, vm, sm, sm, sm] + [hbm] * 5,
        out_specs=(vm, vm, vm, hbm),
        scratch_shapes=[pltpu.VMEM((16, 1024, 128), bf), pltpu.VMEM((528, 2048), bf), pltpu.VMEM((8, 1, 2048), fl), pltpu.VMEM((2048, 512), bf),
                        pltpu.VMEM((1024, 128), bf), pltpu.VMEM((1024, 128), bf), pltpu.VMEM((528, 128), fl), pltpu.VMEM((528, 128), fl),
                        pltpu.SemaphoreType.DMA((60,)), pltpu.SemaphoreType.DMA((60,)), pltpu.SemaphoreType.DMA((5,)), pltpu.SemaphoreType.DMA],
        compiler_params=pltpu.CompilerParams(vmem_limit_bytes=48 << 20, collective_id=2, has_side_effects=True),
        cost_estimate=pl.CostEstimate(flops=10**9, bytes_accessed=10 * 10**6, transcendentals=10**5),
        name="gathers_and_qkv",
    )(hidden, gain.reshape(1, 2048), freq, leaf_length, prompt_leaf, decode_leaf, w_query, w_key, w_value, cache_keys, cache_values)


def per_device(hidden_in, norm_attn, w_query, w_key, w_value, w_out, norm_mlp, w_gate, w_up, w_down,
               cache_keys, cache_values, leaf_parent, leaf_owner, leaf_length, prompt_leaf, decode_leaf):
    freq = 10000.0 ** (-((np.arange(128) % 32).astype(np.float32) * np.float32(2.0) / np.float32(64)))
    freq = jnp.asarray(np.broadcast_to(freq.astype(np.float32), (8, 128)))
    q, qtail, own, kv = head_call(hidden_in, norm_attn, freq, leaf_length, prompt_leaf, decode_leaf,
                                  w_query, w_key, w_value, cache_keys, cache_values)
    attended, att = attn_call((leaf_parent, leaf_owner, leaf_length, prompt_leaf, decode_leaf), q, qtail,
                              kv.reshape(16 * 1024, 128), own)
    return tail_call(att, hidden_in, norm_mlp, w_out, w_gate, w_up, w_down), attended


def solution(mesh):
    in_specs = (P(("kv", "tp"), None), P(), P(None, "tp"), P(), P(), P("tp", None), P(), P(None, "tp"), P(None, "tp"),
                P("tp", None), P("kv", None), P("kv", None), P(), P(), P(), P(), P())
    out_specs = (P(("kv", "tp"), None), P("kv", "tp"))
    return jax.shard_map(per_device, mesh=mesh, in_specs=in_specs, out_specs=out_specs, check_vma=False)
```

```python
import jax
import jax.numpy as jnp
import numpy as np
from jax import lax
from jax.experimental import pallas as pl
from jax.experimental.pallas import tpu as pltpu
from jax.sharding import PartitionSpec as P

NEG = -1e30
NT = (((1,), (1,)), ((), ()))

def flash_many(st, qb, items):
    ss=lax.dot_general(qb, items[0][0], NT, preferred_element_type=jnp.float32)
    for i,(kvb,mask) in enumerate(items):
        nx = lax.dot_general(qb, items[i+1][0], NT, preferred_element_type=jnp.float32) if i+1<len(items) else None
        st = flash_step(st, qb, kvb, mask, ss)
        ss = nx
    return st

def flash_step(state, qb, kvb, mask, s=None):
    m, acc = state
    if s is None:
        s = lax.dot_general(qb, kvb, NT, preferred_element_type=jnp.float32)
    if mask is not None:
        s = jnp.where(mask, s, NEG)
    m_new = jnp.maximum(m, jnp.max(s, axis=1, keepdims=True))
    p = jnp.exp(s - m_new).astype(jnp.bfloat16)
    lane = lax.broadcasted_iota(jnp.int32, kvb.shape, 1)
    vaug = jnp.where(lane < 64, jnp.ones_like(kvb), kvb)
    acc = acc * jnp.exp(m - m_new) + jnp.dot(p, vaug, preferred_element_type=jnp.float32)
    return m_new, acc

def finish(state, rows):
    m, acc = state
    ratio = pltpu.roll(acc, 64, 1) / acc
    h = [ratio[i * rows:(i + 1) * rows] for i in range(4)]
    lane = lax.broadcasted_iota(jnp.int32, (rows, 128), 1)
    a = jnp.where(lane < 64, h[0], pltpu.roll(h[1], 64, 1))
    b = jnp.where(lane < 64, h[2], pltpu.roll(h[3], 64, 1))
    return jnp.concatenate([a, b], axis=1)

def token_of(idx):
    return jnp.where(idx < 512, 65 * (idx // 64) + idx % 64,
                     jnp.where(idx < 520, 65 * (idx - 512) + 64, 1 << 20))

def attn_kernel(leaf_parent, leaf_owner, leaf_length, prompt_leaf, decode_leaf, qmain, qtail, kv, kvown, out, rows_out,
                main_ref, acc_ref, leaf_of, mates):
    me = lax.axis_index("kv")
    my_leaf = prompt_leaf[me]
    my_owner = leaf_owner[my_leaf]
    my_length = leaf_length[my_leaf]
    my_branch = leaf_parent[my_leaf]
    def invert(leaf, _):
        leaf_of[leaf_owner[leaf]] = leaf
        return 0
    lax.fori_loop(0, 16, invert, 0)
    def collect(o, found):
        mates[found] = o
        return found + jnp.where(leaf_parent[leaf_of[o]] == my_branch, 1, 0)
    lax.fori_loop(0, 16, collect, 0)

    def start(rows):
        return jnp.full((rows, 1), NEG, jnp.float32), jnp.zeros((rows, 128), jnp.float32)

    own_rows = kvown.shape[0]
    def block(j, _):
        base = pl.multiple_of(j * 64, 64)
        qb = jnp.concatenate([qmain[h, pl.ds(base, 64), :] for h in range(4)], axis=0)
        def root(g, st):
            kvb = jnp.concatenate([kv[pl.ds(pl.multiple_of(g * 4096 + i * 1024, 256), 256), :] for i in range(4)], axis=0)
            return flash_step(st, qb, kvb, None)
        items = [(jnp.concatenate([kv[pl.ds(g * 4096 + i * 1024, 256), :] for i in range(4)], axis=0), None) for g in range(4)]
        kvb = jnp.concatenate([kv[pl.ds(pl.multiple_of(mates[i] * 1024 + 256, 256), 256), :] for i in range(4)], axis=0)
        items.append((kvb, None))
        kvb = jnp.concatenate([kv[pl.ds(pl.multiple_of(my_owner * 1024 + 512, 256), 512), :], kvown[...]], axis=0)
        col = lax.broadcasted_iota(jnp.int32, (1, 512 + own_rows), 1)
        rtok = 65 * j + lax.broadcasted_iota(jnp.int32, (256, 1), 0) % 64
        ktok = jnp.where(col < 512, jnp.where(col < my_length, -1, 1 << 20), token_of(col - 512))
        items.append((kvb, ktok <= rtok))
        st = flash_many(start(256), qb, items)
        main_ref[pl.ds(base, 64), :] = finish(st, 64)
        return 0
    lax.fori_loop(0, 8, block, 0)

    qt = jnp.concatenate([qtail[h] for h in range(4)], axis=0)
    row = lax.broadcasted_iota(jnp.int32, (64, 1), 0) % 16
    r_tok = jnp.where(row < 8, 511 + row, 65 * (row - 8) + 64)
    r_owner = jnp.full((64, 1), my_owner, jnp.int32)
    r_branch = jnp.full((64, 1), my_branch, jnp.int32)
    for i in range(8):
        leaf = decode_leaf[me * 8 + i]
        r_owner = jnp.where(r_tok == 512 + i, leaf_owner[leaf], r_owner)
        r_branch = jnp.where(r_tok == 512 + i, leaf_parent[leaf], r_branch)
    items_b = []
    for o in range(16):
        kvb = kv[o * 1024:o * 1024 + 1024, :]
        col = lax.broadcasted_iota(jnp.int32, (1, 1024), 1)
        leaf = leaf_of[o]
        see_branch = jnp.where(r_branch == leaf_parent[leaf], 512, 256)
        see_leaf = jnp.where(r_owner == o, 512 + leaf_length[leaf], 512)
        ok = (col < see_branch) | ((col >= 512) & (col < see_leaf))
        items_b.append((kvb, ok))
    ktok = token_of(lax.broadcasted_iota(jnp.int32, (1, own_rows), 1))
    items_b.append((kvown[...], (ktok == r_tok) | ((ktok <= r_tok) & (r_tok < 512))))
    st = flash_many(start(64), qt, items_b)
    res = finish(st, 16)
    main_ref[504:512, :] = res[0:8]
    rows_out[0:512, :] = main_ref[...].astype(jnp.bfloat16)
    rows_out[512:528, :] = jnp.concatenate([res[8:16], jnp.zeros((8, 256), jnp.float32)], axis=0).astype(jnp.bfloat16)
    for b in range(8):
        acc_ref[65 * b:65 * b + 64, :] = main_ref[64 * b:64 * b + 64, :]
    for e in range(8):
        acc_ref[65 * e + 64: 65 * e + 65, :] = res[8 + e: 9 + e]
    out[...] = acc_ref[...].astype(jnp.bfloat16)

def attn_call(tables, qmain, qtail, kv, kvown):
    vm = pl.BlockSpec(memory_space=pltpu.VMEM)
    return pl.pallas_call(
        attn_kernel,
        out_shape=(jax.ShapeDtypeStruct((520, 256), jnp.bfloat16), jax.ShapeDtypeStruct((528, 256), jnp.bfloat16)),
        in_specs=[pl.BlockSpec(memory_space=pltpu.SMEM)] * 5 + [vm] * 4,
        out_specs=(vm, vm),
        scratch_shapes=[pltpu.VMEM((512, 256), jnp.float32), pltpu.VMEM((520, 256), jnp.float32),
                        pltpu.SMEM((16,), jnp.int32), pltpu.SMEM((17,), jnp.int32)],
        compiler_params=pltpu.CompilerParams(vmem_limit_bytes=60 << 20),
        cost_estimate=pl.CostEstimate(flops=4 * 10**9, bytes_accessed=6 * 10**6, transcendentals=13 * 10**6),
        name="tree_attention",
    )(*tables, qmain, qtail, kv, kvown)


MESH = pl.DeviceIdType.MESH
A = pl.ds(0, 1024)
B = pl.ds(1024, 1024)
QUARTERS = tuple(pl.ds(512 * i, 512) for i in range(4))
A0, A1, B0, B1 = QUARTERS


class Links:
    def __init__(self, send_sem, recv_sem):
        self.send_sem, self.recv_sem, self.count, self.open = send_sem, recv_sem, 0, []

    def send(self, src, dst, where):
        k = self.count
        self.count += 1
        copy = pltpu.make_async_remote_copy(src_ref=src, dst_ref=dst, send_sem=self.send_sem.at[k], recv_sem=self.recv_sem.at[k],
                                            device_id=where, device_id_type=MESH)
        copy.start()
        self.open.append(copy)
        return copy

    def drain(self):
        for copy in self.open:
            copy.wait_send()
        self.open = []


class Place:
    def __init__(self):
        self.t = lax.axis_index("tp")
        self.z, self.x = lax.div(self.t, 4), lax.rem(self.t, 4)
        self.xr, self.xl, self.opp = lax.rem(self.x + 1, 4), lax.rem(self.x + 3, 4), lax.rem(self.x + 2, 4)
        self.oz = 1 - self.z
        self.right = {"tp": self.z * 4 + self.xr}
        self.left = {"tp": self.z * 4 + self.xl}
        self.mate = {"tp": self.oz * 4 + self.x}

    def peer(self, k):
        return lax.rem(self.t + k, 8)


def rows_of(rank):
    return pl.ds(pl.multiple_of(rank * 64, 64), 64)


def greet_group(place):
    barrier = pltpu.get_barrier_semaphore()
    for k in range(1, 8):
        pl.semaphore_signal(barrier, inc=1, device_id={"tp": place.peer(k)}, device_id_type=MESH)
    pl.semaphore_wait(barrier, 7)


def gather_rows_steps(links, p, xall, ext):
    def blk(z, x, cols):
        return xall.at[rows_of(z * 4 + x), cols]
    def go(z, x, cols, where):
        return links.send(blk(z, x, cols), blk(z, x, cols), where)
    az = go(p.z, p.x, A, p.mate)
    br, bl = go(p.z, p.x, B, p.right), go(p.z, p.x, B, p.left)
    ar, al = go(p.z, p.x, A, p.right), go(p.z, p.x, A, p.left)
    bz = [go(p.z, p.x, B, p.mate)]
    singles = [links.send(ext.at[p.t], ext.at[p.t], {"tp": p.peer(k)}) for k in range(1, 8)]
    yield 1
    br.wait_recv()
    last = [go(p.z, p.xl, B0, p.right)]
    bz.append(go(p.z, p.xl, B, p.mate))
    yield 1
    bl.wait_recv()
    last.append(go(p.z, p.xr, B1, p.left))
    bz.append(go(p.z, p.xr, B, p.mate))
    yield 1
    az.wait_recv()
    far_r, far_l = go(p.oz, p.x, A, p.right), go(p.oz, p.x, A, p.left)
    yield 1
    ar.wait_recv()
    ends = [go(p.z, p.xl, A0, p.right)]
    yield 1
    al.wait_recv()
    ends.append(go(p.z, p.xr, A1, p.left))
    yield 1
    last[0].wait_recv()
    bz.append(go(p.z, p.opp, B0, p.mate))
    last[1].wait_recv()
    bz.append(go(p.z, p.opp, B1, p.mate))
    yield 1
    far_r.wait_recv()
    ends.append(go(p.oz, p.xl, A0, p.right))
    yield 1
    far_l.wait_recv()
    ends.append(go(p.oz, p.xr, A1, p.left))
    yield 1
    for copy in ends + bz + singles:
        copy.wait_recv()


def gather_rows(links, p, xall, ext):
    for _ in gather_rows_steps(links, p, xall, ext):
        pass


def f32(x):
    return x.astype(jnp.float32)


def scatter_sums(links, p, produce, part, pe, bufs):
    near, wide, zb, bq, bw, za, eb = bufs
    planes = (p.oz, p.z)
    def blk(z, x, cols):
        return part.at[rows_of(z * 4 + x), cols]
    def add(z, x, cols, more):
        at = blk(z, x, cols)
        at[...] = (f32(at[...]) + f32(more)).astype(jnp.bfloat16)
    produce(2)
    produce(3)
    order = (p.opp, p.xr, p.xl, p.x)
    bz = [links.send(blk(p.oz, xd, B), zb.at[i], p.mate) for i, xd in enumerate(order)]
    produce(0)
    ar = [links.send(blk(z, p.opp, A0), near.at[0, i], p.right) for i, z in enumerate(planes)]
    produce(1)
    al = [links.send(blk(z, p.opp, A1), near.at[1, i], p.left) for i, z in enumerate(planes)]
    singles = [links.send(pe.at[p.peer(k)], eb.at[k], {"tp": p.peer(k)}) for k in range(1, 8)]
    bz[0].wait_recv()
    add(p.z, p.opp, B, zb[0])
    b_r = links.send(blk(p.z, p.opp, B0), bq.at[0], p.right)
    b_l = links.send(blk(p.z, p.opp, B1), bq.at[1], p.left)
    wr, wl = [], []
    for i, z in enumerate(planes):
        ar[i].wait_recv()
        add(z, p.xr, A0, near[0, i])
        wr.append(links.send(blk(z, p.xr, A), wide.at[0, i], p.right))
        al[i].wait_recv()
        add(z, p.xl, A1, near[1, i])
        wl.append(links.send(blk(z, p.xl, A), wide.at[1, i], p.left))
    bz[1].wait_recv()
    add(p.z, p.xr, B, zb[1])
    b_r.wait_recv()
    add(p.z, p.xr, B0, bq[0])
    b_rw = links.send(blk(p.z, p.xr, B), bw.at[0], p.right)
    bz[2].wait_recv()
    add(p.z, p.xl, B, zb[2])
    b_l.wait_recv()
    add(p.z, p.xl, B1, bq[1])
    b_lw = links.send(blk(p.z, p.xl, B), bw.at[1], p.left)
    wr[0].wait_recv()
    wl[0].wait_recv()
    add(p.oz, p.x, A, f32(wide[0, 0]) + f32(wide[1, 0]))
    a_z = links.send(blk(p.oz, p.x, A), za, p.mate)
    for copy in (wr[1], wl[1], bz[3], b_rw, b_lw):
        copy.wait_recv()
    mine_a = f32(blk(p.z, p.x, A)[...]) + f32(wide[0, 1]) + f32(wide[1, 1])
    mine_b = f32(blk(p.z, p.x, B)[...]) + f32(zb[3]) + f32(bw[0]) + f32(bw[1])
    for copy in singles:
        copy.wait_recv()
    single = pe[p.t]
    for k in range(1, 8):
        single = single + eb[k]
    a_z.wait_recv()
    return jnp.concatenate([mine_a + f32(za[...]), mine_b], axis=1), single


def sum_bufs():
    bf = jnp.bfloat16
    return [pltpu.VMEM((2, 2, 64, 512), bf), pltpu.VMEM((2, 2, 64, 1024), bf), pltpu.VMEM((4, 64, 1024), bf),
            pltpu.VMEM((2, 64, 512), bf), pltpu.VMEM((2, 64, 1024), bf), pltpu.VMEM((64, 1024), bf),
            pltpu.VMEM((8, 1, 2048), jnp.float32)]


def wide_row(gain):
    rows = gain[...].astype(jnp.float32)
    return jnp.concatenate([rows[i:i + 1] for i in range(16)], axis=1)


def scaled(values, gain):
    mean_square = jnp.mean(values * values, axis=-1, keepdims=True)
    return (values * lax.rsqrt(mean_square + 1e-05) * gain).astype(jnp.bfloat16)


def place_singles(ext, xall):
    rows = [ext[e] for e in range(8)]
    xall[512:528, :] = jnp.concatenate(rows + [jnp.zeros((8, 2048), jnp.float32)], axis=0).astype(jnp.bfloat16)


def tail_kernel(att, hidden, gain, wo_h, wg_h, wu_h, wd_h, out, *s):
    (wo, wg, wu, wd, part, pe, xall, ext, hid, res, part2, pe2), s = s[:12], s[12:]
    bufs1, bufs2, (send_sem, recv_sem, wsem) = s[:7], s[7:14], s[14:]
    loads = [pltpu.make_async_copy(a, b, wsem.at[i]) for i, (a, b) in enumerate(((wo_h, wo), (wg_h, wg), (wu_h, wu), (wd_h, wd)))]
    for load in loads:
        load.start()
    p = Place()
    links = Links(send_sem, recv_sem)
    greet_group(p)
    loads[0].wait()

    def project(lhs, weights, part, pe):
        def produce(q):
            y = jnp.dot(lhs[...], weights[:, QUARTERS[q]], preferred_element_type=jnp.float32)
            part[:, QUARTERS[q]] = y[:512].astype(jnp.bfloat16)
            for e in range(8):
                pe[e, :, QUARTERS[q]] = y[512 + e:513 + e]
        return produce

    gains = wide_row(gain)
    main, single = scatter_sums(links, p, project(att, wo, part, pe), part, pe, bufs1)
    main = f32(hidden[0:64, :]) + main
    single = f32(hidden[64:65, :]) + single
    res[0:64, :] = main
    res[64:65, :] = single
    xall[rows_of(p.t), :] = scaled(main, gains)
    ext[p.t] = f32(scaled(single, gains))
    gather_rows(links, p, xall, ext)
    place_singles(ext, xall)
    loads[1].wait()
    loads[2].wait()
    for lo, n in ((0, 256), (256, 256), (512, 192)):
        g = lax.dot_general(xall[...], wg[lo:lo + n, :], NT, preferred_element_type=jnp.float32)
        u = lax.dot_general(xall[...], wu[lo:lo + n, :], NT, preferred_element_type=jnp.float32)
        hid[:, lo:lo + n] = (g / (1.0 + jnp.exp(-g)) * u).astype(jnp.bfloat16)
    loads[3].wait()
    main, single = scatter_sums(links, p, project(hid, wd, part2, pe2), part2, pe2, bufs2)
    out[0:64, :] = (res[0:64, :] + main).astype(jnp.bfloat16)
    out[64:65, :] = (res[64:65, :] + single).astype(jnp.bfloat16)
    links.drain()


def tail_call(att, hidden, gain, w_out, w_gate, w_up, w_down):
    w_gate, w_up = w_gate.T, w_up.T
    vm = pl.BlockSpec(memory_space=pltpu.VMEM)
    hbm = pl.BlockSpec(memory_space=pltpu.HBM)
    bf, fl = jnp.bfloat16, jnp.float32
    scratch = [pltpu.VMEM(w_out.shape, bf), pltpu.VMEM(w_gate.shape, bf), pltpu.VMEM(w_up.shape, bf), pltpu.VMEM(w_down.shape, bf),
               pltpu.VMEM((512, 2048), bf), pltpu.VMEM((8, 1, 2048), fl), pltpu.VMEM((528, 2048), bf), pltpu.VMEM((8, 1, 2048), fl),
               pltpu.VMEM((528, w_gate.shape[0]), bf), pltpu.VMEM((65, 2048), fl), pltpu.VMEM((512, 2048), bf), pltpu.VMEM((8, 1, 2048), fl)]
    scratch += sum_bufs() + sum_bufs()
    scratch += [pltpu.SemaphoreType.DMA((80,)), pltpu.SemaphoreType.DMA((80,)), pltpu.SemaphoreType.DMA((4,))]
    return pl.pallas_call(
        tail_kernel,
        out_shape=jax.ShapeDtypeStruct((65, 2048), bf),
        in_specs=[vm, vm, vm, hbm, hbm, hbm, hbm],
        out_specs=vm,
        scratch_shapes=scratch,
        compiler_params=pltpu.CompilerParams(vmem_limit_bytes=60 << 20, collective_id=1, has_side_effects=True),
        cost_estimate=pl.CostEstimate(flops=52 * 10**8, bytes_accessed=11 * 10**6, transcendentals=10**6),
        name="out_and_mlp",
    )(att, hidden, gain.reshape(16, 128), w_out, w_gate, w_up, w_down)


def interleave(*chains):
    chains = list(chains)
    while chains:
        for chain in list(chains):
            if next(chain, None) is None:
                chains.remove(chain)


class Ring:
    def __init__(self):
        self.o = lax.axis_index("kv")
        self.y, rest = lax.div(self.o, 4), lax.rem(self.o, 4)
        self.h, self.c = lax.div(rest, 2), lax.rem(rest, 2)
        self.yr, self.yl, self.opp = lax.rem(self.y + 1, 4), lax.rem(self.y + 3, 4), lax.rem(self.y + 2, 4)
        self.oh = 1 - self.h
        self.right, self.left = {"kv": self.at(self.yr, self.h)}, {"kv": self.at(self.yl, self.h)}
        self.mate, self.twin = {"kv": self.at(self.y, self.oh)}, {"kv": self.o + 1 - 2 * self.c}

    def at(self, y, h):
        return y * 4 + h * 2 + self.c


def gather_cache(links, r, kv):
    top, low, whole = pl.ds(0, 512), pl.ds(512, 512), pl.ds(0, 1024)
    twins = []
    def go(y, h, rows, where):
        at = kv.at[r.at(y, h), rows, :]
        return links.send(at, at, where)
    def share(y, h, rows):
        twins.append(go(y, h, rows, r.twin))
    m = go(r.y, r.h, whole, r.mate)
    a = go(r.y, r.h, whole, r.right), go(r.y, r.h, whole, r.left)
    share(r.y, r.h, whole)
    yield 1
    m.wait_recv()
    b = go(r.y, r.oh, whole, r.right), go(r.y, r.oh, whole, r.left)
    share(r.y, r.oh, whole)
    yield 1
    ends = []
    for (from_left, from_right), h in ((a, r.h), (b, r.oh)):
        from_left.wait_recv()
        ends.append((go(r.yl, h, top, r.right), h, top))
        share(r.yl, h, whole)
        yield 1
        from_right.wait_recv()
        ends.append((go(r.yr, h, low, r.left), h, low))
        share(r.yr, h, whole)
        yield 1
    for copy, h, rows in ends:
        copy.wait_recv()
        share(r.opp, h, rows)
        yield 1
    for copy in twins:
        copy.wait_recv()


def head_kernel(hidden, gain, freq, leaf_length, prompt_leaf, decode_leaf, wq_h, wk_h, wv_h, ck_h, cv_h,
                q_out, qt_out, own_out, kv_out, kv, xall, ext, w, ck, cv, cos, sin, send_sem, recv_sem, wsem, osem):
    p, r = Place(), Ring()
    links = Links(send_sem, recv_sem)
    head = lax.div(p.t, 2)
    odd = lax.rem(head, 2)
    pair = pl.ds(pl.multiple_of(lax.div(head, 2) * 128, 128), 128)
    loads = [pltpu.make_async_copy(ck_h.at[:, pair], ck, wsem.at[0]), pltpu.make_async_copy(cv_h.at[:, pair], cv, wsem.at[1]),
             pltpu.make_async_copy(wq_h, w.at[:, 0:256], wsem.at[2]), pltpu.make_async_copy(wk_h.at[:, pair], w.at[:, 256:384], wsem.at[3]),
             pltpu.make_async_copy(wv_h.at[:, pair], w.at[:, 384:512], wsem.at[4])]
    for load in loads:
        load.start()
    barrier = pltpu.get_barrier_semaphore()
    for where in [{"tp": p.peer(k)} for k in range(1, 8)] + [r.right, r.left, r.mate, r.twin]:
        pl.semaphore_signal(barrier, inc=1, device_id=where, device_id_type=MESH)
    gains = wide_row(gain)
    xall[rows_of(p.t), :] = scaled(f32(hidden[0:64, :]), gains)
    ext[p.t] = f32(scaled(f32(hidden[64:65, :]), gains))
    loads[0].wait()
    loads[1].wait()
    lane = lax.broadcasted_iota(jnp.int32, (1, 128), 1)

    def joined(keys, values):
        k = jnp.where(odd == 1, pltpu.roll(keys, 64, 1), keys)
        v = jnp.where(odd == 1, values, pltpu.roll(values, 64, 1))
        return jnp.where(lane < 64, k, v)

    kv[r.o] = joined(f32(ck[...]), f32(cv[...])).astype(jnp.bfloat16)
    pl.semaphore_wait(barrier, 11)

    rows = gather_rows_steps(links, p, xall, ext)
    cache = gather_cache(links, r, kv)
    next(rows)
    next(cache)
    a = r.o
    token = token_of(lax.broadcasted_iota(jnp.int32, (528, 1), 0))
    base = jnp.full((528, 1), leaf_length[prompt_leaf[a]], jnp.int32) + token
    for i in range(8):
        base = jnp.where(token == 512 + i, leaf_length[decode_leaf[a * 8 + i]], base)
    angle = (base + 5120).astype(jnp.float32) * freq[...]
    cos[...] = jnp.cos(angle)
    sin[...] = jnp.sin(angle)
    interleave(rows, cache)
    place_singles(ext, xall)
    for load in loads[2:]:
        load.wait()

    def rotated(x):
        turned = jnp.where(lane % 64 < 32, -pltpu.roll(x, 96, 1), pltpu.roll(x, 32, 1))
        return x * cos[...] + turned * sin[...]

    y = jnp.dot(xall[...], w[...], preferred_element_type=jnp.float32)
    zero = jnp.zeros((528, 128), jnp.float32)
    for i in range(2):
        q = f32(rotated(y[:, 128 * i:128 * i + 128]).astype(jnp.bfloat16)) * 0.125
        for j, x in enumerate((q, pltpu.roll(q, 64, 1))):
            x = jnp.where(lane < 64, x, zero)
            q_out[2 * i + j] = x[:512].astype(jnp.bfloat16)
            qt_out[2 * i + j] = x[504:520].astype(jnp.bfloat16)
    own_out[0:528, :] = joined(rotated(y[:, 256:384]), y[:, 384:512]).astype(jnp.bfloat16)
    own_out[528:640, :] = jnp.zeros((112, 128), jnp.bfloat16)
    out = pltpu.make_async_copy(kv, kv_out, osem)
    out.start()
    out.wait()
    links.drain()


def head_call(hidden, gain, freq, leaf_length, prompt_leaf, decode_leaf, w_query, w_key, w_value, cache_keys, cache_values):
    vm = pl.BlockSpec(memory_space=pltpu.VMEM)
    sm = pl.BlockSpec(memory_space=pltpu.SMEM)
    hbm = pl.BlockSpec(memory_space=pltpu.HBM)
    bf, fl = jnp.bfloat16, jnp.float32
    return pl.pallas_call(
        head_kernel,
        out_shape=(jax.ShapeDtypeStruct((4, 512, 128), bf), jax.ShapeDtypeStruct((4, 16, 128), bf),
                   jax.ShapeDtypeStruct((640, 128), bf), jax.ShapeDtypeStruct((16, 1024, 128), bf)),
        in_specs=[vm, vm, vm, sm, sm, sm] + [hbm] * 5,
        out_specs=(vm, vm, vm, hbm),
        scratch_shapes=[pltpu.VMEM((16, 1024, 128), bf), pltpu.VMEM((528, 2048), bf), pltpu.VMEM((8, 1, 2048), fl), pltpu.VMEM((2048, 512), bf),
                        pltpu.VMEM((1024, 128), bf), pltpu.VMEM((1024, 128), bf), pltpu.VMEM((528, 128), fl), pltpu.VMEM((528, 128), fl),
                        pltpu.SemaphoreType.DMA((60,)), pltpu.SemaphoreType.DMA((60,)), pltpu.SemaphoreType.DMA((5,)), pltpu.SemaphoreType.DMA],
        compiler_params=pltpu.CompilerParams(vmem_limit_bytes=60 << 20, collective_id=2, has_side_effects=True),
        cost_estimate=pl.CostEstimate(flops=10**9, bytes_accessed=10 * 10**6, transcendentals=10**5),
        name="gathers_and_qkv",
    )(hidden, gain.reshape(16, 128), freq, leaf_length, prompt_leaf, decode_leaf, w_query, w_key, w_value, cache_keys, cache_values)


def per_device(hidden_in, norm_attn, w_query, w_key, w_value, w_out, norm_mlp, w_gate, w_up, w_down,
               cache_keys, cache_values, leaf_parent, leaf_owner, leaf_length, prompt_leaf, decode_leaf):
    freq = 10000.0 ** (-((np.arange(128) % 32).astype(np.float32) * np.float32(2.0) / np.float32(64)))
    freq = jnp.asarray(freq.astype(np.float32)[None, :])
    q, qtail, own, kv = head_call(hidden_in, norm_attn, freq, leaf_length, prompt_leaf, decode_leaf,
                                  w_query, w_key, w_value, cache_keys, cache_values)
    attended, att = attn_call((leaf_parent, leaf_owner, leaf_length, prompt_leaf, decode_leaf), q, qtail,
                              kv.reshape(16 * 1024, 128), own)
    return tail_call(att, hidden_in, norm_mlp, w_out, w_gate, w_up, w_down), attended


def solution(mesh):
    in_specs = (P(("kv", "tp"), None), P(), P(None, "tp"), P(), P(), P("tp", None), P(), P(None, "tp"), P(None, "tp"),
                P("tp", None), P("kv", None), P("kv", None), P(), P(), P(), P(), P())
    out_specs = (P(("kv", "tp"), None), P("kv", "tp"))
    return jax.shard_map(per_device, mesh=mesh, in_specs=in_specs, out_specs=out_specs, check_vma=False)
```

```python
import jax
import jax.numpy as jnp
import numpy as np
from jax import lax
from jax.experimental import pallas as pl
from jax.experimental.pallas import tpu as pltpu
from jax.sharding import PartitionSpec as P

NEG = -1e30
NT = (((1,), (1,)), ((), ()))

def flash_many(st, qb, items):
    ss=lax.dot_general(qb, items[0][0], NT, preferred_element_type=jnp.float32)
    for i,(kvb,mask) in enumerate(items):
        nx = lax.dot_general(qb, items[i+1][0], NT, preferred_element_type=jnp.float32) if i+1<len(items) else None
        st = flash_step(st, qb, kvb, mask, ss)
        ss = nx
    return st

def flash_step(state, qb, kvb, mask, s=None):
    m, acc = state
    if s is None:
        s = lax.dot_general(qb, kvb, NT, preferred_element_type=jnp.float32)
    if mask is not None:
        s = jnp.where(mask, s, NEG)
    m_new = jnp.maximum(m, jnp.max(s, axis=1, keepdims=True))
    p = jnp.exp(s - m_new).astype(jnp.bfloat16)
    lane = lax.broadcasted_iota(jnp.int32, kvb.shape, 1)
    vaug = jnp.where(lane < 64, jnp.ones_like(kvb), kvb)
    acc = acc * jnp.exp(m - m_new) + jnp.dot(p, vaug, preferred_element_type=jnp.float32)
    return m_new, acc

def finish(state, rows):
    m, acc = state
    ratio = pltpu.roll(acc, 64, 1) / acc
    h = [ratio[i * rows:(i + 1) * rows] for i in range(4)]
    lane = lax.broadcasted_iota(jnp.int32, (rows, 128), 1)
    a = jnp.where(lane < 64, h[0], pltpu.roll(h[1], 64, 1))
    b = jnp.where(lane < 64, h[2], pltpu.roll(h[3], 64, 1))
    return jnp.concatenate([a, b], axis=1)

def token_of(idx):
    return jnp.where(idx < 512, 65 * (idx // 64) + idx % 64,
                     jnp.where(idx < 520, 65 * (idx - 512) + 64, 1 << 20))

MESH = pl.DeviceIdType.MESH
A = pl.ds(0, 1024)
B = pl.ds(1024, 1024)
QUARTERS = tuple(pl.ds(512 * i, 512) for i in range(4))
A0, A1, B0, B1 = QUARTERS


class Transfer:
    def __init__(self, links, k, src, dst, where):
        self.parts = links, k, src, dst, where

    def copy(self):
        links, k, src, dst, where = self.parts
        return pltpu.make_async_remote_copy(src_ref=src(), dst_ref=dst(), send_sem=links.send_sem.at[k], recv_sem=links.recv_sem.at[k],
                                            device_id=where, device_id_type=MESH)

    def start(self):
        self.copy().start()
        return self

    def wait_recv(self):
        self.copy().wait_recv()

    def wait_send(self):
        self.copy().wait_send()


class Links:
    def __init__(self, send_sem, recv_sem):
        self.send_sem, self.recv_sem, self.open = send_sem, recv_sem, []

    def plan(self, src, dst, where):
        self.open.append(Transfer(self, len(self.open), src, dst, where))
        return self.open[-1]

    def send(self, src, dst, where):
        return self.plan(lambda: src, lambda: dst, where).start()

    def drain(self):
        for transfer in self.open:
            transfer.wait_send()


class Place:
    def __init__(self):
        self.t = lax.axis_index("tp")
        self.z, self.x = lax.div(self.t, 4), lax.rem(self.t, 4)
        self.xr, self.xl, self.opp = lax.rem(self.x + 1, 4), lax.rem(self.x + 3, 4), lax.rem(self.x + 2, 4)
        self.oz = 1 - self.z
        self.right = {"tp": self.z * 4 + self.xr}
        self.left = {"tp": self.z * 4 + self.xl}
        self.mate = {"tp": self.oz * 4 + self.x}

    def peer(self, k):
        return lax.rem(self.t + k, 8)


def rows_of(rank):
    return pl.ds(pl.multiple_of(rank * 64, 64), 64)


def gather_rows_steps(links, p, xall, ext):
    def blk(z, x, cols):
        return xall.at[rows_of(z * 4 + x), cols]
    def go(z, x, cols, where):
        return links.send(blk(z, x, cols), blk(z, x, cols), where)
    az = go(p.z, p.x, A, p.mate)
    br, bl = go(p.z, p.x, B, p.right), go(p.z, p.x, B, p.left)
    ar, al = go(p.z, p.x, A, p.right), go(p.z, p.x, A, p.left)
    bz = [go(p.z, p.x, B, p.mate)]
    singles = [links.send(ext.at[p.t], ext.at[p.t], {"tp": p.peer(k)}) for k in range(1, 8)]
    yield 1
    br.wait_recv()
    last = [go(p.z, p.xl, B0, p.right)]
    bz.append(go(p.z, p.xl, B, p.mate))
    yield 1
    bl.wait_recv()
    last.append(go(p.z, p.xr, B1, p.left))
    bz.append(go(p.z, p.xr, B, p.mate))
    yield 1
    az.wait_recv()
    far_r, far_l = go(p.oz, p.x, A, p.right), go(p.oz, p.x, A, p.left)
    yield 1
    ar.wait_recv()
    ends = [go(p.z, p.xl, A0, p.right)]
    yield 1
    al.wait_recv()
    ends.append(go(p.z, p.xr, A1, p.left))
    yield 1
    last[0].wait_recv()
    bz.append(go(p.z, p.opp, B0, p.mate))
    last[1].wait_recv()
    bz.append(go(p.z, p.opp, B1, p.mate))
    yield 1
    far_r.wait_recv()
    ends.append(go(p.oz, p.xl, A0, p.right))
    yield 1
    far_l.wait_recv()
    ends.append(go(p.oz, p.xr, A1, p.left))
    yield 1
    for copy in ends + bz + singles:
        copy.wait_recv()


def gather_rows(links, p, xall, ext):
    for _ in gather_rows_steps(links, p, xall, ext):
        pass


def f32(x):
    return x.astype(jnp.float32)


def scatter_sums(links, p, produce, part, pe, bufs):
    near, wide, zb, bq, bw, za, eb = bufs
    planes = (p.oz, p.z)
    def blk(z, x, cols):
        return part.at[rows_of(z * 4 + x), cols]
    def add(z, x, cols, more):
        at = blk(z, x, cols)
        at[...] = (f32(at[...]) + f32(more)).astype(jnp.bfloat16)
    produce(2)
    produce(3)
    order = (p.opp, p.xr, p.xl, p.x)
    bz = [links.send(blk(p.oz, xd, B), zb.at[i], p.mate) for i, xd in enumerate(order)]
    produce(0)
    ar = [links.send(blk(z, p.opp, A0), near.at[0, i], p.right) for i, z in enumerate(planes)]
    produce(1)
    al = [links.send(blk(z, p.opp, A1), near.at[1, i], p.left) for i, z in enumerate(planes)]
    singles = [links.send(pe.at[p.peer(k)], eb.at[k], {"tp": p.peer(k)}) for k in range(1, 8)]
    bz[0].wait_recv()
    add(p.z, p.opp, B, zb[0])
    b_r = links.send(blk(p.z, p.opp, B0), bq.at[0], p.right)
    b_l = links.send(blk(p.z, p.opp, B1), bq.at[1], p.left)
    wr, wl = [], []
    for i, z in enumerate(planes):
        ar[i].wait_recv()
        add(z, p.xr, A0, near[0, i])
        wr.append(links.send(blk(z, p.xr, A), wide.at[0, i], p.right))
        al[i].wait_recv()
        add(z, p.xl, A1, near[1, i])
        wl.append(links.send(blk(z, p.xl, A), wide.at[1, i], p.left))
    bz[1].wait_recv()
    add(p.z, p.xr, B, zb[1])
    b_r.wait_recv()
    add(p.z, p.xr, B0, bq[0])
    b_rw = links.send(blk(p.z, p.xr, B), bw.at[0], p.right)
    bz[2].wait_recv()
    add(p.z, p.xl, B, zb[2])
    b_l.wait_recv()
    add(p.z, p.xl, B1, bq[1])
    b_lw = links.send(blk(p.z, p.xl, B), bw.at[1], p.left)
    wr[0].wait_recv()
    wl[0].wait_recv()
    add(p.oz, p.x, A, f32(wide[0, 0]) + f32(wide[1, 0]))
    a_z = links.send(blk(p.oz, p.x, A), za, p.mate)
    for copy in (wr[1], wl[1], bz[3], b_rw, b_lw):
        copy.wait_recv()
    mine_a = f32(blk(p.z, p.x, A)[...]) + f32(wide[0, 1]) + f32(wide[1, 1])
    mine_b = f32(blk(p.z, p.x, B)[...]) + f32(zb[3]) + f32(bw[0]) + f32(bw[1])
    for copy in singles:
        copy.wait_recv()
    single = pe[p.t]
    for k in range(1, 8):
        single = single + eb[k]
    a_z.wait_recv()
    return jnp.concatenate([mine_a + f32(za[...]), mine_b], axis=1), single


def sum_bufs():
    bf = jnp.bfloat16
    return [pltpu.VMEM((2, 2, 64, 512), bf), pltpu.VMEM((2, 2, 64, 1024), bf), pltpu.VMEM((4, 64, 1024), bf),
            pltpu.VMEM((2, 64, 512), bf), pltpu.VMEM((2, 64, 1024), bf), pltpu.VMEM((64, 1024), bf),
            pltpu.VMEM((8, 1, 2048), jnp.float32)]


def wide_row(gain):
    rows = gain[...].astype(jnp.float32)
    return jnp.concatenate([rows[i:i + 1] for i in range(16)], axis=1)


def scaled(values, gain):
    mean_square = jnp.mean(values * values, axis=-1, keepdims=True)
    return (values * lax.rsqrt(mean_square + 1e-05) * gain).astype(jnp.bfloat16)


def place_singles(ext, xall):
    rows = [ext[e] for e in range(8)]
    xall[512:528, :] = jnp.concatenate(rows + [jnp.zeros((8, 2048), jnp.float32)], axis=0).astype(jnp.bfloat16)


class Ring:
    def __init__(self):
        self.o = lax.axis_index("kv")
        self.y, rest = lax.div(self.o, 4), lax.rem(self.o, 4)
        self.h, self.c = lax.div(rest, 2), lax.rem(rest, 2)
        self.yr, self.yl, self.opp = lax.rem(self.y + 1, 4), lax.rem(self.y + 3, 4), lax.rem(self.y + 2, 4)
        self.oh = 1 - self.h
        self.right, self.left = {"kv": self.at(self.yr, self.h)}, {"kv": self.at(self.yl, self.h)}
        self.mate, self.twin = {"kv": self.at(self.y, self.oh)}, {"kv": self.o + 1 - 2 * self.c}

    def at(self, y, h):
        return y * 4 + h * 2 + self.c


def gather_cache(links, r, kv):
    top, low, whole = (0, 512), (512, 512), (0, 1024)
    twins = []
    def go(y, h, rows, where):
        at = kv.at[pl.ds(pl.multiple_of(r.at(y, h) * 1024 + rows[0], 512), rows[1]), :]
        return links.send(at, at, where)
    def share(y, h, rows):
        twins.append(go(y, h, rows, r.twin))
    m = go(r.y, r.h, whole, r.mate)
    a = go(r.y, r.h, whole, r.right), go(r.y, r.h, whole, r.left)
    share(r.y, r.h, whole)
    yield 1
    m.wait_recv()
    b = go(r.y, r.oh, whole, r.right), go(r.y, r.oh, whole, r.left)
    share(r.y, r.oh, whole)
    yield 1
    ends = []
    for (from_left, from_right), h in ((a, r.h), (b, r.oh)):
        from_left.wait_recv()
        ends.append((go(r.yl, h, top, r.right), h, top))
        share(r.yl, h, whole)
        yield 1
        from_right.wait_recv()
        ends.append((go(r.yr, h, low, r.left), h, low))
        share(r.yr, h, whole)
        yield 1
    for copy, h, rows in ends:
        copy.wait_recv()
        share(r.opp, h, rows)
        yield 1
    for copy in twins:
        copy.wait_recv()


def early_sums(links, p, part, pe, bufs):
    near, wide, zb, bq, bw, za, eb = bufs
    planes = (p.oz, p.z)
    order = (p.opp, p.xr, p.xl, p.x)
    def blk(z, x, cols):
        return part.at[rows_of(z * 4 + x), cols]
    def add(z, x, cols, more):
        at = blk(z, x, cols)
        at[...] = (f32(at[...]) + f32(more)).astype(jnp.bfloat16)
    def plan(z, x, cols, dst, where):
        return links.plan(lambda: blk(z, x, cols), dst, where)
    bz = [plan(p.oz, xd, B, lambda i=i: zb.at[i], p.mate) for i, xd in enumerate(order)]
    ar = [plan(z, p.opp, A0, lambda i=i: near.at[0, i], p.right) for i, z in enumerate(planes)]
    al = [plan(z, p.opp, A1, lambda i=i: near.at[1, i], p.left) for i, z in enumerate(planes)]
    wr = [plan(z, p.xr, A, lambda i=i: wide.at[0, i], p.right) for i, z in enumerate(planes)]
    wl = [plan(z, p.xl, A, lambda i=i: wide.at[1, i], p.left) for i, z in enumerate(planes)]
    b_r, b_l = plan(p.z, p.opp, B0, lambda: bq.at[0], p.right), plan(p.z, p.opp, B1, lambda: bq.at[1], p.left)
    b_rw, b_lw = plan(p.z, p.xr, B, lambda: bw.at[0], p.right), plan(p.z, p.xl, B, lambda: bw.at[1], p.left)
    a_z = plan(p.oz, p.x, A, lambda: za, p.mate)
    singles = [links.plan(lambda k=k: pe.at[p.peer(k)], lambda k=k: eb.at[k], {"tp": p.peer(k)}) for k in range(1, 8)]

    def step0():
        for copy in [bz[0]] + ar + al + singles:
            copy.start()

    def step1():
        bz[1].start()
        bz[0].wait_recv()
        add(p.z, p.opp, B, zb[0])
        b_r.start()
        b_l.start()
        for i, z in enumerate(planes):
            ar[i].wait_recv()
            add(z, p.xr, A0, near[0, i])
            wr[i].start()

    def step2():
        bz[2].start()
        for i, z in enumerate(planes):
            al[i].wait_recv()
            add(z, p.xl, A1, near[1, i])
            wl[i].start()
        bz[1].wait_recv()
        add(p.z, p.xr, B, zb[1])
        b_r.wait_recv()
        add(p.z, p.xr, B0, bq[0])
        b_rw.start()

    def step3():
        bz[3].start()
        bz[2].wait_recv()
        add(p.z, p.xl, B, zb[2])
        b_l.wait_recv()
        add(p.z, p.xl, B1, bq[1])
        b_lw.start()
        wr[0].wait_recv()
        wl[0].wait_recv()
        add(p.oz, p.x, A, f32(wide[0, 0]) + f32(wide[1, 0]))
        a_z.start()

    def finish_sums():
        wr[1].wait_recv()
        wl[1].wait_recv()
        mine_a = f32(blk(p.z, p.x, A)[...]) + f32(wide[0, 1]) + f32(wide[1, 1])
        for copy in singles:
            copy.wait_recv()
        single = pe[p.t]
        for k in range(1, 8):
            single = single + eb[k]
        for copy in (b_rw, bz[3], a_z, b_lw):
            copy.wait_recv()
        mine_b = f32(blk(p.z, p.x, B)[...]) + f32(zb[3]) + f32(bw[0]) + f32(bw[1])
        return jnp.concatenate([mine_a + f32(za[...]), mine_b], axis=1), single

    return (step0, step1, step2, step3), finish_sums


def layer_kernel(hidden, gain_a, gain_m, freq, leaf_parent, leaf_owner, leaf_length, prompt_leaf, decode_leaf,
                 wq_h, wk_h, wv_h, ck_h, cv_h, wo_h, wg_h, wu_h, wd_h, out, att_out, *s):
    (kv, xin, ein, w, ck, cv, cos, sin, qs, qt, own, main, tail, joint, near_kv), s = s[:15], s[15:]
    (wo, wg, wu, wd, part, pe, xall, ext, hid, res, part2, pe2), s = s[:12], s[12:]
    bufs1, bufs2, (send_sem, recv_sem, wsem) = s[:7], s[7:14], s[14:]
    p, r = Place(), Ring()
    links = Links(send_sem, recv_sem)
    head = lax.div(p.t, 2)
    odd = lax.rem(head, 2)
    pair = pl.ds(pl.multiple_of(lax.div(head, 2) * 128, 128), 128)
    moves = ((ck_h.at[:, pair], ck), (cv_h.at[:, pair], cv), (wq_h, w.at[:, 0:256]), (wk_h.at[:, pair], w.at[:, 256:384]),
             (wv_h.at[:, pair], w.at[:, 384:512]), (wo_h, wo), (wg_h, wg), (wu_h, wu), (wd_h, wd))
    loads = [pltpu.make_async_copy(a, b, wsem.at[i]) for i, (a, b) in enumerate(moves)]
    for load in loads:
        load.start()
    barrier = pltpu.get_barrier_semaphore()
    for where in [{"tp": p.peer(k)} for k in range(1, 8)] + [r.right, r.left, r.mate, r.twin]:
        pl.semaphore_signal(barrier, inc=1, device_id=where, device_id_type=MESH)
    gains = wide_row(gain_a)
    xin[rows_of(p.t), :] = scaled(f32(hidden[0:64, :]), gains)
    ein[p.t] = f32(scaled(f32(hidden[64:65, :]), gains))
    loads[0].wait()
    loads[1].wait()
    lane = lax.broadcasted_iota(jnp.int32, (1, 128), 1)

    def joined(keys, values):
        k = jnp.where(odd == 1, pltpu.roll(keys, 64, 1), keys)
        v = jnp.where(odd == 1, values, pltpu.roll(values, 64, 1))
        return jnp.where(lane < 64, k, v)

    kv[pl.ds(pl.multiple_of(r.o * 1024, 1024), 1024), :] = joined(f32(ck[...]), f32(cv[...])).astype(jnp.bfloat16)
    pl.semaphore_wait(barrier, 11)

    rows = gather_rows_steps(links, p, xin, ein)
    cache = gather_cache(links, r, kv)
    next(rows)
    next(cache)
    me = r.o
    my_leaf = prompt_leaf[me]
    my_owner = leaf_owner[my_leaf]
    my_length = leaf_length[my_leaf]
    my_branch = leaf_parent[my_leaf]
    token = token_of(lax.broadcasted_iota(jnp.int32, (528, 1), 0))
    spot = my_length + token
    for i in range(8):
        spot = jnp.where(token == 512 + i, leaf_length[decode_leaf[me * 8 + i]], spot)
    angle = (spot + 5120).astype(jnp.float32) * freq[...]
    cos[...] = jnp.cos(angle)
    sin[...] = jnp.sin(angle)
    branch_of, length_of, place_of, count = [], [], [], jnp.int32(0)
    for o in range(16):
        branch, length = jnp.int32(0), jnp.int32(0)
        for leaf in range(16):
            held = leaf_owner[leaf] == o
            branch = jnp.where(held, leaf_parent[leaf], branch)
            length = jnp.where(held, leaf_length[leaf], length)
        branch_of.append(branch)
        length_of.append(length)
        place_of.append(jnp.where(branch == my_branch, count, 4))
        count = count + jnp.where(branch == my_branch, 1, 0)
    for turn in "rrrcccrrrrrccr":
        next(rows if turn == "r" else cache, None)
    place_singles(ein, xin)
    for load in loads[2:5]:
        load.wait()

    def rotated(x):
        turned = jnp.where(lane % 64 < 32, -pltpu.roll(x, 96, 1), pltpu.roll(x, 32, 1))
        return x * cos[...] + turned * sin[...]

    y = jnp.dot(xin[...], w[...], preferred_element_type=jnp.float32)
    zero = jnp.zeros((528, 128), jnp.float32)
    for i in range(2):
        q = f32(rotated(y[:, 128 * i:128 * i + 128]).astype(jnp.bfloat16)) * 0.125
        for j, x in enumerate((q, pltpu.roll(q, 64, 1))):
            x = jnp.where(lane < 64, x, zero)
            qs[2 * i + j] = x[:512].astype(jnp.bfloat16)
            qt[2 * i + j] = x[504:520].astype(jnp.bfloat16)
    own[0:528, :] = joined(rotated(y[:, 256:384]), y[:, 384:512]).astype(jnp.bfloat16)
    own[528:640, :] = jnp.zeros((112, 128), jnp.bfloat16)
    for _ in cache:
        pass

    for i in range(4):
        got = kv[256:512, :]
        for o in range(1, 16):
            got = jnp.where(place_of[o] == i, kv[o * 1024 + 256:o * 1024 + 512, :], got)
        near_kv[256 * i:256 * i + 256, :] = got
    got = kv[512:1024, :]
    for o in range(1, 16):
        got = jnp.where(my_owner == o, kv[o * 1024 + 512:o * 1024 + 1024, :], got)
    near_kv[1024:1536, :] = got
    near_kv[1536:2176, :] = own[...]

    def start(n):
        return jnp.full((n, 1), NEG, jnp.float32), jnp.zeros((n, 128), jnp.float32)

    qb = jnp.concatenate([qt[h] for h in range(4)], axis=0)
    row = lax.broadcasted_iota(jnp.int32, (64, 1), 0) % 16
    r_tok = jnp.where(row < 8, 511 + row, 65 * (row - 8) + 64)
    r_owner = jnp.full((64, 1), my_owner, jnp.int32)
    r_branch = jnp.full((64, 1), my_branch, jnp.int32)
    for i in range(8):
        leaf = decode_leaf[me * 8 + i]
        r_owner = jnp.where(r_tok == 512 + i, leaf_owner[leaf], r_owner)
        r_branch = jnp.where(r_tok == 512 + i, leaf_parent[leaf], r_branch)
    items = []
    col = lax.broadcasted_iota(jnp.int32, (1, 1024), 1)
    for o in range(16):
        see_branch = jnp.where(r_branch == branch_of[o], 512, 256)
        see_leaf = jnp.where(r_owner == o, 512 + length_of[o], 512)
        items.append((kv[o * 1024:o * 1024 + 1024, :], (col < see_branch) | ((col >= 512) & (col < see_leaf))))
    ktok = token_of(lax.broadcasted_iota(jnp.int32, (1, 640), 1))
    items.append((own[...], (ktok == r_tok) | ((ktok <= r_tok) & (r_tok < 512))))
    tail[...] = finish(flash_many(start(64), qb, items), 16)
    loads[5].wait()
    singles = jnp.concatenate([tail[8:16, :], jnp.zeros((8, 256), jnp.float32)], axis=0).astype(jnp.bfloat16)
    y = jnp.dot(singles, wo[...], preferred_element_type=jnp.float32)
    for e in range(8):
        pe[e] = y[e:e + 1]

    steps, finish_sums = early_sums(links, p, part, pe, bufs1)

    def two_ranks(i, _):
        xd = (p.x + 2 + 3 * i + 3 * (i // 2) + 2 * (i // 3)) % 4
        ranks = (p.oz * 4 + xd, p.z * 4 + xd)
        qb = jnp.concatenate([qs[h, rows_of(rank), :] for h in range(4) for rank in ranks], axis=0)
        items = [(jnp.concatenate([kv[g * 4096 + i * 1024:g * 4096 + i * 1024 + 256, :] for i in range(4)], axis=0), None) for g in range(4)]
        items.append((near_kv[0:1024, :], None))
        col = lax.broadcasted_iota(jnp.int32, (1, 1152), 1)
        at = lax.broadcasted_iota(jnp.int32, (512, 1), 0) % 128
        rtok = jnp.where(at < 64, 65 * ranks[0] + at, 65 * ranks[1] + at - 64)
        ktok = jnp.where(col < 512, jnp.where(col < my_length, -1, 1 << 20), token_of(col - 512))
        items.append((near_kv[1024:2176, :], ktok <= rtok))
        got = finish(flash_many(start(512), qb, items), 128)
        for j, rank in enumerate(ranks):
            main[rows_of(rank), :] = got[64 * j:64 * j + 64]
        main[504:512, :] = tail[0:8, :]
        lhs = jnp.concatenate([main[rows_of(rank), :] for rank in ranks], axis=0).astype(jnp.bfloat16)
        for quarter in QUARTERS:
            y = jnp.dot(lhs, wo[:, quarter], preferred_element_type=jnp.float32).astype(jnp.bfloat16)
            for j, rank in enumerate(ranks):
                part[rows_of(rank), quarter] = y[64 * j:64 * j + 64]
        for k, step in enumerate(steps):
            pl.when(i == k)(step)
        return 0

    lax.fori_loop(0, 4, two_ranks, 0)
    mine, single = finish_sums()
    mine = f32(hidden[0:64, :]) + mine
    single = f32(hidden[64:65, :]) + single
    res[0:64, :] = mine
    res[64:65, :] = single
    gains = wide_row(gain_m)
    xall[rows_of(p.t), :] = scaled(mine, gains)
    ext[p.t] = f32(scaled(single, gains))
    rows = gather_rows_steps(links, p, xall, ext)
    next(rows)
    for b in range(8):
        joint[65 * b:65 * b + 64, :] = main[64 * b:64 * b + 64, :]
        joint[65 * b + 64:65 * b + 65, :] = tail[8 + b:9 + b, :]
    att_out[...] = joint[...].astype(jnp.bfloat16)
    for _ in rows:
        pass
    place_singles(ext, xall)
    loads[6].wait()
    loads[7].wait()
    for lo, n in ((0, 256), (256, 256), (512, 192)):
        g = lax.dot_general(xall[...], wg[lo:lo + n, :], NT, preferred_element_type=jnp.float32)
        u = lax.dot_general(xall[...], wu[lo:lo + n, :], NT, preferred_element_type=jnp.float32)
        hid[:, lo:lo + n] = (g / (1.0 + jnp.exp(-g)) * u).astype(jnp.bfloat16)
    loads[8].wait()

    def produce(q):
        y = jnp.dot(hid[...], wd[:, QUARTERS[q]], preferred_element_type=jnp.float32)
        part2[:, QUARTERS[q]] = y[:512].astype(jnp.bfloat16)
        for e in range(8):
            pe2[e, :, QUARTERS[q]] = y[512 + e:513 + e]

    mine, single = scatter_sums(links, p, produce, part2, pe2, bufs2)
    out[0:64, :] = (res[0:64, :] + mine).astype(jnp.bfloat16)
    out[64:65, :] = (res[64:65, :] + single).astype(jnp.bfloat16)
    links.drain()


def per_device(hidden_in, norm_attn, w_query, w_key, w_value, w_out, norm_mlp, w_gate, w_up, w_down,
               cache_keys, cache_values, leaf_parent, leaf_owner, leaf_length, prompt_leaf, decode_leaf):
    freq = 10000.0 ** (-((np.arange(128) % 32).astype(np.float32) * np.float32(2.0) / np.float32(64)))
    freq = jnp.asarray(freq.astype(np.float32)[None, :])
    vm = pl.BlockSpec(memory_space=pltpu.VMEM)
    sm = pl.BlockSpec(memory_space=pltpu.SMEM)
    hbm = pl.BlockSpec(memory_space=pltpu.HBM)
    bf, fl = jnp.bfloat16, jnp.float32
    def buf(*shape, kind=bf):
        return pltpu.VMEM(shape, kind)
    scratch = [buf(16384, 128), buf(528, 2048), buf(8, 1, 2048, kind=fl), buf(2048, 512), buf(1024, 128), buf(1024, 128),
               buf(528, 128, kind=fl), buf(528, 128, kind=fl), buf(4, 512, 128), buf(4, 16, 128), buf(640, 128),
               buf(512, 256, kind=fl), buf(16, 256, kind=fl), buf(520, 256, kind=fl), buf(2176, 128)]
    scratch += [buf(256, 2048), buf(704, 2048), buf(704, 2048), buf(704, 2048), buf(512, 2048), buf(8, 1, 2048, kind=fl),
                buf(528, 2048), buf(8, 1, 2048, kind=fl), buf(528, 704), buf(65, 2048, kind=fl), buf(512, 2048), buf(8, 1, 2048, kind=fl)]
    scratch += sum_bufs() + sum_bufs()
    scratch += [pltpu.SemaphoreType.DMA((128,)), pltpu.SemaphoreType.DMA((128,)), pltpu.SemaphoreType.DMA((9,))]
    return pl.pallas_call(
        layer_kernel,
        out_shape=(jax.ShapeDtypeStruct((65, 2048), bf), jax.ShapeDtypeStruct((520, 256), bf)),
        in_specs=[vm] * 4 + [sm] * 5 + [hbm] * 9,
        out_specs=(vm, vm),
        scratch_shapes=scratch,
        compiler_params=pltpu.CompilerParams(vmem_limit_bytes=60 << 20, collective_id=1, has_side_effects=True),
        cost_estimate=pl.CostEstimate(flops=10**10, bytes_accessed=14 * 10**6, transcendentals=15 * 10**6),
        name="layer",
    )(hidden_in, norm_attn.reshape(16, 128), norm_mlp.reshape(16, 128), freq, leaf_parent, leaf_owner, leaf_length, prompt_leaf,
      decode_leaf, w_query, w_key, w_value, cache_keys, cache_values, w_out, w_gate.T, w_up.T, w_down)


def solution(mesh):
    in_specs = (P(("kv", "tp"), None), P(), P(None, "tp"), P(), P(), P("tp", None), P(), P(None, "tp"), P(None, "tp"),
                P("tp", None), P("kv", None), P("kv", None), P(), P(), P(), P(), P())
    out_specs = (P(("kv", "tp"), None), P("kv", "tp"))
    return jax.shard_map(per_device, mesh=mesh, in_specs=in_specs, out_specs=out_specs, check_vma=False)
```

```python
import jax
import jax.numpy as jnp
import numpy as np
from jax import lax
from jax.experimental import pallas as pl
from jax.experimental.pallas import tpu as pltpu
from jax.sharding import PartitionSpec as P

NEG = -1e30
NT = (((1,), (1,)), ((), ()))

def flash_many(st, qb, items):
    ss=lax.dot_general(qb, items[0][0], NT, preferred_element_type=jnp.float32)
    for i,(kvb,mask) in enumerate(items):
        nx = lax.dot_general(qb, items[i+1][0], NT, preferred_element_type=jnp.float32) if i+1<len(items) else None
        st = flash_step(st, qb, kvb, mask, ss)
        ss = nx
    return st

def flash_step(state, qb, kvb, mask, s=None):
    m, acc = state
    if s is None:
        s = lax.dot_general(qb, kvb, NT, preferred_element_type=jnp.float32)
    if mask is not None:
        s = jnp.where(mask, s, NEG)
    m_new = jnp.maximum(m, jnp.max(s, axis=1, keepdims=True))
    p = jnp.exp(s - m_new).astype(jnp.bfloat16)
    lane = lax.broadcasted_iota(jnp.int32, kvb.shape, 1)
    vaug = jnp.where(lane < 64, jnp.ones_like(kvb), kvb)
    acc = acc * jnp.exp(m - m_new) + jnp.dot(p, vaug, preferred_element_type=jnp.float32)
    return m_new, acc

def finish(state, rows):
    m, acc = state
    ratio = pltpu.roll(acc, 64, 1) / acc
    h = [ratio[i * rows:(i + 1) * rows] for i in range(4)]
    lane = lax.broadcasted_iota(jnp.int32, (rows, 128), 1)
    a = jnp.where(lane < 64, h[0], pltpu.roll(h[1], 64, 1))
    b = jnp.where(lane < 64, h[2], pltpu.roll(h[3], 64, 1))
    return jnp.concatenate([a, b], axis=1)

def token_of(idx):
    return jnp.where(idx < 512, 65 * (idx // 64) + idx % 64,
                     jnp.where(idx < 520, 65 * (idx - 512) + 64, 1 << 20))

MESH = pl.DeviceIdType.MESH
QUARTERS = tuple(pl.ds(512 * i, 512) for i in range(4))


class Transfer:
    def __init__(self, links, k, src, dst, where):
        self.parts = links, k, src, dst, where

    def copy(self):
        links, k, src, dst, where = self.parts
        return pltpu.make_async_remote_copy(src_ref=src(), dst_ref=dst(), send_sem=links.send_sem.at[k], recv_sem=links.recv_sem.at[k],
                                            device_id=where, device_id_type=MESH)

    def start(self):
        self.copy().start()
        return self

    def wait_recv(self):
        self.copy().wait_recv()

    def wait_send(self):
        self.copy().wait_send()


class Links:
    def __init__(self, send_sem, recv_sem):
        self.send_sem, self.recv_sem, self.open = send_sem, recv_sem, []

    def plan(self, src, dst, where):
        self.open.append(Transfer(self, len(self.open), src, dst, where))
        return self.open[-1]

    def send(self, src, dst, where):
        return self.plan(lambda: src, lambda: dst, where).start()

    def drain(self):
        for transfer in self.open:
            transfer.wait_send()


class Place:
    def __init__(self):
        self.t = lax.axis_index("tp")
        self.z, self.x = lax.div(self.t, 4), lax.rem(self.t, 4)
        self.xr, self.xl, self.opp = lax.rem(self.x + 1, 4), lax.rem(self.x + 3, 4), lax.rem(self.x + 2, 4)
        self.oz = 1 - self.z
        self.right = {"tp": self.z * 4 + self.xr}
        self.left = {"tp": self.z * 4 + self.xl}
        self.mate = {"tp": self.oz * 4 + self.x}

    def peer(self, k):
        return lax.rem(self.t + k, 8)


def rows_of(rank):
    return pl.ds(pl.multiple_of(rank * 64, 64), 64)


def cuts(cut):
    a, b = cut // 2, (2048 - cut) // 2
    return ((pl.ds(0, cut), pl.ds(0, a), pl.ds(a, a)), (pl.ds(cut, 2 * b), pl.ds(cut, b), pl.ds(cut + b, b)))


def gather_rows_steps(links, p, xall, ext, cut, over):
    (A, A0, A1), (B, B0, B1) = cuts(cut)
    def blk(z, x, cols, lo=0, n=64):
        return xall.at[pl.ds(pl.multiple_of((z * 4 + x) * 64 + lo, n), n), cols]
    def go(z, x, cols, where):
        return [links.send(blk(z, x, cols), blk(z, x, cols), where)]
    def cross(z, x, cols):
        return [links.send(blk(z, x, cols, lo, n), blk(z, x, cols, lo, n), where) for lo, n, where in over]
    def wait(copies):
        for copy in copies:
            copy.wait_recv()
    az = cross(p.z, p.x, A)
    br, bl = go(p.z, p.x, B, p.right), go(p.z, p.x, B, p.left)
    ar, al = go(p.z, p.x, A, p.right), go(p.z, p.x, A, p.left)
    rest = cross(p.z, p.x, B)
    rest += [links.send(ext.at[p.t], ext.at[p.t], {"tp": p.peer(k)}) for k in range(1, 8)]
    yield 1
    wait(br)
    b0 = go(p.z, p.xl, B0, p.right)
    rest += cross(p.z, p.xl, B)
    yield 1
    wait(bl)
    b1 = go(p.z, p.xr, B1, p.left)
    rest += cross(p.z, p.xr, B)
    yield 1
    wait(az)
    far_r, far_l = go(p.oz, p.x, A, p.right), go(p.oz, p.x, A, p.left)
    yield 1
    wait(ar)
    near = go(p.z, p.xl, A0, p.right)
    yield 1
    wait(al)
    near += go(p.z, p.xr, A1, p.left)
    yield 1
    wait(b0)
    rest += cross(p.z, p.opp, B0)
    wait(b1)
    rest += cross(p.z, p.opp, B1)
    yield 1
    wait(far_r)
    rest += go(p.oz, p.xl, A0, p.right)
    yield 1
    wait(far_l)
    rest += go(p.oz, p.xr, A1, p.left)
    yield 1
    wait(near)
    yield 1
    wait(rest)


def f32(x):
    return x.astype(jnp.float32)


def scatter_sums(links, p, produce, part, pe, bufs, cut, over):
    near, wide, zb, bq, bw, za, eb = bufs
    (A, A0, A1), (B, B0, B1) = cuts(cut)
    planes = (p.oz, p.z)
    def blk(z, x, cols, lo=0, n=64):
        return part.at[pl.ds(pl.multiple_of((z * 4 + x) * 64 + lo, n), n), cols]
    def cross(z, x, cols, dst):
        return [links.send(blk(z, x, cols, lo, n), dst.at[lo:lo + n, :], where) for lo, n, where in over]
    def wait(copies):
        for copy in copies:
            copy.wait_recv()
    def add(z, x, cols, more):
        at = blk(z, x, cols)
        at[...] = (f32(at[...]) + f32(more)).astype(jnp.bfloat16)
    split = cut // 512
    for q in range(split, 4):
        produce(q)
    order = (p.opp, p.xr, p.xl, p.x)
    bz = [cross(p.oz, xd, B, zb.at[i]) for i, xd in enumerate(order)]
    for q in range(split):
        produce(q)
    ar = [links.send(blk(z, p.opp, A0), near.at[0, i], p.right) for i, z in enumerate(planes)]
    al = [links.send(blk(z, p.opp, A1), near.at[1, i], p.left) for i, z in enumerate(planes)]
    singles = [links.send(pe.at[p.peer(k)], eb.at[k], {"tp": p.peer(k)}) for k in range(1, 8)]
    wait(bz[0])
    add(p.z, p.opp, B, zb[0])
    b_r = links.send(blk(p.z, p.opp, B0), bq.at[0], p.right)
    b_l = links.send(blk(p.z, p.opp, B1), bq.at[1], p.left)
    wr, wl = [], []
    for i, z in enumerate(planes):
        ar[i].wait_recv()
        add(z, p.xr, A0, near[0, i])
        wr.append(links.send(blk(z, p.xr, A), wide.at[0, i], p.right))
        al[i].wait_recv()
        add(z, p.xl, A1, near[1, i])
        wl.append(links.send(blk(z, p.xl, A), wide.at[1, i], p.left))
    wait(bz[1])
    add(p.z, p.xr, B, zb[1])
    b_r.wait_recv()
    add(p.z, p.xr, B0, bq[0])
    b_rw = links.send(blk(p.z, p.xr, B), bw.at[0], p.right)
    wait(bz[2])
    add(p.z, p.xl, B, zb[2])
    b_l.wait_recv()
    add(p.z, p.xl, B1, bq[1])
    b_lw = links.send(blk(p.z, p.xl, B), bw.at[1], p.left)
    wr[0].wait_recv()
    wl[0].wait_recv()
    add(p.oz, p.x, A, f32(wide[0, 0]) + f32(wide[1, 0]))
    a_z = cross(p.oz, p.x, A, za)
    wait([wr[1], wl[1]] + bz[3] + [b_rw, b_lw])
    mine_a = f32(blk(p.z, p.x, A)[...]) + f32(wide[0, 1]) + f32(wide[1, 1])
    mine_b = f32(blk(p.z, p.x, B)[...]) + f32(zb[3]) + f32(bw[0]) + f32(bw[1])
    wait(singles)
    single = pe[p.t]
    for k in range(1, 8):
        single = single + eb[k]
    wait(a_z)
    return jnp.concatenate([mine_a + f32(za[...]), mine_b], axis=1), single


def sum_bufs(cut):
    bf, a, b = jnp.bfloat16, cut, 2048 - cut
    return [pltpu.VMEM((2, 2, 64, a // 2), bf), pltpu.VMEM((2, 2, 64, a), bf), pltpu.VMEM((4, 64, b), bf),
            pltpu.VMEM((2, 64, b // 2), bf), pltpu.VMEM((2, 64, b), bf), pltpu.VMEM((64, a), bf),
            pltpu.VMEM((8, 1, 2048), jnp.float32)]


def wide_row(gain):
    rows = gain[...].astype(jnp.float32)
    return jnp.concatenate([rows[i:i + 1] for i in range(16)], axis=1)


def scaled(values, gain):
    mean_square = jnp.mean(values * values, axis=-1, keepdims=True)
    return (values * lax.rsqrt(mean_square + 1e-05) * gain).astype(jnp.bfloat16)


def place_singles(ext, xall):
    rows = [ext[e] for e in range(8)]
    xall[512:528, :] = jnp.concatenate(rows + [jnp.zeros((8, 2048), jnp.float32)], axis=0).astype(jnp.bfloat16)


class Ring:
    def __init__(self):
        self.o = lax.axis_index("kv")
        self.y, rest = lax.div(self.o, 4), lax.rem(self.o, 4)
        self.h, self.c = lax.div(rest, 2), lax.rem(rest, 2)
        self.yr, self.yl, self.opp = lax.rem(self.y + 1, 4), lax.rem(self.y + 3, 4), lax.rem(self.y + 2, 4)
        self.oh = 1 - self.h
        self.right, self.left = {"kv": self.at(self.yr, self.h)}, {"kv": self.at(self.yl, self.h)}
        self.mate, self.twin = {"kv": self.at(self.y, self.oh)}, {"kv": self.o + 1 - 2 * self.c}

    def at(self, y, h):
        return y * 4 + h * 2 + self.c


def gather_cache(links, r, kv, far_slab, far):
    top, low, whole = (0, 512), (512, 512), (0, 1024)
    twins = []
    def go(y, h, rows, where):
        at = kv.at[pl.ds(pl.multiple_of(r.at(y, h) * 1024 + rows[0], 512), rows[1]), :]
        return links.send(at, at, where)
    def share(y, h, rows):
        twins.append(go(y, h, rows, r.twin))
    m = links.send(far_slab, kv.at[pl.ds(pl.multiple_of(r.o * 1024, 1024), 1024), :], far)
    a = go(r.y, r.h, whole, r.right), go(r.y, r.h, whole, r.left)
    share(r.y, r.h, whole)
    yield 1
    m.wait_recv()
    b = go(r.y, r.oh, whole, r.right), go(r.y, r.oh, whole, r.left)
    share(r.y, r.oh, whole)
    yield 1
    ends = []
    for (from_left, from_right), h in ((a, r.h), (b, r.oh)):
        from_left.wait_recv()
        ends.append((go(r.yl, h, top, r.right), h, top))
        share(r.yl, h, whole)
        yield 1
        from_right.wait_recv()
        ends.append((go(r.yr, h, low, r.left), h, low))
        share(r.yr, h, whole)
        yield 1
    for copy, h, rows in ends:
        copy.wait_recv()
        share(r.opp, h, rows)
        yield 1
    for copy in twins:
        copy.wait_recv()


CUT = 512


def early_sums(links, p, part, pe, bufs):
    near, wide, zb, bq, bw, za, eb = bufs
    (A, A0, A1), (B, B0, B1) = cuts(1024)
    planes = (p.oz, p.z)
    order = (p.opp, p.xr, p.xl, p.x)
    def blk(z, x, cols):
        return part.at[rows_of(z * 4 + x), cols]
    def add(z, x, cols, more):
        at = blk(z, x, cols)
        at[...] = (f32(at[...]) + f32(more)).astype(jnp.bfloat16)
    def plan(z, x, cols, dst, where):
        return links.plan(lambda: blk(z, x, cols), dst, where)
    bz = [plan(p.oz, xd, B, lambda i=i: zb.at[i], p.mate) for i, xd in enumerate(order)]
    ar = [plan(z, p.opp, A0, lambda i=i: near.at[0, i], p.right) for i, z in enumerate(planes)]
    al = [plan(z, p.opp, A1, lambda i=i: near.at[1, i], p.left) for i, z in enumerate(planes)]
    wr = [plan(z, p.xr, A, lambda i=i: wide.at[0, i], p.right) for i, z in enumerate(planes)]
    wl = [plan(z, p.xl, A, lambda i=i: wide.at[1, i], p.left) for i, z in enumerate(planes)]
    b_r, b_l = plan(p.z, p.opp, B0, lambda: bq.at[0], p.right), plan(p.z, p.opp, B1, lambda: bq.at[1], p.left)
    b_rw, b_lw = plan(p.z, p.xr, B, lambda: bw.at[0], p.right), plan(p.z, p.xl, B, lambda: bw.at[1], p.left)
    a_z = plan(p.oz, p.x, A, lambda: za, p.mate)
    singles = [links.plan(lambda k=k: pe.at[p.peer(k)], lambda k=k: eb.at[k], {"tp": p.peer(k)}) for k in range(1, 8)]

    def step0():
        for copy in [bz[0]] + ar + al + singles:
            copy.start()

    def step1():
        bz[1].start()
        bz[0].wait_recv()
        add(p.z, p.opp, B, zb[0])
        b_r.start()
        b_l.start()
        for i, z in enumerate(planes):
            ar[i].wait_recv()
            add(z, p.xr, A0, near[0, i])
            wr[i].start()

    def step2():
        bz[2].start()
        for i, z in enumerate(planes):
            al[i].wait_recv()
            add(z, p.xl, A1, near[1, i])
            wl[i].start()
        bz[1].wait_recv()
        add(p.z, p.xr, B, zb[1])
        b_r.wait_recv()
        add(p.z, p.xr, B0, bq[0])
        b_rw.start()

    def step3():
        bz[3].start()
        bz[2].wait_recv()
        add(p.z, p.xl, B, zb[2])
        b_l.wait_recv()
        add(p.z, p.xl, B1, bq[1])
        b_lw.start()
        wr[0].wait_recv()
        wl[0].wait_recv()
        add(p.oz, p.x, A, f32(wide[0, 0]) + f32(wide[1, 0]))
        a_z.start()

    def finish_sums():
        wr[1].wait_recv()
        wl[1].wait_recv()
        mine_a = f32(blk(p.z, p.x, A)[...]) + f32(wide[0, 1]) + f32(wide[1, 1])
        for copy in singles:
            copy.wait_recv()
        single = pe[p.t]
        for k in range(1, 8):
            single = single + eb[k]
        for copy in (b_rw, bz[3], a_z, b_lw):
            copy.wait_recv()
        mine_b = f32(blk(p.z, p.x, B)[...]) + f32(zb[3]) + f32(bw[0]) + f32(bw[1])
        return jnp.concatenate([mine_a + f32(za[...]), mine_b], axis=1), single

    return (step0, step1, step2, step3), finish_sums


def layer_kernel(hidden, gain_a, gain_m, freq, leaf_parent, leaf_owner, leaf_length, prompt_leaf, decode_leaf,
                 wq_h, wk_h, wv_h, ck_h, cv_h, wo_h, wg_h, wu_h, wd_h, out, att_out, *s):
    (kv, xin, ein, w, ck, cv, cos, sin, qs, qt, own, main, tail, joint, near_kv, ck2, cv2, far_slab), s = s[:18], s[18:]
    (wo, wg, wu, wd, part, pe, xall, ext, hid, res, part2, pe2), s = s[:12], s[12:]
    bufs1, bufs2, (send_sem, recv_sem, wsem) = s[:7], s[7:14], s[14:]
    p, r = Place(), Ring()
    links = Links(send_sem, recv_sem)
    head = lax.div(p.t, 2)
    odd = lax.rem(head, 2)
    pair = pl.ds(pl.multiple_of(lax.div(head, 2) * 128, 128), 128)
    pair2 = pl.ds(pl.multiple_of(p.oz * 128, 128), 128)
    far = {"kv": r.at(r.y, r.oh), "tp": p.oz * 4 + p.x}
    moves = ((ck_h.at[:, pair], ck), (cv_h.at[:, pair], cv), (wq_h, w.at[:, 0:256]), (wk_h.at[:, pair], w.at[:, 256:384]),
             (wv_h.at[:, pair], w.at[:, 384:512]), (wo_h, wo), (wg_h, wg), (wu_h, wu), (wd_h, wd),
             (ck_h.at[:, pair2], ck2), (cv_h.at[:, pair2], cv2))
    loads = [pltpu.make_async_copy(a, b, wsem.at[i]) for i, (a, b) in enumerate(moves)]
    for load in loads:
        load.start()
    barrier = pltpu.get_barrier_semaphore()
    for where in [{"tp": p.peer(k)} for k in range(1, 8)] + [r.right, r.left, far, r.twin]:
        pl.semaphore_signal(barrier, inc=1, device_id=where, device_id_type=MESH)
    gains = wide_row(gain_a)
    xin[rows_of(p.t), :] = scaled(f32(hidden[0:64, :]), gains)
    ein[p.t] = f32(scaled(f32(hidden[64:65, :]), gains))
    loads[0].wait()
    loads[1].wait()
    lane = lax.broadcasted_iota(jnp.int32, (1, 128), 1)

    def joined(keys, values):
        k = jnp.where(odd == 1, pltpu.roll(keys, 64, 1), keys)
        v = jnp.where(odd == 1, values, pltpu.roll(values, 64, 1))
        return jnp.where(lane < 64, k, v)

    kv[pl.ds(pl.multiple_of(r.o * 1024, 1024), 1024), :] = joined(f32(ck[...]), f32(cv[...])).astype(jnp.bfloat16)
    loads[9].wait()
    loads[10].wait()
    far_slab[...] = joined(f32(ck2[...]), f32(cv2[...])).astype(jnp.bfloat16)
    pl.semaphore_wait(barrier, 11)

    rows = gather_rows_steps(links, p, xin, ein, 1024, ((0, 64, p.mate),))
    cache = gather_cache(links, r, kv, far_slab, far)
    next(rows)
    next(cache)
    me = r.o
    my_leaf = prompt_leaf[me]
    my_owner = leaf_owner[my_leaf]
    my_length = leaf_length[my_leaf]
    my_branch = leaf_parent[my_leaf]
    token = token_of(lax.broadcasted_iota(jnp.int32, (528, 1), 0))
    spot = my_length + token
    for i in range(8):
        spot = jnp.where(token == 512 + i, leaf_length[decode_leaf[me * 8 + i]], spot)
    angle = (spot + 5120).astype(jnp.float32) * freq[...]
    cos[...] = jnp.cos(angle)
    sin[...] = jnp.sin(angle)
    branch_of, length_of, place_of, count = [], [], [], jnp.int32(0)
    for o in range(16):
        branch, length = jnp.int32(0), jnp.int32(0)
        for leaf in range(16):
            held = leaf_owner[leaf] == o
            branch = jnp.where(held, leaf_parent[leaf], branch)
            length = jnp.where(held, leaf_length[leaf], length)
        branch_of.append(branch)
        length_of.append(length)
        place_of.append(jnp.where(branch == my_branch, count, 4))
        count = count + jnp.where(branch == my_branch, 1, 0)
    for turn in "rrrcccrrrrrccrr":
        next(rows if turn == "r" else cache, None)
    place_singles(ein, xin)
    for load in loads[2:5]:
        load.wait()

    def rotated(x):
        turned = jnp.where(lane % 64 < 32, -pltpu.roll(x, 96, 1), pltpu.roll(x, 32, 1))
        return x * cos[...] + turned * sin[...]

    y = jnp.dot(xin[...], w[...], preferred_element_type=jnp.float32)
    zero = jnp.zeros((528, 128), jnp.float32)
    for i in range(2):
        q = f32(rotated(y[:, 128 * i:128 * i + 128]).astype(jnp.bfloat16)) * 0.125
        for j, x in enumerate((q, pltpu.roll(q, 64, 1))):
            x = jnp.where(lane < 64, x, zero)
            qs[2 * i + j] = x[:512].astype(jnp.bfloat16)
            qt[2 * i + j] = x[504:520].astype(jnp.bfloat16)
    own[0:528, :] = joined(rotated(y[:, 256:384]), y[:, 384:512]).astype(jnp.bfloat16)
    own[528:640, :] = jnp.zeros((112, 128), jnp.bfloat16)
    for _ in cache:
        pass

    for i in range(4):
        got = kv[256:512, :]
        for o in range(1, 16):
            got = jnp.where(place_of[o] == i, kv[o * 1024 + 256:o * 1024 + 512, :], got)
        near_kv[256 * i:256 * i + 256, :] = got
    got = kv[512:1024, :]
    for o in range(1, 16):
        got = jnp.where(my_owner == o, kv[o * 1024 + 512:o * 1024 + 1024, :], got)
    near_kv[1024:1536, :] = got
    near_kv[1536:2176, :] = own[...]

    def start(n):
        return jnp.full((n, 1), NEG, jnp.float32), jnp.zeros((n, 128), jnp.float32)

    qb = jnp.concatenate([qt[h] for h in range(4)], axis=0)
    row = lax.broadcasted_iota(jnp.int32, (64, 1), 0) % 16
    r_tok = jnp.where(row < 8, 511 + row, 65 * (row - 8) + 64)
    r_owner = jnp.full((64, 1), my_owner, jnp.int32)
    r_branch = jnp.full((64, 1), my_branch, jnp.int32)
    for i in range(8):
        leaf = decode_leaf[me * 8 + i]
        r_owner = jnp.where(r_tok == 512 + i, leaf_owner[leaf], r_owner)
        r_branch = jnp.where(r_tok == 512 + i, leaf_parent[leaf], r_branch)
    items = []
    col = lax.broadcasted_iota(jnp.int32, (1, 1024), 1)
    for o in range(16):
        see_branch = jnp.where(r_branch == branch_of[o], 512, 256)
        see_leaf = jnp.where(r_owner == o, 512 + length_of[o], 512)
        items.append((kv[o * 1024:o * 1024 + 1024, :], (col < see_branch) | ((col >= 512) & (col < see_leaf))))
    ktok = token_of(lax.broadcasted_iota(jnp.int32, (1, 640), 1))
    items.append((own[...], (ktok == r_tok) | ((ktok <= r_tok) & (r_tok < 512))))
    tail[...] = finish(flash_many(start(64), qb, items), 16)
    loads[5].wait()
    singles = jnp.concatenate([tail[8:16, :], jnp.zeros((8, 256), jnp.float32)], axis=0).astype(jnp.bfloat16)
    y = jnp.dot(singles, wo[...], preferred_element_type=jnp.float32)
    for e in range(8):
        pe[e] = y[e:e + 1]

    steps, finish_sums = early_sums(links, p, part, pe, bufs1)

    def two_ranks(i, _):
        xd = (p.x + 2 + 3 * i + 3 * (i // 2) + 2 * (i // 3)) % 4
        ranks = (p.oz * 4 + xd, p.z * 4 + xd)
        qb = jnp.concatenate([qs[h, rows_of(rank), :] for h in range(4) for rank in ranks], axis=0)
        items = [(jnp.concatenate([kv[g * 4096 + i * 1024:g * 4096 + i * 1024 + 256, :] for i in range(4)], axis=0), None) for g in range(4)]
        items.append((near_kv[0:1024, :], None))
        col = lax.broadcasted_iota(jnp.int32, (1, 1152), 1)
        at = lax.broadcasted_iota(jnp.int32, (512, 1), 0) % 128
        rtok = jnp.where(at < 64, 65 * ranks[0] + at, 65 * ranks[1] + at - 64)
        ktok = jnp.where(col < 512, jnp.where(col < my_length, -1, 1 << 20), token_of(col - 512))
        items.append((near_kv[1024:2176, :], ktok <= rtok))
        got = finish(flash_many(start(512), qb, items), 128)
        for j, rank in enumerate(ranks):
            main[rows_of(rank), :] = got[64 * j:64 * j + 64]
        main[504:512, :] = tail[0:8, :]
        lhs = jnp.concatenate([main[rows_of(rank), :] for rank in ranks], axis=0).astype(jnp.bfloat16)
        for quarter in QUARTERS:
            y = jnp.dot(lhs, wo[:, quarter], preferred_element_type=jnp.float32).astype(jnp.bfloat16)
            for j, rank in enumerate(ranks):
                part[rows_of(rank), quarter] = y[64 * j:64 * j + 64]
        for k, step in enumerate(steps):
            pl.when(i == k)(step)
        return 0

    lax.fori_loop(0, 4, two_ranks, 0)
    mine, single = finish_sums()
    mine = f32(hidden[0:64, :]) + mine
    single = f32(hidden[64:65, :]) + single
    res[0:64, :] = mine
    res[64:65, :] = single
    gains = wide_row(gain_m)
    over = ((0, 32, p.mate), (32, 32, far))
    xall[rows_of(p.t), :] = scaled(mine, gains)
    ext[p.t] = f32(scaled(single, gains))
    rows = gather_rows_steps(links, p, xall, ext, CUT, over)
    next(rows)
    for b in range(8):
        joint[65 * b:65 * b + 64, :] = main[64 * b:64 * b + 64, :]
        joint[65 * b + 64:65 * b + 65, :] = tail[8 + b:9 + b, :]
    att_out[...] = joint[...].astype(jnp.bfloat16)
    loads[6].wait()
    loads[7].wait()

    def units(lhs, store):
        for lo, n in ((0, 256), (256, 256), (512, 192)):
            g = lax.dot_general(lhs, wg[lo:lo + n, :], NT, preferred_element_type=jnp.float32)
            u = lax.dot_general(lhs, wu[lo:lo + n, :], NT, preferred_element_type=jnp.float32)
            store(lo, n, (g / (1.0 + jnp.exp(-g)) * u).astype(jnp.bfloat16))

    here, there = (pl.ds(pl.multiple_of(z * 256, 256), 256) for z in (p.z, p.oz))
    for _ in range(9):
        next(rows)

    def store_here(lo, n, h):
        hid[here, lo:lo + n] = h

    def store_there(lo, n, h):
        hid[there, lo:lo + n] = h[:256]
        hid[512:528, lo:lo + n] = h[256:]

    units(xall[here, :], store_here)
    for _ in rows:
        pass
    place_singles(ext, xall)
    units(jnp.concatenate([xall[there, :], xall[512:528, :]], axis=0), store_there)
    loads[8].wait()

    def produce(q):
        y = jnp.dot(hid[...], wd[:, QUARTERS[q]], preferred_element_type=jnp.float32)
        part2[:, QUARTERS[q]] = y[:512].astype(jnp.bfloat16)
        for e in range(8):
            pe2[e, :, QUARTERS[q]] = y[512 + e:513 + e]

    mine, single = scatter_sums(links, p, produce, part2, pe2, bufs2, CUT, over)
    out[0:64, :] = (res[0:64, :] + mine).astype(jnp.bfloat16)
    out[64:65, :] = (res[64:65, :] + single).astype(jnp.bfloat16)
    links.drain()


def per_device(hidden_in, norm_attn, w_query, w_key, w_value, w_out, norm_mlp, w_gate, w_up, w_down,
               cache_keys, cache_values, leaf_parent, leaf_owner, leaf_length, prompt_leaf, decode_leaf):
    freq = 10000.0 ** (-((np.arange(128) % 32).astype(np.float32) * np.float32(2.0) / np.float32(64)))
    freq = jnp.asarray(freq.astype(np.float32)[None, :])
    vm = pl.BlockSpec(memory_space=pltpu.VMEM)
    sm = pl.BlockSpec(memory_space=pltpu.SMEM)
    hbm = pl.BlockSpec(memory_space=pltpu.HBM)
    bf, fl = jnp.bfloat16, jnp.float32
    def buf(*shape, kind=bf):
        return pltpu.VMEM(shape, kind)
    scratch = [buf(16384, 128), buf(528, 2048), buf(8, 1, 2048, kind=fl), buf(2048, 512), buf(1024, 128), buf(1024, 128),
               buf(528, 128, kind=fl), buf(528, 128, kind=fl), buf(4, 512, 128), buf(4, 16, 128), buf(640, 128),
               buf(512, 256, kind=fl), buf(16, 256, kind=fl), buf(520, 256, kind=fl), buf(2176, 128),
               buf(1024, 128), buf(1024, 128), buf(1024, 128)]
    scratch += [buf(256, 2048), buf(704, 2048), buf(704, 2048), buf(704, 2048), buf(512, 2048), buf(8, 1, 2048, kind=fl),
                buf(528, 2048), buf(8, 1, 2048, kind=fl), buf(528, 704), buf(65, 2048, kind=fl), buf(512, 2048), buf(8, 1, 2048, kind=fl)]
    scratch += sum_bufs(1024) + sum_bufs(CUT)
    scratch += [pltpu.SemaphoreType.DMA((128,)), pltpu.SemaphoreType.DMA((128,)), pltpu.SemaphoreType.DMA((11,))]
    return pl.pallas_call(
        layer_kernel,
        out_shape=(jax.ShapeDtypeStruct((65, 2048), bf), jax.ShapeDtypeStruct((520, 256), bf)),
        in_specs=[vm] * 4 + [sm] * 5 + [hbm] * 9,
        out_specs=(vm, vm),
        scratch_shapes=scratch,
        compiler_params=pltpu.CompilerParams(vmem_limit_bytes=60 << 20, collective_id=1, has_side_effects=True),
        cost_estimate=pl.CostEstimate(flops=10**10, bytes_accessed=14 * 10**6, transcendentals=15 * 10**6),
        name="layer",
    )(hidden_in, norm_attn.reshape(16, 128), norm_mlp.reshape(16, 128), freq, leaf_parent, leaf_owner, leaf_length, prompt_leaf,
      decode_leaf, w_query, w_key, w_value, cache_keys, cache_values, w_out, w_gate.T, w_up.T, w_down)


def solution(mesh):
    in_specs = (P(("kv", "tp"), None), P(), P(None, "tp"), P(), P(), P("tp", None), P(), P(None, "tp"), P(None, "tp"),
                P("tp", None), P("kv", None), P("kv", None), P(), P(), P(), P(), P())
    out_specs = (P(("kv", "tp"), None), P("kv", "tp"))
    return jax.shard_map(per_device, mesh=mesh, in_specs=in_specs, out_specs=out_specs, check_vma=False)
```

```python
import jax
import jax.numpy as jnp
import numpy as np
from jax import lax
from jax.experimental import pallas as pl
from jax.experimental.pallas import tpu as pltpu
from jax.sharding import PartitionSpec as P

NEG = -1e30
NT = (((1,), (1,)), ((), ()))

def flash_many(st, qb, items):
    ss=lax.dot_general(qb, items[0][0], NT, preferred_element_type=jnp.float32)
    for i,(kvb,mask) in enumerate(items):
        nx = lax.dot_general(qb, items[i+1][0], NT, preferred_element_type=jnp.float32) if i+1<len(items) else None
        st = flash_step(st, qb, kvb, mask, ss)
        ss = nx
    return st

def flash_step(state, qb, kvb, mask, s=None):
    m, acc = state
    if s is None:
        s = lax.dot_general(qb, kvb, NT, preferred_element_type=jnp.float32)
    if mask is not None:
        s = jnp.where(mask, s, NEG)
    m_new = jnp.maximum(m, jnp.max(s, axis=1, keepdims=True))
    p = jnp.exp(s - m_new).astype(jnp.bfloat16)
    lane = lax.broadcasted_iota(jnp.int32, kvb.shape, 1)
    vaug = jnp.where(lane < 64, jnp.ones_like(kvb), kvb)
    acc = acc * jnp.exp(m - m_new) + jnp.dot(p, vaug, preferred_element_type=jnp.float32)
    return m_new, acc

def finish(state, rows):
    m, acc = state
    ratio = pltpu.roll(acc, 64, 1) / acc
    h = [ratio[i * rows:(i + 1) * rows] for i in range(4)]
    lane = lax.broadcasted_iota(jnp.int32, (rows, 128), 1)
    a = jnp.where(lane < 64, h[0], pltpu.roll(h[1], 64, 1))
    b = jnp.where(lane < 64, h[2], pltpu.roll(h[3], 64, 1))
    return jnp.concatenate([a, b], axis=1)

def token_of(idx):
    return jnp.where(idx < 512, 65 * (idx // 64) + idx % 64,
                     jnp.where(idx < 520, 65 * (idx - 512) + 64, 1 << 20))

MESH = pl.DeviceIdType.MESH
QUARTERS = tuple(pl.ds(512 * i, 512) for i in range(4))


class Transfer:
    def __init__(self, links, k, src, dst, where):
        self.parts = links, k, src, dst, where

    def copy(self):
        links, k, src, dst, where = self.parts
        return pltpu.make_async_remote_copy(src_ref=src(), dst_ref=dst(), send_sem=links.send_sem.at[k], recv_sem=links.recv_sem.at[k],
                                            device_id=where, device_id_type=MESH)

    def start(self):
        self.copy().start()
        return self

    def wait_recv(self):
        self.copy().wait_recv()

    def wait_send(self):
        self.copy().wait_send()


class Links:
    def __init__(self, send_sem, recv_sem):
        self.send_sem, self.recv_sem, self.open = send_sem, recv_sem, []

    def plan(self, src, dst, where):
        self.open.append(Transfer(self, len(self.open), src, dst, where))
        return self.open[-1]

    def send(self, src, dst, where):
        return self.plan(lambda: src, lambda: dst, where).start()

    def drain(self):
        for transfer in self.open:
            transfer.wait_send()


class Place:
    def __init__(self):
        self.t = lax.axis_index("tp")
        self.z, self.x = lax.div(self.t, 4), lax.rem(self.t, 4)
        self.xr, self.xl, self.opp = lax.rem(self.x + 1, 4), lax.rem(self.x + 3, 4), lax.rem(self.x + 2, 4)
        self.oz = 1 - self.z
        self.right = {"tp": self.z * 4 + self.xr}
        self.left = {"tp": self.z * 4 + self.xl}
        self.mate = {"tp": self.oz * 4 + self.x}

    def peer(self, k):
        return lax.rem(self.t + k, 8)


def rows_of(rank):
    return pl.ds(pl.multiple_of(rank * 64, 64), 64)


def cuts(cut):
    a, b = cut // 2, (2048 - cut) // 2
    return ((pl.ds(0, cut), pl.ds(0, a), pl.ds(a, a)), (pl.ds(cut, 2 * b), pl.ds(cut, b), pl.ds(cut + b, b)))


def gather_rows_steps(links, p, xall, ext, cut, over):
    (A, A0, A1), (B, B0, B1) = cuts(cut)
    def blk(z, x, cols, lo=0, n=64):
        return xall.at[pl.ds(pl.multiple_of((z * 4 + x) * 64 + lo, n), n), cols]
    def go(z, x, cols, where):
        return [links.send(blk(z, x, cols), blk(z, x, cols), where)]
    def cross(z, x, cols):
        return [links.send(blk(z, x, cols, lo, n), blk(z, x, cols, lo, n), where) for lo, n, where in over]
    def wait(copies):
        for copy in copies:
            copy.wait_recv()
    az = cross(p.z, p.x, A)
    br, bl = go(p.z, p.x, B, p.right), go(p.z, p.x, B, p.left)
    ar, al = go(p.z, p.x, A, p.right), go(p.z, p.x, A, p.left)
    rest = cross(p.z, p.x, B)
    rest += [links.send(ext.at[p.t], ext.at[p.t], {"tp": p.peer(k)}) for k in range(1, 8)]
    yield 1
    wait(br)
    b0 = go(p.z, p.xl, B0, p.right)
    rest += cross(p.z, p.xl, B)
    yield 1
    wait(bl)
    b1 = go(p.z, p.xr, B1, p.left)
    rest += cross(p.z, p.xr, B)
    yield 1
    wait(az)
    far_r, far_l = go(p.oz, p.x, A, p.right), go(p.oz, p.x, A, p.left)
    yield 1
    wait(ar)
    near = go(p.z, p.xl, A0, p.right)
    yield 1
    wait(al)
    near += go(p.z, p.xr, A1, p.left)
    yield 1
    wait(b0)
    rest += cross(p.z, p.opp, B0)
    wait(b1)
    rest += cross(p.z, p.opp, B1)
    yield 1
    wait(far_r)
    rest += go(p.oz, p.xl, A0, p.right)
    yield 1
    wait(far_l)
    rest += go(p.oz, p.xr, A1, p.left)
    yield 1
    wait(near)
    yield 1
    wait(rest)


def f32(x):
    return x.astype(jnp.float32)


def scatter_sums(links, p, produce, part, pe, bufs, cut, over):
    near, wide, zb, bq, bw, za, eb = bufs
    (A, A0, A1), (B, B0, B1) = cuts(cut)
    planes = (p.oz, p.z)
    def blk(z, x, cols, lo=0, n=64):
        return part.at[pl.ds(pl.multiple_of((z * 4 + x) * 64 + lo, n), n), cols]
    def cross(z, x, cols, dst):
        return [links.send(blk(z, x, cols, lo, n), dst.at[lo:lo + n, :], where) for lo, n, where in over]
    def wait(copies):
        for copy in copies:
            copy.wait_recv()
    def add(z, x, cols, more):
        at = blk(z, x, cols)
        at[...] = (f32(at[...]) + f32(more)).astype(jnp.bfloat16)
    split = cut // 512
    for q in range(split, 4):
        produce(q)
    order = (p.opp, p.xr, p.xl, p.x)
    bz = [cross(p.oz, xd, B, zb.at[i]) for i, xd in enumerate(order)]
    for q in range(split):
        produce(q)
    ar = [links.send(blk(z, p.opp, A0), near.at[0, i], p.right) for i, z in enumerate(planes)]
    al = [links.send(blk(z, p.opp, A1), near.at[1, i], p.left) for i, z in enumerate(planes)]
    singles = [links.send(pe.at[p.peer(k)], eb.at[k], {"tp": p.peer(k)}) for k in range(1, 8)]
    wait(bz[0])
    add(p.z, p.opp, B, zb[0])
    b_r = links.send(blk(p.z, p.opp, B0), bq.at[0], p.right)
    b_l = links.send(blk(p.z, p.opp, B1), bq.at[1], p.left)
    wr, wl = [], []
    for i, z in enumerate(planes):
        ar[i].wait_recv()
        add(z, p.xr, A0, near[0, i])
        wr.append(links.send(blk(z, p.xr, A), wide.at[0, i], p.right))
        al[i].wait_recv()
        add(z, p.xl, A1, near[1, i])
        wl.append(links.send(blk(z, p.xl, A), wide.at[1, i], p.left))
    wait(bz[1])
    add(p.z, p.xr, B, zb[1])
    b_r.wait_recv()
    add(p.z, p.xr, B0, bq[0])
    b_rw = links.send(blk(p.z, p.xr, B), bw.at[0], p.right)
    wait(bz[2])
    add(p.z, p.xl, B, zb[2])
    b_l.wait_recv()
    add(p.z, p.xl, B1, bq[1])
    b_lw = links.send(blk(p.z, p.xl, B), bw.at[1], p.left)
    wr[0].wait_recv()
    wl[0].wait_recv()
    add(p.oz, p.x, A, f32(wide[0, 0]) + f32(wide[1, 0]))
    a_z = cross(p.oz, p.x, A, za)
    wait([wr[1], wl[1]] + bz[3] + [b_rw, b_lw])
    mine_a = f32(blk(p.z, p.x, A)[...]) + f32(wide[0, 1]) + f32(wide[1, 1])
    mine_b = f32(blk(p.z, p.x, B)[...]) + f32(zb[3]) + f32(bw[0]) + f32(bw[1])
    wait(singles)
    single = pe[p.t]
    for k in range(1, 8):
        single = single + eb[k]
    wait(a_z)
    return jnp.concatenate([mine_a + f32(za[...]), mine_b], axis=1), single


def sum_bufs(cut):
    bf, a, b = jnp.bfloat16, cut, 2048 - cut
    return [pltpu.VMEM((2, 2, 64, a // 2), bf), pltpu.VMEM((2, 2, 64, a), bf), pltpu.VMEM((4, 64, b), bf),
            pltpu.VMEM((2, 64, b // 2), bf), pltpu.VMEM((2, 64, b), bf), pltpu.VMEM((64, a), bf),
            pltpu.VMEM((8, 1, 2048), jnp.float32)]


def wide_row(gain):
    rows = gain[...].astype(jnp.float32)
    return jnp.concatenate([rows[i:i + 1] for i in range(16)], axis=1)


def scaled(values, gain):
    mean_square = jnp.mean(values * values, axis=-1, keepdims=True)
    return (values * lax.rsqrt(mean_square + 1e-05) * gain).astype(jnp.bfloat16)


def place_singles(ext, xall):
    rows = [ext[e] for e in range(8)]
    xall[512:528, :] = jnp.concatenate(rows + [jnp.zeros((8, 2048), jnp.float32)], axis=0).astype(jnp.bfloat16)


class Ring:
    def __init__(self):
        self.o = lax.axis_index("kv")
        self.y, rest = lax.div(self.o, 4), lax.rem(self.o, 4)
        self.h, self.c = lax.div(rest, 2), lax.rem(rest, 2)
        self.yr, self.yl, self.opp = lax.rem(self.y + 1, 4), lax.rem(self.y + 3, 4), lax.rem(self.y + 2, 4)
        self.oh = 1 - self.h
        self.right, self.left = {"kv": self.at(self.yr, self.h)}, {"kv": self.at(self.yl, self.h)}
        self.mate, self.twin = {"kv": self.at(self.y, self.oh)}, {"kv": self.o + 1 - 2 * self.c}

    def at(self, y, h):
        return y * 4 + h * 2 + self.c


def gather_cache(links, r, kv, far_slab, far, lo, n):
    top, low, whole = (lo, n // 2), (lo + n // 2, n // 2), (lo, n)
    twins = []
    def go(y, h, rows, where):
        at = kv.at[pl.ds(pl.multiple_of(r.at(y, h) * 1024 + rows[0], 256), rows[1]), :]
        return links.send(at, at, where)
    def share(y, h, rows):
        twins.append(go(y, h, rows, r.twin))
    m = links.send(far_slab.at[lo:lo + n, :], kv.at[pl.ds(pl.multiple_of(r.o * 1024 + lo, 512), n), :], far)
    a = go(r.y, r.h, whole, r.right), go(r.y, r.h, whole, r.left)
    share(r.y, r.h, whole)
    yield 1
    m.wait_recv()
    b = go(r.y, r.oh, whole, r.right), go(r.y, r.oh, whole, r.left)
    share(r.y, r.oh, whole)
    yield 1
    ends = []
    for (from_left, from_right), h in ((a, r.h), (b, r.oh)):
        from_left.wait_recv()
        ends.append((go(r.yl, h, top, r.right), h, top))
        share(r.yl, h, whole)
        yield 1
        from_right.wait_recv()
        ends.append((go(r.yr, h, low, r.left), h, low))
        share(r.yr, h, whole)
        yield 1
    for copy, h, rows in ends:
        copy.wait_recv()
        share(r.opp, h, rows)
        yield 1
    for copy in twins:
        copy.wait_recv()


CUT = 512


def early_sums(links, p, part, pe, bufs):
    near, wide, zb, bq, bw, za, eb = bufs
    (A, A0, A1), (B, B0, B1) = cuts(1024)
    planes = (p.oz, p.z)
    order = (p.opp, p.xr, p.xl, p.x)
    def blk(z, x, cols):
        return part.at[rows_of(z * 4 + x), cols]
    def add(z, x, cols, more):
        at = blk(z, x, cols)
        at[...] = (f32(at[...]) + f32(more)).astype(jnp.bfloat16)
    def plan(z, x, cols, dst, where):
        return links.plan(lambda: blk(z, x, cols), dst, where)
    bz = [plan(p.oz, xd, B, lambda i=i: zb.at[i], p.mate) for i, xd in enumerate(order)]
    ar = [plan(z, p.opp, A0, lambda i=i: near.at[0, i], p.right) for i, z in enumerate(planes)]
    al = [plan(z, p.opp, A1, lambda i=i: near.at[1, i], p.left) for i, z in enumerate(planes)]
    wr = [plan(z, p.xr, A, lambda i=i: wide.at[0, i], p.right) for i, z in enumerate(planes)]
    wl = [plan(z, p.xl, A, lambda i=i: wide.at[1, i], p.left) for i, z in enumerate(planes)]
    b_r, b_l = plan(p.z, p.opp, B0, lambda: bq.at[0], p.right), plan(p.z, p.opp, B1, lambda: bq.at[1], p.left)
    b_rw, b_lw = plan(p.z, p.xr, B, lambda: bw.at[0], p.right), plan(p.z, p.xl, B, lambda: bw.at[1], p.left)
    a_z = plan(p.oz, p.x, A, lambda: za, p.mate)
    singles = [links.plan(lambda k=k: pe.at[p.peer(k)], lambda k=k: eb.at[k], {"tp": p.peer(k)}) for k in range(1, 8)]

    def step0():
        for copy in [bz[0]] + ar + al + singles:
            copy.start()

    def step1():
        bz[1].start()
        bz[0].wait_recv()
        add(p.z, p.opp, B, zb[0])
        b_r.start()
        b_l.start()
        for i, z in enumerate(planes):
            ar[i].wait_recv()
            add(z, p.xr, A0, near[0, i])
            wr[i].start()

    def step2():
        bz[2].start()
        for i, z in enumerate(planes):
            al[i].wait_recv()
            add(z, p.xl, A1, near[1, i])
            wl[i].start()
        bz[1].wait_recv()
        add(p.z, p.xr, B, zb[1])
        b_r.wait_recv()
        add(p.z, p.xr, B0, bq[0])
        b_rw.start()

    def step3():
        bz[3].start()
        bz[2].wait_recv()
        add(p.z, p.xl, B, zb[2])
        b_l.wait_recv()
        add(p.z, p.xl, B1, bq[1])
        b_lw.start()
        wr[0].wait_recv()
        wl[0].wait_recv()
        add(p.oz, p.x, A, f32(wide[0, 0]) + f32(wide[1, 0]))
        a_z.start()

    def finish_sums():
        wr[1].wait_recv()
        wl[1].wait_recv()
        mine_a = f32(blk(p.z, p.x, A)[...]) + f32(wide[0, 1]) + f32(wide[1, 1])
        for copy in singles:
            copy.wait_recv()
        single = pe[p.t]
        for k in range(1, 8):
            single = single + eb[k]
        for copy in (b_rw, bz[3], a_z, b_lw):
            copy.wait_recv()
        mine_b = f32(blk(p.z, p.x, B)[...]) + f32(zb[3]) + f32(bw[0]) + f32(bw[1])
        return jnp.concatenate([mine_a + f32(za[...]), mine_b], axis=1), single

    return (step0, step1, step2, step3), finish_sums


def layer_kernel(hidden, gain_a, gain_m, freq, leaf_parent, leaf_owner, leaf_length, prompt_leaf, decode_leaf,
                 wq_h, wk_h, wv_h, ck_h, cv_h, wo_h, wg_h, wu_h, wd_h, out, att_out, *s):
    (kv, xin, ein, w, ck, cv, cos, sin, qs, qt, own, main, tail, joint, near_kv, ck2, cv2, far_slab, qkv, tops, kept), s = s[:21], s[21:]
    (wo, wg, wu, wd, part, pe, xall, ext, hid, res, part2, pe2), s = s[:12], s[12:]
    bufs1, bufs2, (send_sem, recv_sem, wsem) = s[:7], s[7:14], s[14:]
    p, r = Place(), Ring()
    links = Links(send_sem, recv_sem)
    head = lax.div(p.t, 2)
    odd = lax.rem(head, 2)
    pair = pl.ds(pl.multiple_of(lax.div(head, 2) * 128, 128), 128)
    pair2 = pl.ds(pl.multiple_of(p.oz * 128, 128), 128)
    far = {"kv": r.at(r.y, r.oh), "tp": p.oz * 4 + p.x}
    moves = ((ck_h.at[:, pair], ck), (cv_h.at[:, pair], cv), (wq_h, w.at[:, 0:256]), (wk_h.at[:, pair], w.at[:, 256:384]),
             (wv_h.at[:, pair], w.at[:, 384:512]), (wo_h, wo), (wg_h, wg), (wu_h, wu), (wd_h, wd),
             (ck_h.at[:, pair2], ck2), (cv_h.at[:, pair2], cv2))
    loads = [pltpu.make_async_copy(a, b, wsem.at[i]) for i, (a, b) in enumerate(moves)]
    for load in loads:
        load.start()
    barrier = pltpu.get_barrier_semaphore()
    for where in [{"tp": p.peer(k)} for k in range(1, 8)] + [r.right, r.left, far, r.twin]:
        pl.semaphore_signal(barrier, inc=1, device_id=where, device_id_type=MESH)
    gains = wide_row(gain_a)
    xin[rows_of(p.t), :] = scaled(f32(hidden[0:64, :]), gains)
    ein[p.t] = f32(scaled(f32(hidden[64:65, :]), gains))
    pl.semaphore_wait(barrier, 11)
    rows = gather_rows_steps(links, p, xin, ein, 1536, ((0, 64, p.mate),))
    next(rows)
    lane = lax.broadcasted_iota(jnp.int32, (1, 128), 1)

    def joined(keys, values):
        k = jnp.where(odd == 1, pltpu.roll(keys, 64, 1), keys)
        v = jnp.where(odd == 1, values, pltpu.roll(values, 64, 1))
        return jnp.where(lane < 64, k, v)

    loads[9].wait()
    loads[10].wait()
    far_slab[...] = joined(f32(ck2[...]), f32(cv2[...])).astype(jnp.bfloat16)
    loads[0].wait()
    loads[1].wait()
    kv[pl.ds(pl.multiple_of(r.o * 1024, 1024), 1024), :] = joined(f32(ck[...]), f32(cv[...])).astype(jnp.bfloat16)
    early, late = (gather_cache(links, r, kv, far_slab, far, lo, 512) for lo in (0, 512))
    next(early)
    me = r.o
    my_leaf = prompt_leaf[me]
    my_owner = leaf_owner[my_leaf]
    my_length = leaf_length[my_leaf]
    my_branch = leaf_parent[my_leaf]
    ramp = lax.broadcasted_iota(jnp.int32, (64, 1), 0)
    step_angle = ramp.astype(jnp.float32) * freq[...]
    rank_angle = (65 * ramp[:8] + (5120 + my_length)).astype(jnp.float32) * freq[...]
    spot = jnp.where(ramp[:16] < 8, my_length + 511, my_length + 64 + 65 * (ramp[:16] - 8))
    for i in range(8):
        spot = jnp.where(ramp[:16] == (i + 1 if i < 7 else 15), leaf_length[decode_leaf[me * 8 + i]], spot)
    spot_angle = (spot + 5120).astype(jnp.float32) * freq[...]
    c1, s1, c8, s8 = jnp.cos(step_angle), jnp.sin(step_angle), jnp.cos(rank_angle), jnp.sin(rank_angle)
    for b in range(8):
        cos[64 * b:64 * b + 64, :] = c8[b:b + 1] * c1 - s8[b:b + 1] * s1
        sin[64 * b:64 * b + 64, :] = s8[b:b + 1] * c1 + c8[b:b + 1] * s1
    cos[504:520, :] = jnp.cos(spot_angle)
    sin[504:520, :] = jnp.sin(spot_angle)
    cos[520:528, :] = jnp.zeros((8, 128), jnp.float32)
    sin[520:528, :] = jnp.zeros((8, 128), jnp.float32)
    branch_of, length_of, place_of, count = [], [], [], jnp.int32(0)
    for o in range(16):
        branch, length = jnp.int32(0), jnp.int32(0)
        for leaf in range(16):
            held = leaf_owner[leaf] == o
            branch = jnp.where(held, leaf_parent[leaf], branch)
            length = jnp.where(held, leaf_length[leaf], length)
        branch_of.append(branch)
        length_of.append(length)
        place_of.append(jnp.where(branch == my_branch, count, 4))
        count = count + jnp.where(branch == my_branch, 1, 0)
    chains = {"r": rows, "e": early, "l": late}
    for turn in "rrreleerreereeeerrlllr":
        next(chains[turn], None)
    for load in loads[2:5]:
        load.wait()
    here, there = (pl.ds(pl.multiple_of(z * 256, 256), 256) for z in (p.z, p.oz))
    qkv[here, :] = jnp.dot(xin[here, :], w[...], preferred_element_type=jnp.float32)
    for _ in rows:
        pass
    place_singles(ein, xin)
    y = jnp.dot(jnp.concatenate([xin[there, :], xin[512:528, :]], axis=0), w[...], preferred_element_type=jnp.float32)
    qkv[there, :] = y[:256]
    qkv[512:528, :] = y[256:]
    for turn in "ll":
        next(chains[turn], None)

    def rotated(x):
        turned = jnp.where(lane % 64 < 32, -pltpu.roll(x, 96, 1), pltpu.roll(x, 32, 1))
        return x * cos[...] + turned * sin[...]

    zero = jnp.zeros((528, 128), jnp.float32)
    for i in range(2):
        q = f32(rotated(qkv[:, 128 * i:128 * i + 128]).astype(jnp.bfloat16)) * 0.125
        for j, x in enumerate((q, pltpu.roll(q, 64, 1))):
            x = jnp.where(lane < 64, x, zero)
            qs[2 * i + j] = x[:512].astype(jnp.bfloat16)
            qt[2 * i + j] = x[504:520].astype(jnp.bfloat16)
    own[0:528, :] = joined(rotated(qkv[:, 256:384]), qkv[:, 384:512]).astype(jnp.bfloat16)
    own[528:640, :] = jnp.zeros((112, 128), jnp.bfloat16)
    for _ in early:
        pass
    for turn in "llll":
        next(chains[turn], None)
    for i in range(4):
        got = kv[256:512, :]
        for o in range(1, 16):
            got = jnp.where(place_of[o] == i, kv[o * 1024 + 256:o * 1024 + 512, :], got)
        near_kv[256 * i:256 * i + 256, :] = got

    def start(n):
        return jnp.full((n, 1), NEG, jnp.float32), jnp.zeros((n, 128), jnp.float32)

    def ranks_of(i):
        xd = (p.x + 2 + 3 * i + 3 * (i // 2) + 2 * (i // 3)) % 4
        return p.oz * 4 + xd, p.z * 4 + xd

    def queries(ranks):
        return jnp.concatenate([qs[h, rows_of(rank), :] for h in range(4) for rank in ranks], axis=0)

    def wide_items():
        items = [(jnp.concatenate([kv[g * 4096 + o * 1024:g * 4096 + o * 1024 + 256, :] for o in range(4)], axis=0), None) for g in range(4)]
        return items + [(near_kv[0:1024, :], None)]

    def near_item(ranks):
        col = lax.broadcasted_iota(jnp.int32, (1, 1152), 1)
        at = lax.broadcasted_iota(jnp.int32, (512, 1), 0) % 128
        rtok = jnp.where(at < 64, 65 * ranks[0] + at, 65 * ranks[1] + at - 64)
        ktok = jnp.where(col < 512, jnp.where(col < my_length, -1, 1 << 20), token_of(col - 512))
        return [(near_kv[1024:2176, :], ktok <= rtok)]

    top, kept[...] = flash_many(start(512), queries(ranks_of(0)), wide_items())
    tops[...] = jnp.broadcast_to(top, (512, 128))
    for _ in late:
        pass
    got = kv[512:1024, :]
    for o in range(1, 16):
        got = jnp.where(my_owner == o, kv[o * 1024 + 512:o * 1024 + 1024, :], got)
    near_kv[1024:1536, :] = got
    near_kv[1536:2176, :] = own[...]
    qb = jnp.concatenate([qt[h] for h in range(4)], axis=0)
    row = lax.broadcasted_iota(jnp.int32, (64, 1), 0) % 16
    r_tok = jnp.where(row < 8, 511 + row, 65 * (row - 8) + 64)
    r_owner = jnp.full((64, 1), my_owner, jnp.int32)
    r_branch = jnp.full((64, 1), my_branch, jnp.int32)
    for i in range(8):
        leaf = decode_leaf[me * 8 + i]
        r_owner = jnp.where(r_tok == 512 + i, leaf_owner[leaf], r_owner)
        r_branch = jnp.where(r_tok == 512 + i, leaf_parent[leaf], r_branch)
    items = []
    col = lax.broadcasted_iota(jnp.int32, (1, 1024), 1)
    for o in range(16):
        see_branch = jnp.where(r_branch == branch_of[o], 512, 256)
        see_leaf = jnp.where(r_owner == o, 512 + length_of[o], 512)
        items.append((kv[o * 1024:o * 1024 + 1024, :], (col < see_branch) | ((col >= 512) & (col < see_leaf))))
    ktok = token_of(lax.broadcasted_iota(jnp.int32, (1, 640), 1))
    items.append((own[...], (ktok == r_tok) | ((ktok <= r_tok) & (r_tok < 512))))
    tail[...] = finish(flash_many(start(64), qb, items), 16)
    loads[5].wait()
    singles = jnp.concatenate([tail[8:16, :], jnp.zeros((8, 256), jnp.float32)], axis=0).astype(jnp.bfloat16)
    y = jnp.dot(singles, wo[...], preferred_element_type=jnp.float32)
    for e in range(8):
        pe[e] = y[e:e + 1]

    steps, finish_sums = early_sums(links, p, part, pe, bufs1)

    def two_ranks(i, _):
        ranks = ranks_of(i)

        def keep(state):
            got = finish(state, 128)
            for j, rank in enumerate(ranks):
                main[rows_of(rank), :] = got[64 * j:64 * j + 64]

        @pl.when(i == 0)
        def _():
            keep(flash_many((tops[:, 0:1], kept[...]), queries(ranks), near_item(ranks)))

        @pl.when(i > 0)
        def _():
            keep(flash_many(start(512), queries(ranks), wide_items() + near_item(ranks)))

        main[504:512, :] = tail[0:8, :]
        lhs = jnp.concatenate([main[rows_of(rank), :] for rank in ranks], axis=0).astype(jnp.bfloat16)
        for quarter in QUARTERS:
            y = jnp.dot(lhs, wo[:, quarter], preferred_element_type=jnp.float32).astype(jnp.bfloat16)
            for j, rank in enumerate(ranks):
                part[rows_of(rank), quarter] = y[64 * j:64 * j + 64]
        for k, step in enumerate(steps):
            pl.when(i == k)(step)
        return 0

    lax.fori_loop(0, 4, two_ranks, 0)
    mine, single = finish_sums()
    mine = f32(hidden[0:64, :]) + mine
    single = f32(hidden[64:65, :]) + single
    res[0:64, :] = mine
    res[64:65, :] = single
    gains = wide_row(gain_m)
    over = ((0, 32, p.mate), (32, 32, far))
    xall[rows_of(p.t), :] = scaled(mine, gains)
    ext[p.t] = f32(scaled(single, gains))
    rows = gather_rows_steps(links, p, xall, ext, CUT, over)
    next(rows)
    for b in range(8):
        joint[65 * b:65 * b + 64, :] = main[64 * b:64 * b + 64, :]
        joint[65 * b + 64:65 * b + 65, :] = tail[8 + b:9 + b, :]
    att_out[...] = joint[...].astype(jnp.bfloat16)
    loads[6].wait()
    loads[7].wait()

    def units(lhs, store):
        for lo, n in ((0, 256), (256, 256), (512, 192)):
            g = lax.dot_general(lhs, wg[lo:lo + n, :], NT, preferred_element_type=jnp.float32)
            u = lax.dot_general(lhs, wu[lo:lo + n, :], NT, preferred_element_type=jnp.float32)
            store(lo, n, (g / (1.0 + jnp.exp(-g)) * u).astype(jnp.bfloat16))

    for _ in range(9):
        next(rows)

    def store_here(lo, n, h):
        hid[here, lo:lo + n] = h

    def store_there(lo, n, h):
        hid[there, lo:lo + n] = h[:256]
        hid[512:528, lo:lo + n] = h[256:]

    units(xall[here, :], store_here)
    for _ in rows:
        pass
    place_singles(ext, xall)
    units(jnp.concatenate([xall[there, :], xall[512:528, :]], axis=0), store_there)
    loads[8].wait()

    def produce(q):
        y = jnp.dot(hid[...], wd[:, QUARTERS[q]], preferred_element_type=jnp.float32)
        part2[:, QUARTERS[q]] = y[:512].astype(jnp.bfloat16)
        for e in range(8):
            pe2[e, :, QUARTERS[q]] = y[512 + e:513 + e]

    mine, single = scatter_sums(links, p, produce, part2, pe2, bufs2, CUT, over)
    out[0:64, :] = (res[0:64, :] + mine).astype(jnp.bfloat16)
    out[64:65, :] = (res[64:65, :] + single).astype(jnp.bfloat16)
    links.drain()


def per_device(hidden_in, norm_attn, w_query, w_key, w_value, w_out, norm_mlp, w_gate, w_up, w_down,
               cache_keys, cache_values, leaf_parent, leaf_owner, leaf_length, prompt_leaf, decode_leaf):
    freq = 10000.0 ** (-((np.arange(128) % 32).astype(np.float32) * np.float32(2.0) / np.float32(64)))
    freq = jnp.asarray(freq.astype(np.float32)[None, :])
    vm = pl.BlockSpec(memory_space=pltpu.VMEM)
    sm = pl.BlockSpec(memory_space=pltpu.SMEM)
    hbm = pl.BlockSpec(memory_space=pltpu.HBM)
    bf, fl = jnp.bfloat16, jnp.float32
    def buf(*shape, kind=bf):
        return pltpu.VMEM(shape, kind)
    scratch = [buf(16384, 128), buf(528, 2048), buf(8, 1, 2048, kind=fl), buf(2048, 512), buf(1024, 128), buf(1024, 128),
               buf(528, 128, kind=fl), buf(528, 128, kind=fl), buf(4, 512, 128), buf(4, 16, 128), buf(640, 128),
               buf(512, 256, kind=fl), buf(16, 256, kind=fl), buf(520, 256, kind=fl), buf(2176, 128),
               buf(1024, 128), buf(1024, 128), buf(1024, 128), buf(528, 512, kind=fl),
               buf(512, 128, kind=fl), buf(512, 128, kind=fl)]
    scratch += [buf(256, 2048), buf(704, 2048), buf(704, 2048), buf(704, 2048), buf(512, 2048), buf(8, 1, 2048, kind=fl),
                buf(528, 2048), buf(8, 1, 2048, kind=fl), buf(528, 704), buf(65, 2048, kind=fl), buf(512, 2048), buf(8, 1, 2048, kind=fl)]
    scratch += sum_bufs(1024) + sum_bufs(CUT)
    scratch += [pltpu.SemaphoreType.DMA((160,)), pltpu.SemaphoreType.DMA((160,)), pltpu.SemaphoreType.DMA((11,))]
    return pl.pallas_call(
        layer_kernel,
        out_shape=(jax.ShapeDtypeStruct((65, 2048), bf), jax.ShapeDtypeStruct((520, 256), bf)),
        in_specs=[vm] * 4 + [sm] * 5 + [hbm] * 9,
        out_specs=(vm, vm),
        scratch_shapes=scratch,
        compiler_params=pltpu.CompilerParams(vmem_limit_bytes=60 << 20, collective_id=1, has_side_effects=True),
        cost_estimate=pl.CostEstimate(flops=10**10, bytes_accessed=14 * 10**6, transcendentals=15 * 10**6),
        name="layer",
    )(hidden_in, norm_attn.reshape(16, 128), norm_mlp.reshape(16, 128), freq, leaf_parent, leaf_owner, leaf_length, prompt_leaf,
      decode_leaf, w_query, w_key, w_value, cache_keys, cache_values, w_out, w_gate.T, w_up.T, w_down)


def solution(mesh):
    in_specs = (P(("kv", "tp"), None), P(), P(None, "tp"), P(), P(), P("tp", None), P(), P(None, "tp"), P(None, "tp"),
                P("tp", None), P("kv", None), P("kv", None), P(), P(), P(), P(), P())
    out_specs = (P(("kv", "tp"), None), P("kv", "tp"))
    return jax.shard_map(per_device, mesh=mesh, in_specs=in_specs, out_specs=out_specs, check_vma=False)
```

```python
import jax
import jax.numpy as jnp
import numpy as np
from jax import lax
from jax.experimental import pallas as pl
from jax.experimental.pallas import tpu as pltpu
from jax.sharding import PartitionSpec as P

NEG = -1e30
NT = (((1,), (1,)), ((), ()))

def flash_many(st, qb, items):
    ss=lax.dot_general(qb, items[0][0], NT, preferred_element_type=jnp.float32)
    for i,(kvb,mask) in enumerate(items):
        nx = lax.dot_general(qb, items[i+1][0], NT, preferred_element_type=jnp.float32) if i+1<len(items) else None
        st = flash_step(st, qb, kvb, mask, ss)
        ss = nx
    return st

def flash_step(state, qb, kvb, mask, s=None):
    m, acc = state
    if s is None:
        s = lax.dot_general(qb, kvb, NT, preferred_element_type=jnp.float32)
    if mask is not None:
        s = jnp.where(mask, s, NEG)
    m_new = jnp.maximum(m, jnp.max(s, axis=1, keepdims=True))
    p = jnp.exp(s - m_new).astype(jnp.bfloat16)
    lane = lax.broadcasted_iota(jnp.int32, kvb.shape, 1)
    vaug = jnp.where(lane < 64, jnp.ones_like(kvb), kvb)
    acc = acc * jnp.exp(m - m_new) + jnp.dot(p, vaug, preferred_element_type=jnp.float32)
    return m_new, acc

def finish(state, rows):
    m, acc = state
    ratio = pltpu.roll(acc, 64, 1) / acc
    h = [ratio[i * rows:(i + 1) * rows] for i in range(4)]
    lane = lax.broadcasted_iota(jnp.int32, (rows, 128), 1)
    a = jnp.where(lane < 64, h[0], pltpu.roll(h[1], 64, 1))
    b = jnp.where(lane < 64, h[2], pltpu.roll(h[3], 64, 1))
    return jnp.concatenate([a, b], axis=1)

def token_of(idx):
    return jnp.where(idx < 512, 65 * (idx // 64) + idx % 64,
                     jnp.where(idx < 520, 65 * (idx - 512) + 64, 1 << 20))

MESH = pl.DeviceIdType.MESH
QUARTERS = tuple(pl.ds(512 * i, 512) for i in range(4))


class Transfer:
    def __init__(self, links, k, src, dst, where):
        self.parts = links, k, src, dst, where

    def copy(self):
        links, k, src, dst, where = self.parts
        return pltpu.make_async_remote_copy(src_ref=src(), dst_ref=dst(), send_sem=links.send_sem.at[k], recv_sem=links.recv_sem.at[k],
                                            device_id=where, device_id_type=MESH)

    def start(self):
        self.copy().start()
        return self

    def wait_recv(self):
        self.copy().wait_recv()

    def wait_send(self):
        self.copy().wait_send()


class Links:
    def __init__(self, send_sem, recv_sem):
        self.send_sem, self.recv_sem, self.open = send_sem, recv_sem, []

    def plan(self, src, dst, where):
        self.open.append(Transfer(self, len(self.open), src, dst, where))
        return self.open[-1]

    def send(self, src, dst, where):
        return self.plan(lambda: src, lambda: dst, where).start()

    def drain(self):
        for transfer in self.open:
            transfer.wait_send()


class Place:
    def __init__(self):
        self.t = lax.axis_index("tp")
        self.z, self.x = lax.div(self.t, 4), lax.rem(self.t, 4)
        self.xr, self.xl, self.opp = lax.rem(self.x + 1, 4), lax.rem(self.x + 3, 4), lax.rem(self.x + 2, 4)
        self.oz = 1 - self.z
        self.right = {"tp": self.z * 4 + self.xr}
        self.left = {"tp": self.z * 4 + self.xl}
        self.mate = {"tp": self.oz * 4 + self.x}

    def peer(self, k):
        return lax.rem(self.t + k, 8)


def rows_of(rank):
    return pl.ds(pl.multiple_of(rank * 64, 64), 64)


def cuts(cut):
    a, b = cut // 2, (2048 - cut) // 2
    return ((pl.ds(0, cut), pl.ds(0, a), pl.ds(a, a)), (pl.ds(cut, 2 * b), pl.ds(cut, b), pl.ds(cut + b, b)))


def gather_rows_steps(links, p, xall, ext, cut, over):
    (A, A0, A1), (B, B0, B1) = cuts(cut)
    def blk(z, x, cols, lo=0, n=64):
        return xall.at[pl.ds(pl.multiple_of((z * 4 + x) * 64 + lo, n), n), cols]
    def go(z, x, cols, where):
        return [links.send(blk(z, x, cols), blk(z, x, cols), where)]
    def cross(z, x, cols):
        return [links.send(blk(z, x, cols, lo, n), blk(z, x, cols, lo, n), where) for lo, n, where in over]
    def wait(copies):
        for copy in copies:
            copy.wait_recv()
    az = cross(p.z, p.x, A)
    br, bl = go(p.z, p.x, B, p.right), go(p.z, p.x, B, p.left)
    ar, al = go(p.z, p.x, A, p.right), go(p.z, p.x, A, p.left)
    rest = cross(p.z, p.x, B)
    rest += [links.send(ext.at[p.t], ext.at[p.t], {"tp": p.peer(k)}) for k in range(1, 8)]
    yield 1
    wait(br)
    b0 = go(p.z, p.xl, B0, p.right)
    rest += cross(p.z, p.xl, B)
    yield 1
    wait(bl)
    b1 = go(p.z, p.xr, B1, p.left)
    rest += cross(p.z, p.xr, B)
    yield 1
    wait(az)
    far_r, far_l = go(p.oz, p.x, A, p.right), go(p.oz, p.x, A, p.left)
    yield 1
    wait(ar)
    near = go(p.z, p.xl, A0, p.right)
    yield 1
    wait(al)
    near += go(p.z, p.xr, A1, p.left)
    yield 1
    wait(b0)
    rest += cross(p.z, p.opp, B0)
    wait(b1)
    rest += cross(p.z, p.opp, B1)
    yield 1
    wait(far_r)
    rest += go(p.oz, p.xl, A0, p.right)
    yield 1
    wait(far_l)
    rest += go(p.oz, p.xr, A1, p.left)
    yield 1
    wait(near)
    yield 1
    wait(rest)


def f32(x):
    return x.astype(jnp.float32)


def scatter_sums(links, p, produce, part, pe, bufs, cut, over):
    near, wide, zb, bq, bw, za, eb = bufs
    (A, A0, A1), (B, B0, B1) = cuts(cut)
    planes = (p.oz, p.z)
    def blk(z, x, cols, lo=0, n=64):
        return part.at[pl.ds(pl.multiple_of((z * 4 + x) * 64 + lo, n), n), cols]
    def cross(z, x, cols, dst):
        return [links.send(blk(z, x, cols, lo, n), dst.at[lo:lo + n, :], where) for lo, n, where in over]
    def wait(copies):
        for copy in copies:
            copy.wait_recv()
    def add(z, x, cols, more):
        at = blk(z, x, cols)
        at[...] = (f32(at[...]) + f32(more)).astype(jnp.bfloat16)
    split = cut // 512
    for q in range(split, 4):
        produce(q)
    order = (p.opp, p.xr, p.xl, p.x)
    bz = [cross(p.oz, xd, B, zb.at[i]) for i, xd in enumerate(order)]
    for q in range(split):
        produce(q)
    ar = [links.send(blk(z, p.opp, A0), near.at[0, i], p.right) for i, z in enumerate(planes)]
    al = [links.send(blk(z, p.opp, A1), near.at[1, i], p.left) for i, z in enumerate(planes)]
    singles = [links.send(pe.at[p.peer(k)], eb.at[k], {"tp": p.peer(k)}) for k in range(1, 8)]
    wait(bz[0])
    add(p.z, p.opp, B, zb[0])
    b_r = links.send(blk(p.z, p.opp, B0), bq.at[0], p.right)
    b_l = links.send(blk(p.z, p.opp, B1), bq.at[1], p.left)
    wr, wl = [], []
    for i, z in enumerate(planes):
        ar[i].wait_recv()
        add(z, p.xr, A0, near[0, i])
        wr.append(links.send(blk(z, p.xr, A), wide.at[0, i], p.right))
        al[i].wait_recv()
        add(z, p.xl, A1, near[1, i])
        wl.append(links.send(blk(z, p.xl, A), wide.at[1, i], p.left))
    wait(bz[1])
    add(p.z, p.xr, B, zb[1])
    b_r.wait_recv()
    add(p.z, p.xr, B0, bq[0])
    b_rw = links.send(blk(p.z, p.xr, B), bw.at[0], p.right)
    wait(bz[2])
    add(p.z, p.xl, B, zb[2])
    b_l.wait_recv()
    add(p.z, p.xl, B1, bq[1])
    b_lw = links.send(blk(p.z, p.xl, B), bw.at[1], p.left)
    wr[0].wait_recv()
    wl[0].wait_recv()
    add(p.oz, p.x, A, f32(wide[0, 0]) + f32(wide[1, 0]))
    a_z = cross(p.oz, p.x, A, za)
    wait([wr[1], wl[1]] + bz[3] + [b_rw, b_lw])
    mine_a = f32(blk(p.z, p.x, A)[...]) + f32(wide[0, 1]) + f32(wide[1, 1])
    mine_b = f32(blk(p.z, p.x, B)[...]) + f32(zb[3]) + f32(bw[0]) + f32(bw[1])
    wait(singles)
    single = pe[p.t]
    for k in range(1, 8):
        single = single + eb[k]
    wait(a_z)
    return jnp.concatenate([mine_a + f32(za[...]), mine_b], axis=1), single


def sum_bufs(cut):
    bf, a, b = jnp.bfloat16, cut, 2048 - cut
    return [pltpu.VMEM((2, 2, 64, a // 2), bf), pltpu.VMEM((2, 2, 64, a), bf), pltpu.VMEM((4, 64, b), bf),
            pltpu.VMEM((2, 64, b // 2), bf), pltpu.VMEM((2, 64, b), bf), pltpu.VMEM((64, a), bf),
            pltpu.VMEM((8, 1, 2048), jnp.float32)]


def wide_row(gain):
    rows = gain[...].astype(jnp.float32)
    return jnp.concatenate([rows[i:i + 1] for i in range(16)], axis=1)


def scaled(values, gain):
    mean_square = jnp.mean(values * values, axis=-1, keepdims=True)
    return (values * lax.rsqrt(mean_square + 1e-05) * gain).astype(jnp.bfloat16)


def place_singles(ext, xall):
    rows = [ext[e] for e in range(8)]
    xall[512:528, :] = jnp.concatenate(rows + [jnp.zeros((8, 2048), jnp.float32)], axis=0).astype(jnp.bfloat16)


class Ring:
    def __init__(self):
        self.o = lax.axis_index("kv")
        self.y, rest = lax.div(self.o, 4), lax.rem(self.o, 4)
        self.h, self.c = lax.div(rest, 2), lax.rem(rest, 2)
        self.yr, self.yl, self.opp = lax.rem(self.y + 1, 4), lax.rem(self.y + 3, 4), lax.rem(self.y + 2, 4)
        self.oh = 1 - self.h
        self.right, self.left = {"kv": self.at(self.yr, self.h)}, {"kv": self.at(self.yl, self.h)}
        self.mate, self.twin = {"kv": self.at(self.y, self.oh)}, {"kv": self.o + 1 - 2 * self.c}

    def at(self, y, h):
        return y * 4 + h * 2 + self.c


def gather_cache(links, r, kv, far_slab, far, lo, n):
    top, low, whole = (lo, n // 2), (lo + n // 2, n // 2), (lo, n)
    twins = []
    def go(y, h, rows, where):
        at = kv.at[pl.ds(pl.multiple_of(r.at(y, h) * 1024 + rows[0], 256), rows[1]), :]
        return links.send(at, at, where)
    def share(y, h, rows):
        twins.append(go(y, h, rows, r.twin))
    m = links.send(far_slab.at[lo:lo + n, :], kv.at[pl.ds(pl.multiple_of(r.o * 1024 + lo, 512), n), :], far)
    a = go(r.y, r.h, whole, r.right), go(r.y, r.h, whole, r.left)
    share(r.y, r.h, whole)
    yield 1
    m.wait_recv()
    b = go(r.y, r.oh, whole, r.right), go(r.y, r.oh, whole, r.left)
    share(r.y, r.oh, whole)
    yield 1
    ends = []
    for (from_left, from_right), h in ((a, r.h), (b, r.oh)):
        from_left.wait_recv()
        ends.append((go(r.yl, h, top, r.right), h, top))
        share(r.yl, h, whole)
        yield 1
        from_right.wait_recv()
        ends.append((go(r.yr, h, low, r.left), h, low))
        share(r.yr, h, whole)
        yield 1
    for copy, h, rows in ends:
        copy.wait_recv()
        share(r.opp, h, rows)
        yield 1
    for copy in twins:
        copy.wait_recv()


CUT = 512


def early_sums(links, p, part, pe, bufs):
    near, wide, zb, bq, bw, za, eb = bufs
    (A, A0, A1), (B, B0, B1) = cuts(1024)
    planes = (p.oz, p.z)
    order = (p.opp, p.xr, p.xl, p.x)
    def blk(z, x, cols):
        return part.at[rows_of(z * 4 + x), cols]
    def add(z, x, cols, more):
        at = blk(z, x, cols)
        at[...] = (f32(at[...]) + f32(more)).astype(jnp.bfloat16)
    def plan(z, x, cols, dst, where):
        return links.plan(lambda: blk(z, x, cols), dst, where)
    bz = [plan(p.oz, xd, B, lambda i=i: zb.at[i], p.mate) for i, xd in enumerate(order)]
    ar = [plan(z, p.opp, A0, lambda i=i: near.at[0, i], p.right) for i, z in enumerate(planes)]
    al = [plan(z, p.opp, A1, lambda i=i: near.at[1, i], p.left) for i, z in enumerate(planes)]
    wr = [plan(z, p.xr, A, lambda i=i: wide.at[0, i], p.right) for i, z in enumerate(planes)]
    wl = [plan(z, p.xl, A, lambda i=i: wide.at[1, i], p.left) for i, z in enumerate(planes)]
    b_r, b_l = plan(p.z, p.opp, B0, lambda: bq.at[0], p.right), plan(p.z, p.opp, B1, lambda: bq.at[1], p.left)
    b_rw, b_lw = plan(p.z, p.xr, B, lambda: bw.at[0], p.right), plan(p.z, p.xl, B, lambda: bw.at[1], p.left)
    a_z = plan(p.oz, p.x, A, lambda: za, p.mate)
    singles = [links.plan(lambda k=k: pe.at[p.peer(k)], lambda k=k: eb.at[k], {"tp": p.peer(k)}) for k in range(1, 8)]

    def step0():
        for copy in [bz[0]] + ar + al + singles:
            copy.start()

    def step1():
        bz[1].start()
        bz[0].wait_recv()
        add(p.z, p.opp, B, zb[0])
        b_r.start()
        b_l.start()
        for i, z in enumerate(planes):
            ar[i].wait_recv()
            add(z, p.xr, A0, near[0, i])
            wr[i].start()

    def step2():
        bz[2].start()
        for i, z in enumerate(planes):
            al[i].wait_recv()
            add(z, p.xl, A1, near[1, i])
            wl[i].start()
        bz[1].wait_recv()
        add(p.z, p.xr, B, zb[1])
        b_r.wait_recv()
        add(p.z, p.xr, B0, bq[0])
        b_rw.start()

    def step3():
        bz[3].start()
        bz[2].wait_recv()
        add(p.z, p.xl, B, zb[2])
        b_l.wait_recv()
        add(p.z, p.xl, B1, bq[1])
        b_lw.start()
        wr[0].wait_recv()
        wl[0].wait_recv()
        add(p.oz, p.x, A, f32(wide[0, 0]) + f32(wide[1, 0]))
        a_z.start()

    def finish_sums():
        wr[1].wait_recv()
        wl[1].wait_recv()
        mine_a = f32(blk(p.z, p.x, A)[...]) + f32(wide[0, 1]) + f32(wide[1, 1])
        for copy in singles:
            copy.wait_recv()
        single = pe[p.t]
        for k in range(1, 8):
            single = single + eb[k]
        for copy in (b_rw, bz[3], a_z, b_lw):
            copy.wait_recv()
        mine_b = f32(blk(p.z, p.x, B)[...]) + f32(zb[3]) + f32(bw[0]) + f32(bw[1])
        return jnp.concatenate([mine_a + f32(za[...]), mine_b], axis=1), single

    return (step0, step1, step2, step3), finish_sums


def layer_kernel(hidden, gain_a, gain_m, freq, leaf_parent, leaf_owner, leaf_length, prompt_leaf, decode_leaf,
                 wq_h, wk_h, wv_h, ck_h, cv_h, wo_h, wg_h, wu_h, wd_h, out, att_out, *s):
    (kv, xin, ein, w, ck, cv, cos, sin, qs, qt, own, main, tail, joint, near_kv, ck2, cv2, far_slab, qkv, tops, kept), s = s[:21], s[21:]
    (wo, wg, wu, wd, part, pe, xall, ext, hid, res, part2, pe2), s = s[:12], s[12:]
    bufs1, bufs2, (send_sem, recv_sem, wsem) = s[:7], s[7:14], s[14:]
    p, r = Place(), Ring()
    links = Links(send_sem, recv_sem)
    far = {"kv": r.at(r.y, r.oh), "tp": p.oz * 4 + p.x}
    barrier = pltpu.get_barrier_semaphore()
    for where in [{"tp": p.peer(k)} for k in range(1, 8)] + [r.right, r.left, far, r.twin]:
        pl.semaphore_signal(barrier, inc=1, device_id=where, device_id_type=MESH)
    head = lax.div(p.t, 2)
    odd = lax.rem(head, 2)
    pair = pl.ds(pl.multiple_of(lax.div(head, 2) * 128, 128), 128)
    pair2 = pl.ds(pl.multiple_of(p.oz * 128, 128), 128)
    moves = ((ck_h.at[:, pair], ck), (cv_h.at[:, pair], cv), (wq_h, w.at[:, 0:256]), (wk_h.at[:, pair], w.at[:, 256:384]),
             (wv_h.at[:, pair], w.at[:, 384:512]), (wo_h, wo), (wg_h, wg), (wu_h, wu), (wd_h, wd),
             (ck_h.at[:, pair2], ck2), (cv_h.at[:, pair2], cv2))
    loads = [pltpu.make_async_copy(a, b, wsem.at[i]) for i, (a, b) in enumerate(moves)]
    for i in (9, 10, 0, 1):
        loads[i].start()
    gains = wide_row(gain_a)
    xin[rows_of(p.t), :] = scaled(f32(hidden[0:64, :]), gains)
    ein[p.t] = f32(scaled(f32(hidden[64:65, :]), gains))
    pl.semaphore_wait(barrier, 11)
    rows = gather_rows_steps(links, p, xin, ein, 1536, ((0, 64, p.mate),))
    next(rows)
    lane = lax.broadcasted_iota(jnp.int32, (1, 128), 1)

    def joined(keys, values):
        k = jnp.where(odd == 1, pltpu.roll(keys, 64, 1), keys)
        v = jnp.where(odd == 1, values, pltpu.roll(values, 64, 1))
        return jnp.where(lane < 64, k, v)

    loads[9].wait()
    loads[10].wait()
    far_slab[...] = joined(f32(ck2[...]), f32(cv2[...])).astype(jnp.bfloat16)
    loads[0].wait()
    loads[1].wait()
    kv[pl.ds(pl.multiple_of(r.o * 1024, 1024), 1024), :] = joined(f32(ck[...]), f32(cv[...])).astype(jnp.bfloat16)
    early, late = (gather_cache(links, r, kv, far_slab, far, lo, 512) for lo in (0, 512))
    next(early)
    for load in loads[2:9]:
        load.start()
    me = r.o
    my_leaf = prompt_leaf[me]
    my_owner = leaf_owner[my_leaf]
    my_length = leaf_length[my_leaf]
    my_branch = leaf_parent[my_leaf]
    ramp = lax.broadcasted_iota(jnp.int32, (64, 1), 0)
    step_angle = ramp.astype(jnp.float32) * freq[...]
    rank_angle = (65 * ramp[:8] + (5120 + my_length)).astype(jnp.float32) * freq[...]
    spot = jnp.where(ramp[:16] < 8, my_length + 511, my_length + 64 + 65 * (ramp[:16] - 8))
    for i in range(8):
        spot = jnp.where(ramp[:16] == (i + 1 if i < 7 else 15), leaf_length[decode_leaf[me * 8 + i]], spot)
    spot_angle = (spot + 5120).astype(jnp.float32) * freq[...]
    c1, s1, c8, s8 = jnp.cos(step_angle), jnp.sin(step_angle), jnp.cos(rank_angle), jnp.sin(rank_angle)
    for b in range(8):
        cos[64 * b:64 * b + 64, :] = c8[b:b + 1] * c1 - s8[b:b + 1] * s1
        sin[64 * b:64 * b + 64, :] = s8[b:b + 1] * c1 + c8[b:b + 1] * s1
    cos[504:520, :] = jnp.cos(spot_angle)
    sin[504:520, :] = jnp.sin(spot_angle)
    cos[520:528, :] = jnp.zeros((8, 128), jnp.float32)
    sin[520:528, :] = jnp.zeros((8, 128), jnp.float32)
    branch_of, length_of, place_of, count = [], [], [], jnp.int32(0)
    for o in range(16):
        branch, length = jnp.int32(0), jnp.int32(0)
        for leaf in range(16):
            held = leaf_owner[leaf] == o
            branch = jnp.where(held, leaf_parent[leaf], branch)
            length = jnp.where(held, leaf_length[leaf], length)
        branch_of.append(branch)
        length_of.append(length)
        place_of.append(jnp.where(branch == my_branch, count, 4))
        count = count + jnp.where(branch == my_branch, 1, 0)
    chains = {"r": rows, "e": early, "l": late}
    for turn in "rrreleerreereeeerrlllr":
        next(chains[turn], None)
    for load in loads[2:5]:
        load.wait()
    here, there = (pl.ds(pl.multiple_of(z * 256, 256), 256) for z in (p.z, p.oz))
    qkv[here, :] = jnp.dot(xin[here, :], w[...], preferred_element_type=jnp.float32)
    for _ in rows:
        pass
    place_singles(ein, xin)
    y = jnp.dot(jnp.concatenate([xin[there, :], xin[512:528, :]], axis=0), w[...], preferred_element_type=jnp.float32)
    qkv[there, :] = y[:256]
    qkv[512:528, :] = y[256:]
    for turn in "ll":
        next(chains[turn], None)

    def rotated(x):
        turned = jnp.where(lane % 64 < 32, -pltpu.roll(x, 96, 1), pltpu.roll(x, 32, 1))
        return x * cos[...] + turned * sin[...]

    zero = jnp.zeros((528, 128), jnp.float32)
    for i in range(2):
        q = f32(rotated(qkv[:, 128 * i:128 * i + 128]).astype(jnp.bfloat16)) * 0.125
        for j, x in enumerate((q, pltpu.roll(q, 64, 1))):
            x = jnp.where(lane < 64, x, zero)
            qs[2 * i + j] = x[:512].astype(jnp.bfloat16)
            qt[2 * i + j] = x[504:520].astype(jnp.bfloat16)
    own[0:528, :] = joined(rotated(qkv[:, 256:384]), qkv[:, 384:512]).astype(jnp.bfloat16)
    own[528:640, :] = jnp.zeros((112, 128), jnp.bfloat16)
    for _ in early:
        pass
    for turn in "llll":
        next(chains[turn], None)
    for i in range(4):
        got = kv[256:512, :]
        for o in range(1, 16):
            got = jnp.where(place_of[o] == i, kv[o * 1024 + 256:o * 1024 + 512, :], got)
        near_kv[256 * i:256 * i + 256, :] = got

    def start(n):
        return jnp.full((n, 1), NEG, jnp.float32), jnp.zeros((n, 128), jnp.float32)

    def ranks_of(i):
        xd = (p.x + 2 + 3 * i + 3 * (i // 2) + 2 * (i // 3)) % 4
        return p.oz * 4 + xd, p.z * 4 + xd

    def queries(ranks):
        return jnp.concatenate([qs[h, rows_of(rank), :] for h in range(4) for rank in ranks], axis=0)

    def wide_items():
        items = [(jnp.concatenate([kv[g * 4096 + o * 1024:g * 4096 + o * 1024 + 256, :] for o in range(4)], axis=0), None) for g in range(4)]
        return items + [(near_kv[0:1024, :], None)]

    def near_item(ranks):
        col = lax.broadcasted_iota(jnp.int32, (1, 1152), 1)
        at = lax.broadcasted_iota(jnp.int32, (512, 1), 0) % 128
        rtok = jnp.where(at < 64, 65 * ranks[0] + at, 65 * ranks[1] + at - 64)
        ktok = jnp.where(col < 512, jnp.where(col < my_length, -1, 1 << 20), token_of(col - 512))
        return [(near_kv[1024:2176, :], ktok <= rtok)]

    top, kept[...] = flash_many(start(512), queries(ranks_of(0)), wide_items())
    tops[...] = jnp.broadcast_to(top, (512, 128))
    for _ in late:
        pass
    got = kv[512:1024, :]
    for o in range(1, 16):
        got = jnp.where(my_owner == o, kv[o * 1024 + 512:o * 1024 + 1024, :], got)
    near_kv[1024:1536, :] = got
    near_kv[1536:2176, :] = own[...]
    qb = jnp.concatenate([qt[h] for h in range(4)], axis=0)
    row = lax.broadcasted_iota(jnp.int32, (64, 1), 0) % 16
    r_tok = jnp.where(row < 8, 511 + row, 65 * (row - 8) + 64)
    r_owner = jnp.full((64, 1), my_owner, jnp.int32)
    r_branch = jnp.full((64, 1), my_branch, jnp.int32)
    for i in range(8):
        leaf = decode_leaf[me * 8 + i]
        r_owner = jnp.where(r_tok == 512 + i, leaf_owner[leaf], r_owner)
        r_branch = jnp.where(r_tok == 512 + i, leaf_parent[leaf], r_branch)
    items = []
    col = lax.broadcasted_iota(jnp.int32, (1, 1024), 1)
    for o in range(16):
        see_branch = jnp.where(r_branch == branch_of[o], 512, 256)
        see_leaf = jnp.where(r_owner == o, 512 + length_of[o], 512)
        items.append((kv[o * 1024:o * 1024 + 1024, :], (col < see_branch) | ((col >= 512) & (col < see_leaf))))
    ktok = token_of(lax.broadcasted_iota(jnp.int32, (1, 640), 1))
    items.append((own[...], (ktok == r_tok) | ((ktok <= r_tok) & (r_tok < 512))))
    tail[...] = finish(flash_many(start(64), qb, items), 16)
    loads[5].wait()
    singles = jnp.concatenate([tail[8:16, :], jnp.zeros((8, 256), jnp.float32)], axis=0).astype(jnp.bfloat16)
    y = jnp.dot(singles, wo[...], preferred_element_type=jnp.float32)
    for e in range(8):
        pe[e] = y[e:e + 1]

    steps, finish_sums = early_sums(links, p, part, pe, bufs1)

    def two_ranks(i, _):
        ranks = ranks_of(i)

        def keep(state):
            got = finish(state, 128)
            for j, rank in enumerate(ranks):
                main[rows_of(rank), :] = got[64 * j:64 * j + 64]

        @pl.when(i == 0)
        def _():
            keep(flash_many((tops[:, 0:1], kept[...]), queries(ranks), near_item(ranks)))

        @pl.when(i > 0)
        def _():
            keep(flash_many(start(512), queries(ranks), wide_items() + near_item(ranks)))

        main[504:512, :] = tail[0:8, :]
        lhs = jnp.concatenate([main[rows_of(rank), :] for rank in ranks], axis=0).astype(jnp.bfloat16)
        for quarter in QUARTERS:
            y = jnp.dot(lhs, wo[:, quarter], preferred_element_type=jnp.float32).astype(jnp.bfloat16)
            for j, rank in enumerate(ranks):
                part[rows_of(rank), quarter] = y[64 * j:64 * j + 64]
        for k, step in enumerate(steps):
            pl.when(i == k)(step)
        return 0

    lax.fori_loop(0, 4, two_ranks, 0)
    mine, single = finish_sums()
    mine = f32(hidden[0:64, :]) + mine
    single = f32(hidden[64:65, :]) + single
    res[0:64, :] = mine
    res[64:65, :] = single
    gains = wide_row(gain_m)
    over = ((0, 32, p.mate), (32, 32, far))
    xall[rows_of(p.t), :] = scaled(mine, gains)
    ext[p.t] = f32(scaled(single, gains))
    rows = gather_rows_steps(links, p, xall, ext, CUT, over)
    next(rows)
    for b in range(8):
        joint[65 * b:65 * b + 64, :] = main[64 * b:64 * b + 64, :]
        joint[65 * b + 64:65 * b + 65, :] = tail[8 + b:9 + b, :]
    att_out[...] = joint[...].astype(jnp.bfloat16)
    loads[6].wait()
    loads[7].wait()

    def units(lhs, store):
        for lo, n in ((0, 256), (256, 256), (512, 192)):
            g = lax.dot_general(lhs, wg[lo:lo + n, :], NT, preferred_element_type=jnp.float32)
            u = lax.dot_general(lhs, wu[lo:lo + n, :], NT, preferred_element_type=jnp.float32)
            store(lo, n, (g / (1.0 + jnp.exp(-g)) * u).astype(jnp.bfloat16))

    for _ in range(9):
        next(rows)

    def store_here(lo, n, h):
        hid[here, lo:lo + n] = h

    def store_there(lo, n, h):
        hid[there, lo:lo + n] = h[:256]
        hid[512:528, lo:lo + n] = h[256:]

    units(xall[here, :], store_here)
    for _ in rows:
        pass
    place_singles(ext, xall)
    units(jnp.concatenate([xall[there, :], xall[512:528, :]], axis=0), store_there)
    loads[8].wait()

    def produce(q):
        y = jnp.dot(hid[...], wd[:, QUARTERS[q]], preferred_element_type=jnp.float32)
        part2[:, QUARTERS[q]] = y[:512].astype(jnp.bfloat16)
        for e in range(8):
            pe2[e, :, QUARTERS[q]] = y[512 + e:513 + e]

    mine, single = scatter_sums(links, p, produce, part2, pe2, bufs2, CUT, over)
    out[0:64, :] = (res[0:64, :] + mine).astype(jnp.bfloat16)
    out[64:65, :] = (res[64:65, :] + single).astype(jnp.bfloat16)
    links.drain()


def per_device(hidden_in, norm_attn, w_query, w_key, w_value, w_out, norm_mlp, w_gate, w_up, w_down,
               cache_keys, cache_values, leaf_parent, leaf_owner, leaf_length, prompt_leaf, decode_leaf):
    freq = 10000.0 ** (-((np.arange(128) % 32).astype(np.float32) * np.float32(2.0) / np.float32(64)))
    freq = jnp.asarray(freq.astype(np.float32)[None, :])
    vm = pl.BlockSpec(memory_space=pltpu.VMEM)
    sm = pl.BlockSpec(memory_space=pltpu.SMEM)
    hbm = pl.BlockSpec(memory_space=pltpu.HBM)
    bf, fl = jnp.bfloat16, jnp.float32
    def buf(*shape, kind=bf):
        return pltpu.VMEM(shape, kind)
    scratch = [buf(16384, 128), buf(528, 2048), buf(8, 1, 2048, kind=fl), buf(2048, 512), buf(1024, 128), buf(1024, 128),
               buf(528, 128, kind=fl), buf(528, 128, kind=fl), buf(4, 512, 128), buf(4, 16, 128), buf(640, 128),
               buf(512, 256, kind=fl), buf(16, 256, kind=fl), buf(520, 256, kind=fl), buf(2176, 128),
               buf(1024, 128), buf(1024, 128), buf(1024, 128), buf(528, 512, kind=fl),
               buf(512, 128, kind=fl), buf(512, 128, kind=fl)]
    scratch += [buf(256, 2048), buf(704, 2048), buf(704, 2048), buf(704, 2048), buf(512, 2048), buf(8, 1, 2048, kind=fl),
                buf(528, 2048), buf(8, 1, 2048, kind=fl), buf(528, 704), buf(65, 2048, kind=fl), buf(512, 2048), buf(8, 1, 2048, kind=fl)]
    scratch += sum_bufs(1024) + sum_bufs(CUT)
    scratch += [pltpu.SemaphoreType.DMA((160,)), pltpu.SemaphoreType.DMA((160,)), pltpu.SemaphoreType.DMA((11,))]
    return pl.pallas_call(
        layer_kernel,
        out_shape=(jax.ShapeDtypeStruct((65, 2048), bf), jax.ShapeDtypeStruct((520, 256), bf)),
        in_specs=[vm] * 4 + [sm] * 5 + [hbm] * 9,
        out_specs=(vm, vm),
        scratch_shapes=scratch,
        compiler_params=pltpu.CompilerParams(vmem_limit_bytes=60 << 20, collective_id=1, has_side_effects=True),
        cost_estimate=pl.CostEstimate(flops=10**10, bytes_accessed=14 * 10**6, transcendentals=15 * 10**6),
        name="layer",
    )(hidden_in, norm_attn.reshape(16, 128), norm_mlp.reshape(16, 128), freq, leaf_parent, leaf_owner, leaf_length, prompt_leaf,
      decode_leaf, w_query, w_key, w_value, cache_keys, cache_values, w_out, w_gate.T, w_up.T, w_down)


def solution(mesh):
    in_specs = (P(("kv", "tp"), None), P(), P(None, "tp"), P(), P(), P("tp", None), P(), P(None, "tp"), P(None, "tp"),
                P("tp", None), P("kv", None), P("kv", None), P(), P(), P(), P(), P())
    out_specs = (P(("kv", "tp"), None), P("kv", "tp"))
    return jax.shard_map(per_device, mesh=mesh, in_specs=in_specs, out_specs=out_specs, check_vma=False)
```
